32 devices in a mesh: dp: 8 (over z, y), mp: 4 (over x, core).
Axes of the slice: x: 2, y: 2, z: 4, core: 2. Of those that a mesh axis runs over, the one named last changes fastest.
Arguments:
- public_input_activations: bfloat16 [8, 112, 8192], P('dp', None, 'mp')
- public_output_cotangents: bfloat16 [8, 112, 8192], P('dp', None, 'mp')
- public_token_lengths: int32 [8], P('dp'), may hold values from 28 to 112, as said below
- private_input_activations: bfloat16 [32, 112, 8192], P('dp', None, 'mp')
- private_output_cotangents: bfloat16 [32, 112, 8192], P('dp', None, 'mp')
- private_token_lengths: int32 [32], P('dp'), may hold values from 28 to 112, as said below
- adapter_down_matrix: bfloat16 [8192, 16], P('mp'), may hold values from -0.0625 to 0.0625
- adapter_up_matrix: bfloat16 [16, 8192], P(None, 'mp'), may hold values from -0.0625 to 0.0625
- embedding_coefficient_noise: float32 [8], replicated, may hold values from -6 to 6
- residual_down_noise: float32 [4, 32768], P('mp', 'dp'), may hold values from -6 to 6
- residual_up_noise: float32 [4, 32768], P('mp', 'dp'), may hold values from -6 to 6
Outputs:
- update_down: float32 [4, 32768], P('mp', 'dp')
- update_up: float32 [4, 32768], P('mp', 'dp')
The draws below stay inside these ranges and needn't reach their ends.
Inputs may be any that keep to these rules, and one draw needn't show every extreme that they name: `public_token_lengths`: each example has between 28 and 112 live tokens at the start of its slots. `private_token_lengths`: each example has between 28 and 112 live tokens at the start of its slots.
All inputs are finite; a program needn't handle non-finite values.
Results may differ from the reference program's by a relative error of at most 0.0028.
Values may be sent and summed in bfloat16 or wider, within the bound.
No kernel may reach another device: no remote copies, remote signals or barrier semaphores. Data moves between devices by JAX's collectives and lax.ppermute only.
A program may use at most 64 MiB of HBM per device.

```python
import math
import jax
import jax.numpy as jnp
from jax import lax

MODEL_WIDTH = 8192
ADAPTER_RANK = 16
TOKEN_SLOTS = 112
PRIV = 32
PUB = 8
PSHARD = 4096
N_MP = 4


def feature_profile(key):
    inner = jax.random.fold_in(key, 7)
    first_key, second_key, third_key = jax.random.split(inner, 3)
    ramp = 1.0 + 2.0 * jnp.arange(MODEL_WIDTH, dtype=jnp.float32) / (MODEL_WIDTH - 1)
    rough = jax.random.uniform(first_key, (MODEL_WIDTH,), jnp.float32, 0.7, 1.4)
    heavy_count = max(PSHARD // ADAPTER_RANK, 1)
    heavy_start = jax.random.randint(third_key, (), 0, MODEL_WIDTH // heavy_count, dtype=jnp.int32) * heavy_count
    feature_index = jnp.arange(MODEL_WIDTH, dtype=jnp.int32)
    heavy_mask = jnp.logical_and(feature_index >= heavy_start, feature_index < heavy_start + heavy_count)
    boost = jnp.where(heavy_mask, 6.0, 1.0).astype(jnp.float32)
    centre = jax.random.normal(second_key, (MODEL_WIDTH,), jnp.float32)
    return (ramp * rough * boost, centre)


def cluster_centres(key, public, example_total_count):
    input_centres = jax.random.normal(jax.random.fold_in(key, 31), (PUB, MODEL_WIDTH), jnp.float32)
    output_centres = jax.random.normal(jax.random.fold_in(key, 32), (PUB, MODEL_WIDTH), jnp.float32)
    if public:
        cluster = jnp.arange(PUB, dtype=jnp.int32)
        weight_key = jax.random.fold_in(key, 41)
    else:
        cluster = jax.random.randint(jax.random.fold_in(key, 33), (example_total_count,), 0, PUB, dtype=jnp.int32)
        weight_key = jax.random.fold_in(key, 42)
    strength = jnp.exp(jax.random.uniform(weight_key, (example_total_count,), jnp.float32, math.log(0.25), math.log(2.0)))
    return (input_centres[cluster] * strength[:, None], output_centres[cluster])


def draw_activations(key, salt, example_total_count, public):
    feature_scale, centre = feature_profile(key)
    input_cluster, output_cluster = cluster_centres(key, public, example_total_count)
    noise_key, example_key = jax.random.split(jax.random.fold_in(key, salt), 2)
    fresh = jax.random.normal(noise_key, (example_total_count, TOKEN_SLOTS, MODEL_WIDTH), jnp.float32)
    spread = jnp.log(3.0)
    example_scale = jnp.exp(jax.random.uniform(example_key, (example_total_count, 1, 1), jnp.float32, 0.0, 1.0) * spread)
    return (example_scale * feature_scale * (centre + input_cluster[:, None, :] + fresh)).astype(jnp.bfloat16)


def draw_cotangents(key, salt, example_total_count, public):
    input_cluster, output_cluster = cluster_centres(key, public, example_total_count)
    noise_key = jax.random.fold_in(key, salt)
    fresh = jax.random.normal(noise_key, (example_total_count, TOKEN_SLOTS, MODEL_WIDTH), jnp.float32)
    cluster_gain = 3.0 / math.sqrt(TOKEN_SLOTS)
    return (fresh + cluster_gain * output_cluster[:, None, :]).astype(jnp.bfloat16)


def draw_token_lengths(key, salt, example_total_count):
    values = jax.random.randint(jax.random.fold_in(key, salt), (example_total_count,), TOKEN_SLOTS // 4, TOKEN_SLOTS + 1, dtype=jnp.int32)
    return values.at[0].set(TOKEN_SLOTS).at[1].set(TOKEN_SLOTS // 4)


def draw_public_input_activations(key, part):
    return draw_activations(key, 11, PUB, True)


def draw_private_input_activations(key, part):
    return draw_activations(key, 13, PRIV, False)


def draw_public_output_cotangents(key, part):
    return draw_cotangents(key, 15, PUB, True)


def draw_private_output_cotangents(key, part):
    return draw_cotangents(key, 17, PRIV, False)


def draw_public_token_lengths(key, part):
    return draw_token_lengths(key, 21, PUB)


def draw_private_token_lengths(key, part):
    return draw_token_lengths(key, 22, PRIV)


def levels(rng, shape, cuts, low, largest):
    gain, own = 1.0, jax.random.fold_in(rng, 6)
    for dim, shards_of in cuts:
        heights = jnp.exp(jax.random.uniform(jax.random.fold_in(own, dim), (shards_of,), jnp.float32, low / len(cuts), largest / len(cuts)))
        gain = gain * jnp.repeat(heights, shape[dim] // shards_of).reshape([-1 if axis == dim else 1 for axis in range(len(shape))])
    return gain


def centred(rng, extent, scale, reach, shards=(), kind=jnp.bfloat16):
    values = jax.random.normal(rng, extent, jnp.float32) * scale
    if len(shards) > 0:
        values = levels(rng, extent, shards, -0.22, 0.18) * values
    return jnp.clip(values, min=-reach, max=reach).astype(kind)


def setup_inputs(seed: int = 0) -> dict:
    streams_of = jax.random.split(jax.random.key(seed), 12)
    public_input_activations = draw_public_input_activations(jax.random.fold_in(streams_of[11], 71), 0)
    public_output_cotangents = draw_public_output_cotangents(jax.random.fold_in(streams_of[11], 71), 0)
    public_token_lengths = draw_public_token_lengths(jax.random.fold_in(streams_of[11], 71), 0)
    private_input_activations = draw_private_input_activations(jax.random.fold_in(streams_of[11], 71), 0)
    private_output_cotangents = draw_private_output_cotangents(jax.random.fold_in(streams_of[11], 71), 0)
    private_token_lengths = draw_private_token_lengths(jax.random.fold_in(streams_of[11], 71), 0)
    adapter_down_matrix = centred(streams_of[6], (MODEL_WIDTH, ADAPTER_RANK), MODEL_WIDTH ** -0.5, 0.0625, ((0, 4),))
    adapter_up_matrix = centred(streams_of[7], (ADAPTER_RANK, MODEL_WIDTH), MODEL_WIDTH ** -0.5, 0.0625, ((1, 4),))
    embedding_coefficient_noise = centred(streams_of[8], (PUB,), 1.0, 6.0, (), jnp.float32)
    residual_down_noise = centred(streams_of[9], (N_MP, MODEL_WIDTH // N_MP * ADAPTER_RANK), 1.0, 6.0, ((0, 4), (1, 8)), jnp.float32)
    residual_up_noise = centred(streams_of[10], (N_MP, MODEL_WIDTH // N_MP * ADAPTER_RANK), 1.0, 6.0, ((0, 4), (1, 8)), jnp.float32)
    return dict(public_input_activations=public_input_activations, public_output_cotangents=public_output_cotangents, public_token_lengths=public_token_lengths, private_input_activations=private_input_activations, private_output_cotangents=private_output_cotangents, private_token_lengths=private_token_lengths, adapter_down_matrix=adapter_down_matrix, adapter_up_matrix=adapter_up_matrix, embedding_coefficient_noise=embedding_coefficient_noise, residual_down_noise=residual_down_noise, residual_up_noise=residual_up_noise)


CLIP_COEF = 0.5
CLIP_RESIDUAL = 0.7
SIGMA_COEF = 1.0
SIGMA_RESIDUAL = 0.04
PRECISE = lax.Precision.HIGHEST

def per_example_gradients(input_activations, output_cotangents, token_lengths, adapter_down_matrix, adapter_up_matrix):
    example_total_count = input_activations.shape[0]
    block_width = MODEL_WIDTH // N_MP
    projected_gradients = jnp.dot(input_activations.reshape(example_total_count * TOKEN_SLOTS, MODEL_WIDTH).astype(jnp.float32), adapter_down_matrix.astype(jnp.float32), preferred_element_type=jnp.float32).reshape(example_total_count, TOKEN_SLOTS, ADAPTER_RANK)
    reconstructed_gradients = jnp.dot(output_cotangents.reshape(example_total_count * TOKEN_SLOTS, MODEL_WIDTH).astype(jnp.float32), adapter_up_matrix.T.astype(jnp.float32), preferred_element_type=jnp.float32).reshape(example_total_count, TOKEN_SLOTS, ADAPTER_RANK)
    positions = lax.broadcasted_iota(jnp.int32, (example_total_count, TOKEN_SLOTS), 1)
    live_mask = (positions < token_lengths[:, None]).astype(jnp.float32)[:, :, None]
    projected_live = lax.optimization_barrier((projected_gradients * live_mask).astype(jnp.bfloat16)).astype(jnp.float32)
    returned_live = lax.optimization_barrier((reconstructed_gradients * live_mask).astype(jnp.bfloat16)).astype(jnp.float32)

    def one_block(block_index):
        start = (block_index * block_width).astype(jnp.int32)
        input_block = lax.dynamic_slice_in_dim(input_activations, start, block_width, 2).astype(jnp.float32)
        cotangent_block = lax.dynamic_slice_in_dim(output_cotangents, start, block_width, 2).astype(jnp.float32)
        grad_down = jnp.einsum('etd,etr->edr', input_block, returned_live, precision=PRECISE)
        grad_up = jnp.einsum('etr,eto->ero', projected_live, cotangent_block, precision=PRECISE)
        joined = jnp.concatenate([grad_down.reshape(example_total_count, block_width * ADAPTER_RANK), grad_up.reshape(example_total_count, ADAPTER_RANK * block_width)], axis=1)
        return joined.astype(jnp.bfloat16)
    return lax.map(one_block, jnp.arange(N_MP, dtype=jnp.int32))

def lower_solve(factor, right_side, backward):
    return lax.linalg.triangular_solve(factor, right_side, left_side=True, lower=True, transpose_a=backward)

def reference(public_input_activations, public_output_cotangents, public_token_lengths, private_input_activations, private_output_cotangents, private_token_lengths, adapter_down_matrix, adapter_up_matrix, embedding_coefficient_noise, residual_down_noise, residual_up_noise):
    public_group = per_example_gradients(public_input_activations, public_output_cotangents, public_token_lengths, adapter_down_matrix, adapter_up_matrix)
    private_group = per_example_gradients(private_input_activations, private_output_cotangents, private_token_lengths, adapter_down_matrix, adapter_up_matrix)
    public_flat = public_group.transpose(1, 0, 2).reshape(PUB, -1)
    private_flat = private_group.transpose(1, 0, 2).reshape(PRIV, -1)
    gram_matrix = jnp.dot(public_flat.astype(jnp.float32), public_flat.T.astype(jnp.float32), preferred_element_type=jnp.float32)
    cross_terms = jnp.dot(public_flat.astype(jnp.float32), private_flat.T.astype(jnp.float32), preferred_element_type=jnp.float32)
    factor = jnp.linalg.cholesky(gram_matrix)
    norm_scale = jnp.mean(jnp.sqrt(jnp.diagonal(gram_matrix)))
    coefficient_limit = CLIP_COEF * norm_scale
    residual_limit = CLIP_RESIDUAL * norm_scale
    coeffs = lower_solve(factor, cross_terms, False)
    weights = lower_solve(factor, coeffs, True)

    def residual_block(running, block_index):
        public_block = public_group[block_index].astype(jnp.float32)
        private_block = private_group[block_index].astype(jnp.float32)
        residual = private_block - jnp.dot(weights.T, public_block, precision=PRECISE)
        return (running + lax.optimization_barrier(jnp.sum(residual * residual, axis=1)), block_index)
    residual_squares = lax.scan(residual_block, jnp.zeros((PRIV,), jnp.float32), jnp.arange(N_MP, dtype=jnp.int32))[0]
    coefficient_norm = jnp.sqrt(lax.optimization_barrier(jnp.sum(coeffs * coeffs, axis=0)))
    keep_coefficient = coefficient_limit / jnp.maximum(coefficient_norm, coefficient_limit)
    keep_residual = residual_limit / jnp.maximum(jnp.sqrt(residual_squares), residual_limit)
    target = jnp.dot(coeffs, keep_coefficient - keep_residual, precision=PRECISE) + SIGMA_COEF * coefficient_limit * embedding_coefficient_noise
    anchor = lower_solve(factor, target[:, None], True)[:, 0]

    def update_block(block_index):
        public_block = public_group[block_index].astype(jnp.float32)
        private_block = private_group[block_index].astype(jnp.float32)
        return jnp.dot(anchor, public_block, precision=PRECISE) + jnp.dot(keep_residual, private_block, precision=PRECISE)
    update = lax.map(update_block, jnp.arange(N_MP, dtype=jnp.int32))
    noise_whole = jnp.concatenate([residual_down_noise, residual_up_noise], axis=1)
    update_gain = 1.0 / math.sqrt(PRIV * TOKEN_SLOTS)
    update = (update + SIGMA_RESIDUAL * residual_limit * noise_whole) * update_gain
    split_point = MODEL_WIDTH // N_MP * ADAPTER_RANK
    return (update[:, :split_point], update[:, split_point:])
```

```python
import functools
import math

import jax
import jax.numpy as jnp
from jax import lax
from jax.experimental import pallas as pl
from jax.experimental.pallas import tpu as pltpu
from jax.sharding import PartitionSpec as P

CLIP_COEF = 0.5
CLIP_RESIDUAL = 0.7
SIGMA_COEF = 1.0
SIGMA_RESIDUAL = 0.04
PRECISE = lax.Precision.HIGHEST
LANES = 128
VMEM = pl.BlockSpec(memory_space=pltpu.VMEM)
SMEM = pl.BlockSpec(memory_space=pltpu.SMEM)
BOTH_LAST = (((1,), (1,)), ((), ()))
FIRST_LAST = (((1,), (0,)), ((), ()))
PARAMS = pltpu.CompilerParams(vmem_limit_bytes=40 * 1024 * 1024)


def dot(a, b, dims, precision=None):
    return lax.dot_general(a, b, dims, precision=precision, preferred_element_type=jnp.float32)


def iota(shape, axis):
    return lax.broadcasted_iota(jnp.int32, shape, axis)


def project_kernel(pub_in, pub_out, priv_in, priv_out, down_t, up, out):
    rank = up.shape[0]
    tokens = pub_in.shape[1]
    out[...] = jnp.zeros_like(out)
    slot = 0
    for inputs, cotangents in ((pub_in, pub_out), (priv_in, priv_out)):
        for e in range(inputs.shape[0]):
            at = slice(slot * LANES, slot * LANES + tokens)
            out[0:rank, at] = dot(down_t[...], inputs[e], BOTH_LAST)
            out[rank : 2 * rank, at] = dot(up[...], cotangents[e], BOTH_LAST)
            slot += 1


def gradient_kernel(dp, pub_len, priv_len, own, other, pub_in, pub_out, priv_in, priv_out, *rest):
    blocks, down_rows, up_rows = rest[:dp], rest[dp], rest[dp + 1]
    me = lax.axis_index("dp")
    rank = own.shape[0] // 2
    tokens, width = pub_in.shape[1:]
    lanes = width // dp
    per = rank // dp
    slot = 0
    for inputs, cotangents, lengths in (
        (pub_in, pub_out, pub_len),
        (priv_in, priv_out, priv_len),
    ):
        for e in range(inputs.shape[0]):
            at = slice(slot * LANES, slot * LANES + tokens)
            both = own[:, at] + other[:, at]
            live = iota(both.shape, 1) < lengths[e]
            both = jnp.where(live, both, 0.0).astype(jnp.bfloat16)
            for c in range(dp):
                features = slice(c * lanes, (c + 1) * lanes)
                at = slice(c * rank, (c + 1) * rank)
                down_part = dot(both[rank:], inputs[e, :, features], FIRST_LAST)
                up_part = dot(both[:rank], cotangents[e, :, features], FIRST_LAST)
                down_rows[at, :] = down_part.astype(jnp.bfloat16)
                for h in range(lanes // LANES):
                    up_rows[h, at, :] = up_part[:, h * LANES : (h + 1) * LANES]
            for k in range(dp):
                to = me ^ k
                row = slot * 2 * rank
                blocks[k][row : row + rank, :] = down_rows[
                    pl.ds(pl.multiple_of(to * rank, rank), rank), :
                ]
                for h in range(lanes // LANES):
                    pieces = [
                        up_rows[h, pl.ds(to * per + r, dp, stride=rank), :] for r in range(per)
                    ]
                    blocks[k][row + rank : row + 2 * rank, h * LANES : (h + 1) * LANES] = (
                        jnp.concatenate(pieces, axis=0).astype(jnp.bfloat16)
                    )
            slot += 1


def gram_kernel(dp, n_pub, n_priv, *refs):
    blocks, group, out = refs[:dp], refs[dp], refs[dp + 1]
    me = lax.axis_index("dp")
    rows = blocks[0].shape[0] // (n_pub + n_priv)
    pub_rows, priv_rows = n_pub * rows, n_priv * rows
    for k in range(dp):
        source = me ^ k
        group[pl.ds(pl.multiple_of(source * pub_rows, pub_rows), pub_rows), :] = blocks[k][:pub_rows]
        group[
            pl.ds(pl.multiple_of(dp * pub_rows + source * priv_rows, priv_rows), priv_rows), :
        ] = blocks[k][pub_rows:]
    publics = dp * n_pub
    span = publics * rows
    lanes = group.shape[1]
    public = group[:span, :]
    total = jnp.zeros((publics, LANES), jnp.float32)
    same = iota((span, span), 0) % rows == iota((span, span), 1) % rows
    squares = []
    for c in range(group.shape[0] // span):
        part = group[c * span : (c + 1) * span, :]
        products = jnp.where(same, dot(public, part, BOTH_LAST), 0.0)
        products = jnp.sum(products.reshape(publics, rows, span), axis=1)
        pick = (iota((span, LANES), 0) // rows + c * publics == iota((span, LANES), 1)).astype(
            jnp.float32
        )
        total += dot(products, pick, FIRST_LAST, PRECISE)
        if c > 0:
            wide = part.astype(jnp.float32)
            squares.append(jnp.sum((wide * wide).reshape(publics, rows, lanes), axis=1))
    examples = group.shape[0] // rows
    before = LANES // 2 + publics
    after = LANES // 2 - examples
    stacked = jnp.concatenate(
        [jnp.zeros((before, lanes), jnp.float32)]
        + squares
        + ([jnp.zeros((after, lanes), jnp.float32)] if after else []),
        axis=0,
    )
    total_squares = dot(jnp.ones((publics, lanes), jnp.float32), stacked, BOTH_LAST, PRECISE)
    total += jnp.where(iota(total.shape, 0) == 0, total_squares, 0.0)
    for d in range(out.shape[0]):
        out[d] = total


def update_kernel(gain, shares, group, noise, down_noise, up_noise, down, up):
    total = shares[0]
    for d in range(1, shares.shape[0]):
        total = total + shares[d]
    publics = total.shape[0]
    shape = total.shape
    row, lane = iota(shape, 0), iota(shape, 1)
    half = LANES // 2
    squares = pltpu.roll(total, half, 1)[0:1]
    gram_diagonal = jnp.sum(jnp.where(row == lane, total, 0.0), axis=1, keepdims=True)
    norm_scale = jnp.mean(jnp.sqrt(gram_diagonal), axis=0, keepdims=True)
    coefficient_limit = CLIP_COEF * norm_scale
    residual_limit = CLIP_RESIDUAL * norm_scale
    work = jnp.where(lane < half, total, jnp.where(lane == row + half, 1.0, 0.0))
    for j in range(publics):
        inverse = lax.rsqrt(work[j : j + 1, j : j + 1])
        pivot = work[j : j + 1, :] * inverse
        column = work[:, j : j + 1] * inverse
        work = jnp.where(row > j, work - column * pivot, jnp.where(row == j, pivot, work))
    examples = group.shape[0] * publics // (publics * (2 * up.shape[1] // group.shape[1]))
    private = jnp.logical_and(lane >= publics, lane < examples)
    coeffs = jnp.where(private, work, 0.0)
    coefficient_squares = jnp.sum(coeffs * coeffs, axis=0, keepdims=True)
    residual_squares = jnp.maximum(squares - coefficient_squares, 0.0)
    keep_coefficient = coefficient_limit / jnp.maximum(
        jnp.sqrt(coefficient_squares), coefficient_limit
    )
    keep_residual = residual_limit / jnp.maximum(jnp.sqrt(residual_squares), residual_limit)
    correction = jnp.sum(
        coeffs * (keep_coefficient - keep_residual), axis=1, keepdims=True
    )
    noise_column = jnp.zeros((publics, 1), jnp.float32)
    for j in range(publics):
        noise_column = jnp.where(iota((publics, 1), 0) == j, noise[j], noise_column)
    target = correction + SIGMA_COEF * coefficient_limit * noise_column
    inverse_factor = jnp.where(lane >= half, work, 0.0)
    anchor = pltpu.roll(jnp.sum(inverse_factor * target, axis=0, keepdims=True), half, 1)
    weights = jnp.where(lane[0:1] < publics, anchor, keep_residual)

    lanes = group.shape[1]
    rows = group.shape[0] // examples
    rank = rows // 2
    acc = jnp.zeros((rows, lanes), jnp.float32)
    for i in range(examples):
        acc = acc + weights[:, i : i + 1] * group[i * rows : (i + 1) * rows, :].astype(jnp.float32)
    scale = SIGMA_RESIDUAL * residual_limit
    per = LANES // rank
    flat = lanes * rank // LANES
    wide = jnp.concatenate([acc[:rank]] * per, axis=0)
    wide = jnp.where(iota((LANES, lanes), 0) // rank == iota((LANES, lanes), 1) % per, wide, 0.0)
    pick = (iota((flat, lanes), 0) == iota((flat, lanes), 1) // per).astype(jnp.float32)
    turned = dot(pick, wide, BOTH_LAST, PRECISE)
    for a in range(flat):
        at = slice(a * LANES, (a + 1) * LANES)
        down[0:1, at] = (turned[a : a + 1] + scale * down_noise[0:1, at]) * gain
    for a in range(rank):
        at = slice(a * lanes, (a + 1) * lanes)
        up[0:1, at] = (acc[rank + a : rank + a + 1] + scale * up_noise[0:1, at]) * gain


def exchange(x, axis, step):
    return lax.ppermute(x, axis, [(s, s ^ step) for s in range(lax.axis_size(axis))])


def small_group(
    pub_in, pub_out, pub_len, priv_in, priv_out, priv_len, down, up, noise, down_noise, up_noise
):
    dp, mp = lax.axis_size("dp"), lax.axis_size("mp")
    n_pub, tokens, width = pub_in.shape
    n_priv = priv_in.shape[0]
    examples = n_pub + n_priv
    rank = up.shape[0]
    lanes = width // dp
    f32, bf16 = jnp.float32, jnp.bfloat16

    own = pl.pallas_call(
        project_kernel,
        out_shape=jax.ShapeDtypeStruct((2 * rank, examples * LANES), f32),
        in_specs=[VMEM] * 6,
        out_specs=VMEM,
        compiler_params=PARAMS,
        name="project",
    )(pub_in, pub_out, priv_in, priv_out, down.T, up)
    step = 1
    while step < mp:
        other = exchange(own, "mp", step)
        step *= 2
        if step < mp:
            own = own + other

    block = jax.ShapeDtypeStruct((examples * 2 * rank, lanes), bf16)
    blocks = pl.pallas_call(
        functools.partial(gradient_kernel, dp),
        out_shape=[block] * dp,
        in_specs=[SMEM] * 2 + [VMEM] * 6,
        out_specs=[VMEM] * dp,
        scratch_shapes=[
            pltpu.VMEM((dp * rank, lanes), bf16),
            pltpu.VMEM((lanes // LANES, dp * rank, LANES), f32),
        ],
        compiler_params=PARAMS,
        name="gradients",
    )(pub_len, priv_len, own, other, pub_in, pub_out, priv_in, priv_out)
    blocks = [blocks[0]] + [exchange(blocks[k], "dp", k) for k in range(1, dp)]

    group, shares = pl.pallas_call(
        functools.partial(gram_kernel, dp, n_pub, n_priv),
        out_shape=[
            jax.ShapeDtypeStruct((dp * examples * 2 * rank, lanes), bf16),
            jax.ShapeDtypeStruct((dp * mp, dp * n_pub, LANES), f32),
        ],
        in_specs=[VMEM] * dp,
        out_specs=[VMEM] * 2,
        compiler_params=PARAMS,
        name="inner_products",
    )(*blocks)
    shares = lax.all_to_all(shares, ("dp", "mp"), 0, 0, tiled=True)

    gain = 1.0 / math.sqrt(n_priv * dp * tokens)
    return pl.pallas_call(
        functools.partial(update_kernel, gain),
        out_shape=[
            jax.ShapeDtypeStruct(down_noise.shape, f32),
            jax.ShapeDtypeStruct(up_noise.shape, f32),
        ],
        in_specs=[VMEM, VMEM, SMEM, VMEM, VMEM],
        out_specs=[VMEM] * 2,
        compiler_params=PARAMS,
        name="update",
    )(shares, group, noise, down_noise, up_noise)


def fits(mesh, pub_in, priv_in, up):
    dp = mesh.shape["dp"]
    width = pub_in.shape[2] // mesh.shape["mp"]
    publics = pub_in.shape[0]
    return (
        up.shape[0] == 16
        and dp in (2, 4, 8)
        and width % (dp * LANES) == 0
        and publics == 8
        and priv_in.shape[0] % 8 == 0
        and publics + priv_in.shape[0] <= LANES // 2
        and pub_in.shape[1] <= LANES
    )


def partial_gram_terms(
    input_activations, output_cotangents, adapter_down_matrix, adapter_up_matrix
):
    projected_gradients = jnp.einsum(
        "umo,ov->umv", input_activations, adapter_down_matrix, preferred_element_type=jnp.float32
    )
    reconstructed_gradients = jnp.einsum(
        "fpb,ab->fpa", output_cotangents, adapter_up_matrix, preferred_element_type=jnp.float32
    )
    return (projected_gradients, reconstructed_gradients)


def shard_grads(
    input_activations,
    output_cotangents,
    token_lengths,
    projected_gradients,
    reconstructed_gradients,
):
    example_total_count = input_activations.shape[0]
    token_steps = input_activations.shape[1]
    positions = lax.broadcasted_iota(jnp.int32, (example_total_count, token_steps), 1)
    live_mask = (positions < token_lengths[:, None]).astype(jnp.float32)[:, :, None]
    projected_live = (projected_gradients * live_mask).astype(jnp.bfloat16)
    returned_live = (reconstructed_gradients * live_mask).astype(jnp.bfloat16)
    grad_down = jnp.einsum(
        "etd,etr->edr", input_activations, returned_live, preferred_element_type=jnp.float32
    ).astype(jnp.bfloat16)
    grad_up = jnp.einsum(
        "etr,eto->ero", projected_live, output_cotangents, preferred_element_type=jnp.float32
    ).astype(jnp.bfloat16)
    return (grad_down.reshape(example_total_count, -1), grad_up.reshape(example_total_count, -1))


def lower_solve(factor, right_side, backward):
    return lax.linalg.triangular_solve(
        factor, right_side, left_side=True, lower=True, transpose_a=backward
    )


def limits(gram_matrix):
    factor = jnp.linalg.cholesky(gram_matrix)
    norm_scale = jnp.mean(jnp.sqrt(jnp.diagonal(gram_matrix)))
    return (factor, CLIP_COEF * norm_scale, CLIP_RESIDUAL * norm_scale)


def keep_factors(coeffs, residual_squares, coefficient_limit, residual_limit):
    coefficient_norm = jnp.sqrt(jnp.sum(coeffs * coeffs, axis=0))
    keep_coefficient = coefficient_limit / jnp.maximum(coefficient_norm, coefficient_limit)
    keep_residual = residual_limit / jnp.maximum(jnp.sqrt(residual_squares), residual_limit)
    return (keep_coefficient, keep_residual)


def large_group(
    public_input_activations,
    public_output_cotangents,
    public_token_lengths,
    private_input_activations,
    private_output_cotangents,
    private_token_lengths,
    adapter_down_matrix,
    adapter_up_matrix,
    embedding_coefficient_noise,
    residual_down_noise,
    residual_up_noise,
):
    public_projected, public_returned = partial_gram_terms(
        public_input_activations, public_output_cotangents, adapter_down_matrix, adapter_up_matrix
    )
    private_projected, private_returned = partial_gram_terms(
        private_input_activations, private_output_cotangents, adapter_down_matrix, adapter_up_matrix
    )
    public_projected, public_returned, private_projected, private_returned = lax.psum(
        (public_projected, public_returned, private_projected, private_returned), "mp"
    )
    public_down, public_up = shard_grads(
        public_input_activations,
        public_output_cotangents,
        public_token_lengths,
        public_projected,
        public_returned,
    )
    private_down, private_up = shard_grads(
        private_input_activations,
        private_output_cotangents,
        private_token_lengths,
        private_projected,
        private_returned,
    )
    public_down, public_up, private_down, private_up = (
        lax.all_to_all(public_down, "dp", split_axis=1, concat_axis=0, tiled=True),
        lax.all_to_all(public_up, "dp", split_axis=1, concat_axis=0, tiled=True),
        lax.all_to_all(private_down, "dp", split_axis=1, concat_axis=0, tiled=True),
        lax.all_to_all(private_up, "dp", split_axis=1, concat_axis=0, tiled=True),
    )
    public_group = jnp.concatenate([public_down, public_up], axis=1)
    private_group = jnp.concatenate([private_down, private_up], axis=1)
    public_wide = public_group.astype(jnp.float32)
    private_wide = private_group.astype(jnp.float32)
    gram_partial = jnp.einsum(
        "pk,qk->pq", public_group, public_group, preferred_element_type=jnp.float32
    )
    cross_partial = jnp.einsum(
        "pk,qk->pq", public_group, private_group, preferred_element_type=jnp.float32
    )
    square_partial = jnp.sum(private_wide * private_wide, axis=1)
    gram_matrix, cross_terms, square_totals = lax.psum(
        (gram_partial, cross_partial, square_partial), ("dp", "mp")
    )
    factor, coefficient_limit, residual_limit = limits(gram_matrix)
    coeffs = lower_solve(factor, cross_terms, False)
    residual_squares = square_totals - jnp.sum(coeffs * coeffs, axis=0)
    keep_coefficient, keep_residual = keep_factors(
        coeffs, residual_squares, coefficient_limit, residual_limit
    )
    correction = jnp.dot(coeffs, keep_coefficient - keep_residual, precision=PRECISE)
    target = correction + SIGMA_COEF * coefficient_limit * embedding_coefficient_noise
    anchor = lower_solve(factor, target[:, None], True)[:, 0]
    update = jnp.dot(anchor, public_wide, precision=PRECISE) + jnp.dot(
        keep_residual, private_wide, precision=PRECISE
    )
    noise_shard = jnp.concatenate([residual_down_noise[0], residual_up_noise[0]], axis=0)
    private_total = private_input_activations.shape[0] * lax.axis_size("dp")
    update_gain = 1.0 / math.sqrt(private_total * private_input_activations.shape[1])
    result = (update + SIGMA_RESIDUAL * residual_limit * noise_shard) * update_gain
    split_point = public_down.shape[1]
    return (result[None, :split_point], result[None, split_point:])


def solution(mesh):
    placed = (
        P("dp", None, "mp"),
        P("dp", None, "mp"),
        P("dp"),
        P("dp", None, "mp"),
        P("dp", None, "mp"),
        P("dp"),
        P("mp", None),
        P(None, "mp"),
        P(),
        P("mp", "dp"),
        P("mp", "dp"),
    )

    def run(*arrays):
        body = small_group if fits(mesh, arrays[0], arrays[3], arrays[7]) else large_group
        return jax.shard_map(
            body,
            mesh=mesh,
            in_specs=placed,
            out_specs=(P("mp", "dp"), P("mp", "dp")),
            check_vma=False,
        )(*arrays)

    return run
```

```python
import functools
import math

import jax
import jax.numpy as jnp
from jax import lax
from jax.experimental import pallas as pl
from jax.experimental.pallas import tpu as pltpu
from jax.sharding import PartitionSpec as P

CLIP_COEF = 0.5
CLIP_RESIDUAL = 0.7
SIGMA_COEF = 1.0
SIGMA_RESIDUAL = 0.04
PRECISE = lax.Precision.HIGHEST
LANES = 128
GROUP = 4
VMEM = pl.BlockSpec(memory_space=pltpu.VMEM)
HBM = pl.BlockSpec(memory_space=pltpu.HBM)
SMEM = pl.BlockSpec(memory_space=pltpu.SMEM)
BOTH_LAST = (((1,), (1,)), ((), ()))
FIRST_LAST = (((1,), (0,)), ((), ()))
PARAMS = pltpu.CompilerParams(vmem_limit_bytes=40 * 1024 * 1024)


def dot(a, b, dims, precision=None):
    return lax.dot_general(a, b, dims, precision=precision, preferred_element_type=jnp.float32)


def iota(shape, axis):
    return lax.broadcasted_iota(jnp.int32, shape, axis)


def project_kernel(pub_in, pub_out, priv_in, priv_out, down_t, up, *rest):
    out, held, (down_held, up_held, sems) = rest[0], rest[1:5], rest[5:]
    rank = up.shape[0]
    tokens = pub_in.shape[1]
    copies = [
        pltpu.make_async_copy(down_t, down_held, sems.at[0]),
        pltpu.make_async_copy(up, up_held, sems.at[1]),
    ]
    pieces = []
    for inputs, cotangents, inputs_held, cotangents_held in (
        (pub_in, pub_out, held[0], held[1]),
        (priv_in, priv_out, held[2], held[3]),
    ):
        for e in range(inputs.shape[0]):
            pieces += [(down_held, inputs_held.at[e]), (up_held, cotangents_held.at[e])]
            for source, to in ((inputs, inputs_held), (cotangents, cotangents_held)):
                copies.append(
                    pltpu.make_async_copy(source.at[e], to.at[e], sems.at[len(copies)])
                )
    for copy in copies:
        copy.start()
    out[...] = jnp.zeros_like(out)
    for copy in copies[:2]:
        copy.wait()
    for i, (weights, piece) in enumerate(pieces):
        if i % GROUP == 0:
            for copy in copies[2 + i : 2 + i + GROUP]:
                copy.wait()
        slot, half = i // 2, i % 2
        out[half * rank : (half + 1) * rank, slot * LANES : slot * LANES + tokens] = dot(
            weights[...], piece[...], BOTH_LAST
        )


def gradient_kernel(dp, pub_len, priv_len, own, other, pub_in, pub_out, priv_in, priv_out, *rest):
    blocks, down_rows, up_rows = rest[:dp], rest[dp], rest[dp + 1]
    me = lax.axis_index("dp")
    rank = own.shape[0] // 2
    tokens, width = pub_in.shape[1:]
    lanes = width // dp
    per = rank // dp
    slot = 0
    for inputs, cotangents, lengths in (
        (pub_in, pub_out, pub_len),
        (priv_in, priv_out, priv_len),
    ):
        for e in range(inputs.shape[0]):
            at = slice(slot * LANES, slot * LANES + tokens)
            both = own[:, at] + other[:, at]
            live = iota(both.shape, 1) < lengths[e]
            both = jnp.where(live, both, 0.0).astype(jnp.bfloat16)
            for c in range(dp):
                features = slice(c * lanes, (c + 1) * lanes)
                at = slice(c * rank, (c + 1) * rank)
                down_part = dot(both[rank:], inputs[e, :, features], FIRST_LAST)
                up_part = dot(both[:rank], cotangents[e, :, features], FIRST_LAST)
                down_rows[at, :] = down_part.astype(jnp.bfloat16)
                for h in range(lanes // LANES):
                    up_rows[h, at, :] = up_part[:, h * LANES : (h + 1) * LANES]
            for k in range(dp):
                to = me ^ k
                row = slot * 2 * rank
                blocks[k][row : row + rank, :] = down_rows[
                    pl.ds(pl.multiple_of(to * rank, rank), rank), :
                ]
                for h in range(lanes // LANES):
                    pieces = [
                        up_rows[h, pl.ds(to * per + r, dp, stride=rank), :] for r in range(per)
                    ]
                    blocks[k][row + rank : row + 2 * rank, h * LANES : (h + 1) * LANES] = (
                        jnp.concatenate(pieces, axis=0).astype(jnp.bfloat16)
                    )
            slot += 1


def gram_kernel(order, n_pub, n_priv, *refs):
    dp = len(order)
    blocks, group, out = refs[:dp], refs[dp], refs[dp + 1]
    me = lax.axis_index("dp")
    rows = blocks[0].shape[0] // (n_pub + n_priv)
    pub_rows, priv_rows = n_pub * rows, n_priv * rows
    for k, block in zip(order, blocks):
        source = me ^ k
        group[pl.ds(pl.multiple_of(source * pub_rows, pub_rows), pub_rows), :] = block[:pub_rows]
        group[
            pl.ds(pl.multiple_of(dp * pub_rows + source * priv_rows, priv_rows), priv_rows), :
        ] = block[pub_rows:]
    publics = dp * n_pub
    span = publics * rows
    lanes = group.shape[1]
    public = group[:span, :]
    total = jnp.zeros((publics, LANES), jnp.float32)
    same = iota((span, span), 0) % rows == iota((span, span), 1) % rows
    squares = []
    for c in range(group.shape[0] // span):
        part = group[c * span : (c + 1) * span, :]
        products = jnp.where(same, dot(public, part, BOTH_LAST), 0.0)
        products = jnp.sum(products.reshape(publics, rows, span), axis=1)
        pick = (iota((span, LANES), 0) // rows + c * publics == iota((span, LANES), 1)).astype(
            jnp.float32
        )
        total += dot(products, pick, FIRST_LAST, PRECISE)
        if c > 0:
            wide = part.astype(jnp.float32)
            squares.append(jnp.sum((wide * wide).reshape(publics, rows, lanes), axis=1))
    examples = group.shape[0] // rows
    before = LANES // 2 + publics
    after = LANES // 2 - examples
    stacked = jnp.concatenate(
        [jnp.zeros((before, lanes), jnp.float32)]
        + squares
        + ([jnp.zeros((after, lanes), jnp.float32)] if after else []),
        axis=0,
    )
    total_squares = dot(jnp.ones((publics, lanes), jnp.float32), stacked, BOTH_LAST, PRECISE)
    total += jnp.where(iota(total.shape, 0) == 0, total_squares, 0.0)
    for d in range(out.shape[0]):
        out[d] = total


def update_kernel(gain, shares, group, noise, down_noise, up_noise, down, up):
    total = shares[0]
    for d in range(1, shares.shape[0]):
        total = total + shares[d]
    publics = total.shape[0]
    shape = total.shape
    row, lane = iota(shape, 0), iota(shape, 1)
    half = LANES // 2
    squares = pltpu.roll(total, half, 1)[0:1]
    gram_diagonal = jnp.sum(jnp.where(row == lane, total, 0.0), axis=1, keepdims=True)
    norm_scale = jnp.mean(jnp.sqrt(gram_diagonal), axis=0, keepdims=True)
    coefficient_limit = CLIP_COEF * norm_scale
    residual_limit = CLIP_RESIDUAL * norm_scale
    work = jnp.where(lane < half, total, jnp.where(lane == row + half, 1.0, 0.0))
    for j in range(publics):
        inverse = lax.rsqrt(work[j : j + 1, j : j + 1])
        pivot = work[j : j + 1, :] * inverse
        column = work[:, j : j + 1] * inverse
        work = jnp.where(row > j, work - column * pivot, jnp.where(row == j, pivot, work))
    examples = group.shape[0] * publics // (publics * (2 * up.shape[1] // group.shape[1]))
    private = jnp.logical_and(lane >= publics, lane < examples)
    coeffs = jnp.where(private, work, 0.0)
    coefficient_squares = jnp.sum(coeffs * coeffs, axis=0, keepdims=True)
    residual_squares = jnp.maximum(squares - coefficient_squares, 0.0)
    keep_coefficient = coefficient_limit / jnp.maximum(
        jnp.sqrt(coefficient_squares), coefficient_limit
    )
    keep_residual = residual_limit / jnp.maximum(jnp.sqrt(residual_squares), residual_limit)
    correction = jnp.sum(
        coeffs * (keep_coefficient - keep_residual), axis=1, keepdims=True
    )
    noise_column = jnp.zeros((publics, 1), jnp.float32)
    for j in range(publics):
        noise_column = jnp.where(iota((publics, 1), 0) == j, noise[j], noise_column)
    target = correction + SIGMA_COEF * coefficient_limit * noise_column
    inverse_factor = jnp.where(lane >= half, work, 0.0)
    anchor = pltpu.roll(jnp.sum(inverse_factor * target, axis=0, keepdims=True), half, 1)
    weights = jnp.where(lane[0:1] < publics, anchor, keep_residual)

    lanes = group.shape[1]
    rows = group.shape[0] // examples
    rank = rows // 2
    acc = jnp.zeros((rows, lanes), jnp.float32)
    for i in range(examples):
        acc = acc + weights[:, i : i + 1] * group[i * rows : (i + 1) * rows, :].astype(jnp.float32)
    scale = SIGMA_RESIDUAL * residual_limit
    per = LANES // rank
    flat = lanes * rank // LANES
    wide = jnp.concatenate([acc[:rank]] * per, axis=0)
    wide = jnp.where(iota((LANES, lanes), 0) // rank == iota((LANES, lanes), 1) % per, wide, 0.0)
    pick = (iota((flat, lanes), 0) == iota((flat, lanes), 1) // per).astype(jnp.float32)
    turned = dot(pick, wide, BOTH_LAST, PRECISE)
    for a in range(flat):
        at = slice(a * LANES, (a + 1) * LANES)
        down[0:1, at] = (turned[a : a + 1] + scale * down_noise[0:1, at]) * gain
    for a in range(rank):
        at = slice(a * lanes, (a + 1) * lanes)
        up[0:1, at] = (acc[rank + a : rank + a + 1] + scale * up_noise[0:1, at]) * gain


def exchange(x, axis, step):
    return lax.ppermute(x, axis, [(s, s ^ step) for s in range(lax.axis_size(axis))])


def small_group(
    pub_in, pub_out, pub_len, priv_in, priv_out, priv_len, down, up, noise, down_noise, up_noise
):
    dp, mp = lax.axis_size("dp"), lax.axis_size("mp")
    n_pub, tokens, width = pub_in.shape
    n_priv = priv_in.shape[0]
    examples = n_pub + n_priv
    rank = up.shape[0]
    lanes = width // dp
    f32, bf16 = jnp.float32, jnp.bfloat16

    own, *held = pl.pallas_call(
        project_kernel,
        out_shape=[jax.ShapeDtypeStruct((2 * rank, examples * LANES), f32)]
        + [jax.ShapeDtypeStruct(x.shape, bf16) for x in (pub_in, pub_out, priv_in, priv_out)],
        in_specs=[HBM] * 6,
        out_specs=[VMEM] * 5,
        scratch_shapes=[
            pltpu.VMEM(up.shape, bf16),
            pltpu.VMEM(up.shape, bf16),
            pltpu.SemaphoreType.DMA((2 + 2 * examples,)),
        ],
        compiler_params=PARAMS,
        name="project",
    )(
        *(
            pltpu.with_memory_space_constraint(x, pltpu.HBM)
            for x in (pub_in, pub_out, priv_in, priv_out, down.T, up)
        )
    )
    step = 1
    while step < mp:
        other = exchange(own, "mp", step)
        step *= 2
        if step < mp:
            own = own + other

    block = jax.ShapeDtypeStruct((examples * 2 * rank, lanes), bf16)
    blocks = pl.pallas_call(
        functools.partial(gradient_kernel, dp),
        out_shape=[block] * dp,
        in_specs=[SMEM] * 2 + [VMEM] * 6,
        out_specs=[VMEM] * dp,
        scratch_shapes=[
            pltpu.VMEM((dp * rank, lanes), bf16),
            pltpu.VMEM((lanes // LANES, dp * rank, LANES), f32),
        ],
        compiler_params=PARAMS,
        name="gradients",
    )(pub_len, priv_len, own, other, *held)
    order = sorted(range(1, dp), key=lambda k: (-k.bit_length(), k & 1, k)) + [0]
    blocks = [exchange(blocks[k], "dp", k) if k else blocks[k] for k in order]

    group, shares = pl.pallas_call(
        functools.partial(gram_kernel, order, n_pub, n_priv),
        out_shape=[
            jax.ShapeDtypeStruct((dp * examples * 2 * rank, lanes), bf16),
            jax.ShapeDtypeStruct((dp * mp, dp * n_pub, LANES), f32),
        ],
        in_specs=[VMEM] * dp,
        out_specs=[VMEM] * 2,
        compiler_params=PARAMS,
        name="inner_products",
    )(*blocks)
    shares = lax.all_to_all(shares, ("dp", "mp"), 0, 0, tiled=True)

    gain = 1.0 / math.sqrt(n_priv * dp * tokens)
    return pl.pallas_call(
        functools.partial(update_kernel, gain),
        out_shape=[
            jax.ShapeDtypeStruct(down_noise.shape, f32),
            jax.ShapeDtypeStruct(up_noise.shape, f32),
        ],
        in_specs=[VMEM, VMEM, SMEM, VMEM, VMEM],
        out_specs=[VMEM] * 2,
        compiler_params=PARAMS,
        name="update",
    )(shares, group, noise, down_noise, up_noise)


def fits(mesh, pub_in, priv_in, up):
    dp = mesh.shape["dp"]
    width = pub_in.shape[2] // mesh.shape["mp"]
    publics = pub_in.shape[0]
    return (
        up.shape[0] == 16
        and dp in (2, 4, 8)
        and width % (dp * LANES) == 0
        and publics == 8
        and priv_in.shape[0] % 8 == 0
        and publics + priv_in.shape[0] <= LANES // 2
        and pub_in.shape[1] <= LANES
    )


def partial_gram_terms(
    input_activations, output_cotangents, adapter_down_matrix, adapter_up_matrix
):
    projected_gradients = jnp.einsum(
        "umo,ov->umv", input_activations, adapter_down_matrix, preferred_element_type=jnp.float32
    )
    reconstructed_gradients = jnp.einsum(
        "fpb,ab->fpa", output_cotangents, adapter_up_matrix, preferred_element_type=jnp.float32
    )
    return (projected_gradients, reconstructed_gradients)


def shard_grads(
    input_activations,
    output_cotangents,
    token_lengths,
    projected_gradients,
    reconstructed_gradients,
):
    example_total_count = input_activations.shape[0]
    token_steps = input_activations.shape[1]
    positions = lax.broadcasted_iota(jnp.int32, (example_total_count, token_steps), 1)
    live_mask = (positions < token_lengths[:, None]).astype(jnp.float32)[:, :, None]
    projected_live = (projected_gradients * live_mask).astype(jnp.bfloat16)
    returned_live = (reconstructed_gradients * live_mask).astype(jnp.bfloat16)
    grad_down = jnp.einsum(
        "etd,etr->edr", input_activations, returned_live, preferred_element_type=jnp.float32
    ).astype(jnp.bfloat16)
    grad_up = jnp.einsum(
        "etr,eto->ero", projected_live, output_cotangents, preferred_element_type=jnp.float32
    ).astype(jnp.bfloat16)
    return (grad_down.reshape(example_total_count, -1), grad_up.reshape(example_total_count, -1))


def lower_solve(factor, right_side, backward):
    return lax.linalg.triangular_solve(
        factor, right_side, left_side=True, lower=True, transpose_a=backward
    )


def limits(gram_matrix):
    factor = jnp.linalg.cholesky(gram_matrix)
    norm_scale = jnp.mean(jnp.sqrt(jnp.diagonal(gram_matrix)))
    return (factor, CLIP_COEF * norm_scale, CLIP_RESIDUAL * norm_scale)


def keep_factors(coeffs, residual_squares, coefficient_limit, residual_limit):
    coefficient_norm = jnp.sqrt(jnp.sum(coeffs * coeffs, axis=0))
    keep_coefficient = coefficient_limit / jnp.maximum(coefficient_norm, coefficient_limit)
    keep_residual = residual_limit / jnp.maximum(jnp.sqrt(residual_squares), residual_limit)
    return (keep_coefficient, keep_residual)


def large_group(
    public_input_activations,
    public_output_cotangents,
    public_token_lengths,
    private_input_activations,
    private_output_cotangents,
    private_token_lengths,
    adapter_down_matrix,
    adapter_up_matrix,
    embedding_coefficient_noise,
    residual_down_noise,
    residual_up_noise,
):
    public_projected, public_returned = partial_gram_terms(
        public_input_activations, public_output_cotangents, adapter_down_matrix, adapter_up_matrix
    )
    private_projected, private_returned = partial_gram_terms(
        private_input_activations, private_output_cotangents, adapter_down_matrix, adapter_up_matrix
    )
    public_projected, public_returned, private_projected, private_returned = lax.psum(
        (public_projected, public_returned, private_projected, private_returned), "mp"
    )
    public_down, public_up = shard_grads(
        public_input_activations,
        public_output_cotangents,
        public_token_lengths,
        public_projected,
        public_returned,
    )
    private_down, private_up = shard_grads(
        private_input_activations,
        private_output_cotangents,
        private_token_lengths,
        private_projected,
        private_returned,
    )
    public_down, public_up, private_down, private_up = (
        lax.all_to_all(public_down, "dp", split_axis=1, concat_axis=0, tiled=True),
        lax.all_to_all(public_up, "dp", split_axis=1, concat_axis=0, tiled=True),
        lax.all_to_all(private_down, "dp", split_axis=1, concat_axis=0, tiled=True),
        lax.all_to_all(private_up, "dp", split_axis=1, concat_axis=0, tiled=True),
    )
    public_group = jnp.concatenate([public_down, public_up], axis=1)
    private_group = jnp.concatenate([private_down, private_up], axis=1)
    public_wide = public_group.astype(jnp.float32)
    private_wide = private_group.astype(jnp.float32)
    gram_partial = jnp.einsum(
        "pk,qk->pq", public_group, public_group, preferred_element_type=jnp.float32
    )
    cross_partial = jnp.einsum(
        "pk,qk->pq", public_group, private_group, preferred_element_type=jnp.float32
    )
    square_partial = jnp.sum(private_wide * private_wide, axis=1)
    gram_matrix, cross_terms, square_totals = lax.psum(
        (gram_partial, cross_partial, square_partial), ("dp", "mp")
    )
    factor, coefficient_limit, residual_limit = limits(gram_matrix)
    coeffs = lower_solve(factor, cross_terms, False)
    residual_squares = square_totals - jnp.sum(coeffs * coeffs, axis=0)
    keep_coefficient, keep_residual = keep_factors(
        coeffs, residual_squares, coefficient_limit, residual_limit
    )
    correction = jnp.dot(coeffs, keep_coefficient - keep_residual, precision=PRECISE)
    target = correction + SIGMA_COEF * coefficient_limit * embedding_coefficient_noise
    anchor = lower_solve(factor, target[:, None], True)[:, 0]
    update = jnp.dot(anchor, public_wide, precision=PRECISE) + jnp.dot(
        keep_residual, private_wide, precision=PRECISE
    )
    noise_shard = jnp.concatenate([residual_down_noise[0], residual_up_noise[0]], axis=0)
    private_total = private_input_activations.shape[0] * lax.axis_size("dp")
    update_gain = 1.0 / math.sqrt(private_total * private_input_activations.shape[1])
    result = (update + SIGMA_RESIDUAL * residual_limit * noise_shard) * update_gain
    split_point = public_down.shape[1]
    return (result[None, :split_point], result[None, split_point:])


def solution(mesh):
    placed = (
        P("dp", None, "mp"),
        P("dp", None, "mp"),
        P("dp"),
        P("dp", None, "mp"),
        P("dp", None, "mp"),
        P("dp"),
        P("mp", None),
        P(None, "mp"),
        P(),
        P("mp", "dp"),
        P("mp", "dp"),
    )

    def run(*arrays):
        body = small_group if fits(mesh, arrays[0], arrays[3], arrays[7]) else large_group
        return jax.shard_map(
            body,
            mesh=mesh,
            in_specs=placed,
            out_specs=(P("mp", "dp"), P("mp", "dp")),
            check_vma=False,
        )(*arrays)

    return run
```

```python
import functools
import math

import jax
import jax.numpy as jnp
from jax import lax
from jax.experimental import pallas as pl
from jax.experimental.pallas import tpu as pltpu
from jax.sharding import PartitionSpec as P

CLIP_COEF = 0.5
CLIP_RESIDUAL = 0.7
SIGMA_COEF = 1.0
SIGMA_RESIDUAL = 0.04
PRECISE = lax.Precision.HIGHEST
LANES = 128
GROUP = 4
VMEM = pl.BlockSpec(memory_space=pltpu.VMEM)
HBM = pl.BlockSpec(memory_space=pltpu.HBM)
SMEM = pl.BlockSpec(memory_space=pltpu.SMEM)
BOTH_LAST = (((1,), (1,)), ((), ()))
FIRST_LAST = (((1,), (0,)), ((), ()))
PARAMS = pltpu.CompilerParams(vmem_limit_bytes=40 * 1024 * 1024)


def dot(a, b, dims, precision=None):
    return lax.dot_general(a, b, dims, precision=precision, preferred_element_type=jnp.float32)


def iota(shape, axis):
    return lax.broadcasted_iota(jnp.int32, shape, axis)


def project_kernel(pub_in, pub_out, priv_in, priv_out, down_t, up, *rest):
    out, held, (down_held, up_held, sems) = rest[0], rest[1:5], rest[5:]
    rank = up.shape[0]
    tokens = pub_in.shape[1]
    copies = [
        pltpu.make_async_copy(down_t, down_held, sems.at[0]),
        pltpu.make_async_copy(up, up_held, sems.at[1]),
    ]
    pieces = []
    for inputs, cotangents, inputs_held, cotangents_held in (
        (pub_in, pub_out, held[0], held[1]),
        (priv_in, priv_out, held[2], held[3]),
    ):
        for e in range(inputs.shape[0]):
            pieces += [(down_held, inputs_held.at[e]), (up_held, cotangents_held.at[e])]
            for source, to in ((inputs, inputs_held), (cotangents, cotangents_held)):
                copies.append(
                    pltpu.make_async_copy(source.at[e], to.at[e], sems.at[len(copies)])
                )
    for copy in copies:
        copy.start()
    out[...] = jnp.zeros_like(out)
    for copy in copies[:2]:
        copy.wait()
    for i, (weights, piece) in enumerate(pieces):
        if i % GROUP == 0:
            for copy in copies[2 + i : 2 + i + GROUP]:
                copy.wait()
        slot, half = i // 2, i % 2
        out[half * rank : (half + 1) * rank, slot * LANES : slot * LANES + tokens] = dot(
            weights[...], piece[...], BOTH_LAST
        )


def gradient_kernel(dp, pub_len, priv_len, own, other, pub_in, pub_out, priv_in, priv_out, *rest):
    blocks, down_rows, up_rows = rest[:dp], rest[dp], rest[dp + 1]
    me = lax.axis_index("dp")
    rank = own.shape[0] // 2
    tokens, width = pub_in.shape[1:]
    lanes = width // dp
    per = rank // dp
    slot = 0
    for inputs, cotangents, lengths in (
        (pub_in, pub_out, pub_len),
        (priv_in, priv_out, priv_len),
    ):
        for e in range(inputs.shape[0]):
            at = slice(slot * LANES, slot * LANES + tokens)
            both = own[:, at] + other[:, at]
            live = iota(both.shape, 1) < lengths[e]
            both = jnp.where(live, both, 0.0).astype(jnp.bfloat16)
            for c in range(dp):
                features = slice(c * lanes, (c + 1) * lanes)
                at = slice(c * rank, (c + 1) * rank)
                down_part = dot(both[rank:], inputs[e, :, features], FIRST_LAST)
                up_part = dot(both[:rank], cotangents[e, :, features], FIRST_LAST)
                down_rows[at, :] = down_part.astype(jnp.bfloat16)
                for h in range(lanes // LANES):
                    up_rows[h, at, :] = up_part[:, h * LANES : (h + 1) * LANES]
            for k in range(dp):
                to = me ^ k
                row = slot * 2 * rank
                blocks[k][row : row + rank, :] = down_rows[
                    pl.ds(pl.multiple_of(to * rank, rank), rank), :
                ]
                for h in range(lanes // LANES):
                    pieces = [
                        up_rows[h, pl.ds(to * per + r, dp, stride=rank), :] for r in range(per)
                    ]
                    blocks[k][row + rank : row + 2 * rank, h * LANES : (h + 1) * LANES] = (
                        jnp.concatenate(pieces, axis=0).astype(jnp.bfloat16)
                    )
            slot += 1


def gram_kernel(order, n_pub, n_priv, *refs):
    dp = len(order)
    blocks, group, out = refs[:dp], refs[dp], refs[dp + 1]
    me = lax.axis_index("dp")
    rows = blocks[0].shape[0] // (n_pub + n_priv)
    pub_rows, priv_rows = n_pub * rows, n_priv * rows
    for k, block in zip(order, blocks):
        source = me ^ k
        group[pl.ds(pl.multiple_of(source * pub_rows, pub_rows), pub_rows), :] = block[:pub_rows]
        group[
            pl.ds(pl.multiple_of(dp * pub_rows + source * priv_rows, priv_rows), priv_rows), :
        ] = block[pub_rows:]
    publics = dp * n_pub
    span = publics * rows
    lanes = group.shape[1]
    public = group[:span, :]
    total = jnp.zeros((publics, LANES), jnp.float32)
    same = iota((span, span), 0) % rows == iota((span, span), 1) % rows
    squares = []
    for c in range(group.shape[0] // span):
        part = group[c * span : (c + 1) * span, :]
        products = jnp.where(same, dot(public, part, BOTH_LAST), 0.0)
        products = jnp.sum(products.reshape(publics, rows, span), axis=1)
        pick = (iota((span, LANES), 0) // rows + c * publics == iota((span, LANES), 1)).astype(
            jnp.float32
        )
        total += dot(products, pick, FIRST_LAST, PRECISE)
        if c > 0:
            wide = part.astype(jnp.float32)
            squares.append(jnp.sum((wide * wide).reshape(publics, rows, lanes), axis=1))
    examples = group.shape[0] // rows
    before = LANES // 2 + publics
    after = LANES // 2 - examples
    stacked = jnp.concatenate(
        [jnp.zeros((before, lanes), jnp.float32)]
        + squares
        + ([jnp.zeros((after, lanes), jnp.float32)] if after else []),
        axis=0,
    )
    total_squares = dot(jnp.ones((publics, lanes), jnp.float32), stacked, BOTH_LAST, PRECISE)
    total += jnp.where(iota(total.shape, 0) == 0, total_squares, 0.0)
    for d in range(out.shape[0]):
        out[d] = total


def update_kernel(gain, shares, group, noise, down_noise, up_noise, down, up):
    total = shares[0]
    for d in range(1, shares.shape[0]):
        total = total + shares[d]
    publics = total.shape[0]
    shape = total.shape
    row, lane = iota(shape, 0), iota(shape, 1)
    half = LANES // 2
    squares = pltpu.roll(total, half, 1)[0:1]
    gram_diagonal = jnp.sum(jnp.where(row == lane, total, 0.0), axis=1, keepdims=True)
    norm_scale = jnp.mean(jnp.sqrt(gram_diagonal), axis=0, keepdims=True)
    coefficient_limit = CLIP_COEF * norm_scale
    residual_limit = CLIP_RESIDUAL * norm_scale
    work = jnp.where(lane < half, total, jnp.where(lane == row + half, 1.0, 0.0))
    for j in range(publics):
        inverse = lax.rsqrt(work[j : j + 1, j : j + 1])
        pivot = work[j : j + 1, :] * inverse
        column = work[:, j : j + 1] * inverse
        work = jnp.where(row > j, work - column * pivot, jnp.where(row == j, pivot, work))
    examples = group.shape[0] * publics // (publics * (2 * up.shape[1] // group.shape[1]))
    private = jnp.logical_and(lane >= publics, lane < examples)
    coeffs = jnp.where(private, work, 0.0)
    coefficient_squares = jnp.sum(coeffs * coeffs, axis=0, keepdims=True)
    residual_squares = jnp.maximum(squares - coefficient_squares, 0.0)
    keep_coefficient = coefficient_limit / jnp.maximum(
        jnp.sqrt(coefficient_squares), coefficient_limit
    )
    keep_residual = residual_limit / jnp.maximum(jnp.sqrt(residual_squares), residual_limit)
    correction = jnp.sum(
        coeffs * (keep_coefficient - keep_residual), axis=1, keepdims=True
    )
    noise_column = jnp.zeros((publics, 1), jnp.float32)
    for j in range(publics):
        noise_column = jnp.where(iota((publics, 1), 0) == j, noise[j], noise_column)
    target = correction + SIGMA_COEF * coefficient_limit * noise_column
    inverse_factor = jnp.where(lane >= half, work, 0.0)
    anchor = pltpu.roll(jnp.sum(inverse_factor * target, axis=0, keepdims=True), half, 1)
    weights = jnp.where(lane[0:1] < publics, anchor, keep_residual)

    lanes = group.shape[1]
    rows = group.shape[0] // examples
    rank = rows // 2
    acc = jnp.zeros((rows, lanes), jnp.float32)
    for i in range(examples):
        acc = acc + weights[:, i : i + 1] * group[i * rows : (i + 1) * rows, :].astype(jnp.float32)
    scale = SIGMA_RESIDUAL * residual_limit
    per = LANES // rank
    flat = lanes * rank // LANES
    wide = jnp.concatenate([acc[:rank]] * per, axis=0)
    wide = jnp.where(iota((LANES, lanes), 0) // rank == iota((LANES, lanes), 1) % per, wide, 0.0)
    pick = (iota((flat, lanes), 0) == iota((flat, lanes), 1) // per).astype(jnp.float32)
    turned = dot(pick, wide, BOTH_LAST, PRECISE)
    for a in range(flat):
        at = slice(a * LANES, (a + 1) * LANES)
        down[0:1, at] = (turned[a : a + 1] + scale * down_noise[0:1, at]) * gain
    for a in range(rank):
        at = slice(a * lanes, (a + 1) * lanes)
        up[0:1, at] = (acc[rank + a : rank + a + 1] + scale * up_noise[0:1, at]) * gain


def exchange(x, axis, step):
    return lax.ppermute(x, axis, [(s, s ^ step) for s in range(lax.axis_size(axis))])


def small_group(
    pub_in, pub_out, pub_len, priv_in, priv_out, priv_len, down, up, noise, down_noise, up_noise
):
    dp, mp = lax.axis_size("dp"), lax.axis_size("mp")
    n_pub, tokens, width = pub_in.shape
    n_priv = priv_in.shape[0]
    examples = n_pub + n_priv
    rank = up.shape[0]
    lanes = width // dp
    f32, bf16 = jnp.float32, jnp.bfloat16

    own, *held = pl.pallas_call(
        project_kernel,
        out_shape=[jax.ShapeDtypeStruct((2 * rank, examples * LANES), f32)]
        + [jax.ShapeDtypeStruct(x.shape, bf16) for x in (pub_in, pub_out, priv_in, priv_out)],
        in_specs=[HBM] * 6,
        out_specs=[VMEM] * 5,
        scratch_shapes=[
            pltpu.VMEM(up.shape, bf16),
            pltpu.VMEM(up.shape, bf16),
            pltpu.SemaphoreType.DMA((2 + 2 * examples,)),
        ],
        compiler_params=PARAMS,
        name="project",
    )(
        *(
            pltpu.with_memory_space_constraint(x, pltpu.HBM)
            for x in (pub_in, pub_out, priv_in, priv_out, down.T, up)
        )
    )
    step = 1
    while step < mp:
        other = exchange(own, "mp", step)
        step *= 2
        if step < mp:
            own = own + other

    block = jax.ShapeDtypeStruct((examples * 2 * rank, lanes), bf16)
    blocks = pl.pallas_call(
        functools.partial(gradient_kernel, dp),
        out_shape=[block] * dp,
        in_specs=[SMEM] * 2 + [VMEM] * 6,
        out_specs=[VMEM] * dp,
        scratch_shapes=[
            pltpu.VMEM((dp * rank, lanes), bf16),
            pltpu.VMEM((lanes // LANES, dp * rank, LANES), f32),
        ],
        compiler_params=PARAMS,
        name="gradients",
    )(pub_len, priv_len, own, other, *held)
    ranked = sorted(range(1, dp), key=lambda k: (k & 1, k if k & 1 else -k))
    far, near = [k for k in ranked if 2 * k >= dp], [k for k in ranked if 2 * k < dp]
    order = [k for pair in zip(far, near + [0]) for k in pair]
    blocks = [exchange(blocks[k], "dp", k) if k else blocks[k] for k in order]

    group, shares = pl.pallas_call(
        functools.partial(gram_kernel, order, n_pub, n_priv),
        out_shape=[
            jax.ShapeDtypeStruct((dp * examples * 2 * rank, lanes), bf16),
            jax.ShapeDtypeStruct((dp * mp, dp * n_pub, LANES), f32),
        ],
        in_specs=[VMEM] * dp,
        out_specs=[VMEM] * 2,
        compiler_params=PARAMS,
        name="inner_products",
    )(*blocks)
    shares = lax.all_to_all(shares, ("dp", "mp"), 0, 0, tiled=True)

    gain = 1.0 / math.sqrt(n_priv * dp * tokens)
    return pl.pallas_call(
        functools.partial(update_kernel, gain),
        out_shape=[
            jax.ShapeDtypeStruct(down_noise.shape, f32),
            jax.ShapeDtypeStruct(up_noise.shape, f32),
        ],
        in_specs=[VMEM, VMEM, SMEM, VMEM, VMEM],
        out_specs=[VMEM] * 2,
        compiler_params=PARAMS,
        name="update",
    )(shares, group, noise, down_noise, up_noise)


def fits(mesh, pub_in, priv_in, up):
    dp = mesh.shape["dp"]
    width = pub_in.shape[2] // mesh.shape["mp"]
    publics = pub_in.shape[0]
    return (
        up.shape[0] == 16
        and dp in (2, 4, 8)
        and width % (dp * LANES) == 0
        and publics == 8
        and priv_in.shape[0] % 8 == 0
        and publics + priv_in.shape[0] <= LANES // 2
        and pub_in.shape[1] <= LANES
    )


def partial_gram_terms(
    input_activations, output_cotangents, adapter_down_matrix, adapter_up_matrix
):
    projected_gradients = jnp.einsum(
        "umo,ov->umv", input_activations, adapter_down_matrix, preferred_element_type=jnp.float32
    )
    reconstructed_gradients = jnp.einsum(
        "fpb,ab->fpa", output_cotangents, adapter_up_matrix, preferred_element_type=jnp.float32
    )
    return (projected_gradients, reconstructed_gradients)


def shard_grads(
    input_activations,
    output_cotangents,
    token_lengths,
    projected_gradients,
    reconstructed_gradients,
):
    example_total_count = input_activations.shape[0]
    token_steps = input_activations.shape[1]
    positions = lax.broadcasted_iota(jnp.int32, (example_total_count, token_steps), 1)
    live_mask = (positions < token_lengths[:, None]).astype(jnp.float32)[:, :, None]
    projected_live = (projected_gradients * live_mask).astype(jnp.bfloat16)
    returned_live = (reconstructed_gradients * live_mask).astype(jnp.bfloat16)
    grad_down = jnp.einsum(
        "etd,etr->edr", input_activations, returned_live, preferred_element_type=jnp.float32
    ).astype(jnp.bfloat16)
    grad_up = jnp.einsum(
        "etr,eto->ero", projected_live, output_cotangents, preferred_element_type=jnp.float32
    ).astype(jnp.bfloat16)
    return (grad_down.reshape(example_total_count, -1), grad_up.reshape(example_total_count, -1))


def lower_solve(factor, right_side, backward):
    return lax.linalg.triangular_solve(
        factor, right_side, left_side=True, lower=True, transpose_a=backward
    )


def limits(gram_matrix):
    factor = jnp.linalg.cholesky(gram_matrix)
    norm_scale = jnp.mean(jnp.sqrt(jnp.diagonal(gram_matrix)))
    return (factor, CLIP_COEF * norm_scale, CLIP_RESIDUAL * norm_scale)


def keep_factors(coeffs, residual_squares, coefficient_limit, residual_limit):
    coefficient_norm = jnp.sqrt(jnp.sum(coeffs * coeffs, axis=0))
    keep_coefficient = coefficient_limit / jnp.maximum(coefficient_norm, coefficient_limit)
    keep_residual = residual_limit / jnp.maximum(jnp.sqrt(residual_squares), residual_limit)
    return (keep_coefficient, keep_residual)


def large_group(
    public_input_activations,
    public_output_cotangents,
    public_token_lengths,
    private_input_activations,
    private_output_cotangents,
    private_token_lengths,
    adapter_down_matrix,
    adapter_up_matrix,
    embedding_coefficient_noise,
    residual_down_noise,
    residual_up_noise,
):
    public_projected, public_returned = partial_gram_terms(
        public_input_activations, public_output_cotangents, adapter_down_matrix, adapter_up_matrix
    )
    private_projected, private_returned = partial_gram_terms(
        private_input_activations, private_output_cotangents, adapter_down_matrix, adapter_up_matrix
    )
    public_projected, public_returned, private_projected, private_returned = lax.psum(
        (public_projected, public_returned, private_projected, private_returned), "mp"
    )
    public_down, public_up = shard_grads(
        public_input_activations,
        public_output_cotangents,
        public_token_lengths,
        public_projected,
        public_returned,
    )
    private_down, private_up = shard_grads(
        private_input_activations,
        private_output_cotangents,
        private_token_lengths,
        private_projected,
        private_returned,
    )
    public_down, public_up, private_down, private_up = (
        lax.all_to_all(public_down, "dp", split_axis=1, concat_axis=0, tiled=True),
        lax.all_to_all(public_up, "dp", split_axis=1, concat_axis=0, tiled=True),
        lax.all_to_all(private_down, "dp", split_axis=1, concat_axis=0, tiled=True),
        lax.all_to_all(private_up, "dp", split_axis=1, concat_axis=0, tiled=True),
    )
    public_group = jnp.concatenate([public_down, public_up], axis=1)
    private_group = jnp.concatenate([private_down, private_up], axis=1)
    public_wide = public_group.astype(jnp.float32)
    private_wide = private_group.astype(jnp.float32)
    gram_partial = jnp.einsum(
        "pk,qk->pq", public_group, public_group, preferred_element_type=jnp.float32
    )
    cross_partial = jnp.einsum(
        "pk,qk->pq", public_group, private_group, preferred_element_type=jnp.float32
    )
    square_partial = jnp.sum(private_wide * private_wide, axis=1)
    gram_matrix, cross_terms, square_totals = lax.psum(
        (gram_partial, cross_partial, square_partial), ("dp", "mp")
    )
    factor, coefficient_limit, residual_limit = limits(gram_matrix)
    coeffs = lower_solve(factor, cross_terms, False)
    residual_squares = square_totals - jnp.sum(coeffs * coeffs, axis=0)
    keep_coefficient, keep_residual = keep_factors(
        coeffs, residual_squares, coefficient_limit, residual_limit
    )
    correction = jnp.dot(coeffs, keep_coefficient - keep_residual, precision=PRECISE)
    target = correction + SIGMA_COEF * coefficient_limit * embedding_coefficient_noise
    anchor = lower_solve(factor, target[:, None], True)[:, 0]
    update = jnp.dot(anchor, public_wide, precision=PRECISE) + jnp.dot(
        keep_residual, private_wide, precision=PRECISE
    )
    noise_shard = jnp.concatenate([residual_down_noise[0], residual_up_noise[0]], axis=0)
    private_total = private_input_activations.shape[0] * lax.axis_size("dp")
    update_gain = 1.0 / math.sqrt(private_total * private_input_activations.shape[1])
    result = (update + SIGMA_RESIDUAL * residual_limit * noise_shard) * update_gain
    split_point = public_down.shape[1]
    return (result[None, :split_point], result[None, split_point:])


def solution(mesh):
    placed = (
        P("dp", None, "mp"),
        P("dp", None, "mp"),
        P("dp"),
        P("dp", None, "mp"),
        P("dp", None, "mp"),
        P("dp"),
        P("mp", None),
        P(None, "mp"),
        P(),
        P("mp", "dp"),
        P("mp", "dp"),
    )

    def run(*arrays):
        body = small_group if fits(mesh, arrays[0], arrays[3], arrays[7]) else large_group
        return jax.shard_map(
            body,
            mesh=mesh,
            in_specs=placed,
            out_specs=(P("mp", "dp"), P("mp", "dp")),
            check_vma=False,
        )(*arrays)

    return run
```

```python
import functools
import math

import jax
import jax.numpy as jnp
from jax import lax
from jax.experimental import pallas as pl
from jax.experimental.pallas import tpu as pltpu
from jax.sharding import PartitionSpec as P

CLIP_COEF = 0.5
CLIP_RESIDUAL = 0.7
SIGMA_COEF = 1.0
SIGMA_RESIDUAL = 0.04
PRECISE = lax.Precision.HIGHEST
LANES = 128
GROUP = 4
VMEM = pl.BlockSpec(memory_space=pltpu.VMEM)
HBM = pl.BlockSpec(memory_space=pltpu.HBM)
SMEM = pl.BlockSpec(memory_space=pltpu.SMEM)
BOTH_LAST = (((1,), (1,)), ((), ()))
FIRST_LAST = (((1,), (0,)), ((), ()))
PARAMS = pltpu.CompilerParams(vmem_limit_bytes=40 * 1024 * 1024)


def dot(a, b, dims, precision=None):
    return lax.dot_general(a, b, dims, precision=precision, preferred_element_type=jnp.float32)


def iota(shape, axis):
    return lax.broadcasted_iota(jnp.int32, shape, axis)


def exact_parts(x):
    high = x.astype(jnp.bfloat16)
    rest = x - high.astype(jnp.float32)
    middle = rest.astype(jnp.bfloat16)
    return [high, middle, (rest - middle.astype(jnp.float32)).astype(jnp.bfloat16)]


def project_kernel(pub_in, pub_out, priv_in, priv_out, down_t, up, *rest):
    out, held, (down_held, up_held, sems) = rest[0], rest[1:5], rest[5:]
    rank = up.shape[0]
    tokens = pub_in.shape[1]
    copies = [
        pltpu.make_async_copy(down_t, down_held, sems.at[0]),
        pltpu.make_async_copy(up, up_held, sems.at[1]),
    ]
    pieces = []
    for inputs, cotangents, inputs_held, cotangents_held in (
        (pub_in, pub_out, held[0], held[1]),
        (priv_in, priv_out, held[2], held[3]),
    ):
        for e in range(inputs.shape[0]):
            pieces += [(down_held, inputs_held.at[e]), (up_held, cotangents_held.at[e])]
            for source, to in ((inputs, inputs_held), (cotangents, cotangents_held)):
                copies.append(
                    pltpu.make_async_copy(source.at[e], to.at[e], sems.at[len(copies)])
                )
    for copy in copies:
        copy.start()
    out[...] = jnp.zeros_like(out)
    for copy in copies[:2]:
        copy.wait()
    for i, (weights, piece) in enumerate(pieces):
        if i % GROUP == 0:
            for copy in copies[2 + i : 2 + i + GROUP]:
                copy.wait()
        slot, half = i // 2, i % 2
        out[half * rank : (half + 1) * rank, slot * LANES : slot * LANES + tokens] = dot(
            weights[...], piece[...], BOTH_LAST
        )


def gradient_kernel(dp, pub_len, priv_len, own, other, pub_in, pub_out, priv_in, priv_out, *rest):
    blocks, down_rows, up_rows = rest[:dp], rest[dp], rest[dp + 1]
    me = lax.axis_index("dp")
    rank = own.shape[0] // 2
    tokens, width = pub_in.shape[1:]
    lanes = width // dp
    per = rank // dp
    slot = 0
    for inputs, cotangents, lengths in (
        (pub_in, pub_out, pub_len),
        (priv_in, priv_out, priv_len),
    ):
        for e in range(inputs.shape[0]):
            at = slice(slot * LANES, slot * LANES + tokens)
            both = own[:, at] + other[:, at]
            live = iota(both.shape, 1) < lengths[e]
            both = jnp.where(live, both, 0.0).astype(jnp.bfloat16)
            for c in range(dp):
                features = slice(c * lanes, (c + 1) * lanes)
                at = slice(c * rank, (c + 1) * rank)
                down_part = dot(both[rank:], inputs[e, :, features], FIRST_LAST)
                up_part = dot(both[:rank], cotangents[e, :, features], FIRST_LAST)
                down_rows[at, :] = down_part.astype(jnp.bfloat16)
                for h in range(lanes // LANES):
                    up_rows[h, at, :] = up_part[:, h * LANES : (h + 1) * LANES]
            for k in range(dp):
                to = me ^ k
                row = slot * 2 * rank
                blocks[k][row : row + rank, :] = down_rows[
                    pl.ds(pl.multiple_of(to * rank, rank), rank), :
                ]
                for h in range(lanes // LANES):
                    pieces = [
                        up_rows[h, pl.ds(to * per + r, dp, stride=rank), :] for r in range(per)
                    ]
                    blocks[k][row + rank : row + 2 * rank, h * LANES : (h + 1) * LANES] = (
                        jnp.concatenate(pieces, axis=0).astype(jnp.bfloat16)
                    )
            slot += 1


def gram_kernel(order, n_pub, n_priv, *refs):
    dp = len(order)
    blocks, group, out = refs[:dp], refs[dp], refs[dp + 1]
    me = lax.axis_index("dp")
    rows = blocks[0].shape[0] // (n_pub + n_priv)
    pub_rows, priv_rows = n_pub * rows, n_priv * rows
    for k, block in zip(order, blocks):
        source = me ^ k
        group[pl.ds(pl.multiple_of(source * pub_rows, pub_rows), pub_rows), :] = block[:pub_rows]
        group[
            pl.ds(pl.multiple_of(dp * pub_rows + source * priv_rows, priv_rows), priv_rows), :
        ] = block[pub_rows:]
    publics, privates = dp * n_pub, dp * n_priv
    span = publics * rows
    lanes = group.shape[1]
    public = group[:span, :]
    same = iota((span, span), 0) % rows == iota((span, span), 1) % rows
    parts, squares = [], []
    for c in range(group.shape[0] // span):
        part = group[c * span : (c + 1) * span, :]
        products = jnp.where(same, dot(public, part, BOTH_LAST), 0.0)
        products = jnp.sum(products.reshape(publics, rows // 8, 8, span), axis=1)
        parts += exact_parts(products.reshape(publics * 8, span))
        if c > 0:
            wide = part.astype(jnp.float32)
            squares.append(jnp.sum((wide * wide).reshape(publics, rows, lanes), axis=1))
    pick = (iota((span, LANES), 0) // rows == iota((span, LANES), 1)).astype(jnp.bfloat16)
    sums = dot(jnp.concatenate(parts, axis=0), pick, FIRST_LAST).reshape(-1, 3, publics * 8, LANES)
    total = jnp.zeros((publics * 8, LANES), jnp.float32)
    for c in range(sums.shape[0]):
        total += pltpu.roll(sums[c, 0] + sums[c, 1] + sums[c, 2], c * publics, 1)
    total = jnp.sum(total.reshape(publics, 8, LANES), axis=1)
    half, each = LANES // 2, privates // 2
    squares = jnp.concatenate(squares, axis=0)
    used = publics + privates
    gap = jnp.zeros((used, lanes), jnp.float32)
    rest = jnp.zeros((half - used - each, lanes), jnp.float32)
    stacked = jnp.concatenate([gap, squares[:each], rest, gap, squares[each:], rest], axis=0)
    total_squares = dot(jnp.ones((8, lanes), jnp.float32), stacked, BOTH_LAST, PRECISE)
    short = publics // 2
    lane = iota((short, LANES), 1)
    packed = jnp.where(lane < half, total[:short], pltpu.roll(total[short:], half, 1))
    beside = jnp.logical_and(lane % half >= used, iota((short, LANES), 0) == 0)
    packed = jnp.where(beside, total_squares[:short], packed)
    for d in range(out.shape[0]):
        out[d] = packed


def update_kernel(gain, shares, group, noise, down_noise, up_noise, down, up):
    packed = shares[0]
    for d in range(1, shares.shape[0]):
        packed = packed + shares[d]
    publics = 2 * packed.shape[0]
    half = LANES // 2
    rows = 2 * up.shape[1] // group.shape[1]
    examples = group.shape[0] // rows
    each = (examples - publics) // 2
    total = jnp.concatenate([packed, pltpu.roll(packed, half, 1)], axis=0)
    row, lane = iota(total.shape, 0), iota(total.shape, 1)
    squares = jnp.where(
        lane[0:1] < publics + each,
        pltpu.roll(packed[0:1], LANES - (examples - publics), 1),
        pltpu.roll(packed[0:1], LANES - (half + each), 1),
    )
    gram_diagonal = jnp.sum(jnp.where(row == lane, total, 0.0), axis=1, keepdims=True)
    norm_scale = jnp.mean(jnp.sqrt(gram_diagonal), axis=0, keepdims=True)
    coefficient_limit = CLIP_COEF * norm_scale
    residual_limit = CLIP_RESIDUAL * norm_scale
    work = jnp.where(lane < half, total, jnp.where(lane == row + half, 1.0, 0.0))
    for j in range(0, publics, 2):
        first = jnp.broadcast_to(work[:, j : j + 1], work.shape)
        second = jnp.broadcast_to(work[:, j + 1 : j + 2], work.shape)
        inverse = lax.rsqrt(first[j : j + 1])
        pivot = work[j : j + 1] * inverse
        below = first[j + 1 : j + 2] * inverse
        next_inverse = lax.rsqrt(second[j + 1 : j + 2] - below * below)
        next_pivot = (work[j + 1 : j + 2] - below * pivot) * next_inverse
        first = first * inverse
        second = (second - first * below) * next_inverse
        work = jnp.where(
            row > j + 1,
            work - first * pivot - second * next_pivot,
            jnp.where(row == j, pivot, jnp.where(row == j + 1, next_pivot, work)),
        )
    private = jnp.logical_and(lane >= publics, lane < examples)
    coeffs = jnp.where(private, work, 0.0)
    coefficient_squares = jnp.sum(coeffs * coeffs, axis=0, keepdims=True)
    residual_squares = jnp.maximum(squares - coefficient_squares, 0.0)
    keep_coefficient = coefficient_limit / jnp.maximum(
        jnp.sqrt(coefficient_squares), coefficient_limit
    )
    keep_residual = residual_limit / jnp.maximum(jnp.sqrt(residual_squares), residual_limit)
    correction = jnp.sum(
        coeffs * (keep_coefficient - keep_residual), axis=1, keepdims=True
    )
    noise_column = jnp.zeros((publics, 1), jnp.float32)
    for j in range(publics):
        noise_column = jnp.where(iota((publics, 1), 0) == j, noise[j], noise_column)
    target = correction + SIGMA_COEF * coefficient_limit * noise_column
    inverse_factor = jnp.where(lane >= half, work, 0.0)
    anchor = pltpu.roll(jnp.sum(inverse_factor * target, axis=0, keepdims=True), half, 1)
    weights = jnp.where(lane[0:1] < publics, anchor, keep_residual)

    lanes = group.shape[1]
    rank = rows // 2
    acc = jnp.zeros((rows, lanes), jnp.float32)
    for i in range(examples):
        acc = acc + weights[:, i : i + 1] * group[i * rows : (i + 1) * rows, :].astype(jnp.float32)
    scale = SIGMA_RESIDUAL * residual_limit
    per = LANES // rank
    flat = lanes * rank // LANES
    wide = jnp.concatenate([acc[:rank]] * per, axis=0)
    wide = jnp.where(iota((LANES, lanes), 0) // rank == iota((LANES, lanes), 1) % per, wide, 0.0)
    pick = (iota((flat, lanes), 0) == iota((flat, lanes), 1) // per).astype(jnp.bfloat16)
    parts = dot(pick, jnp.concatenate(exact_parts(wide), axis=0), BOTH_LAST)
    turned = parts[:, :LANES] + parts[:, LANES : 2 * LANES] + parts[:, 2 * LANES :]
    for a in range(flat):
        at = slice(a * LANES, (a + 1) * LANES)
        down[0:1, at] = (turned[a : a + 1] + scale * down_noise[0:1, at]) * gain
    for a in range(rank):
        at = slice(a * lanes, (a + 1) * lanes)
        up[0:1, at] = (acc[rank + a : rank + a + 1] + scale * up_noise[0:1, at]) * gain


def exchange(x, axis, step):
    return lax.ppermute(x, axis, [(s, s ^ step) for s in range(lax.axis_size(axis))])


def small_group(
    pub_in, pub_out, pub_len, priv_in, priv_out, priv_len, down, up, noise, down_noise, up_noise
):
    dp, mp = lax.axis_size("dp"), lax.axis_size("mp")
    n_pub, tokens, width = pub_in.shape
    n_priv = priv_in.shape[0]
    examples = n_pub + n_priv
    rank = up.shape[0]
    lanes = width // dp
    f32, bf16 = jnp.float32, jnp.bfloat16

    own, *held = pl.pallas_call(
        project_kernel,
        out_shape=[jax.ShapeDtypeStruct((2 * rank, examples * LANES), f32)]
        + [jax.ShapeDtypeStruct(x.shape, bf16) for x in (pub_in, pub_out, priv_in, priv_out)],
        in_specs=[HBM] * 6,
        out_specs=[VMEM] * 5,
        scratch_shapes=[
            pltpu.VMEM(up.shape, bf16),
            pltpu.VMEM(up.shape, bf16),
            pltpu.SemaphoreType.DMA((2 + 2 * examples,)),
        ],
        compiler_params=PARAMS,
        name="project",
    )(
        *(
            pltpu.with_memory_space_constraint(x, pltpu.HBM)
            for x in (pub_in, pub_out, priv_in, priv_out, down.T, up)
        )
    )
    step = 1
    while step < mp:
        other = exchange(own, "mp", step)
        step *= 2
        if step < mp:
            own = own + other

    block = jax.ShapeDtypeStruct((examples * 2 * rank, lanes), bf16)
    blocks = pl.pallas_call(
        functools.partial(gradient_kernel, dp),
        out_shape=[block] * dp,
        in_specs=[SMEM] * 2 + [VMEM] * 6,
        out_specs=[VMEM] * dp,
        scratch_shapes=[
            pltpu.VMEM((dp * rank, lanes), bf16),
            pltpu.VMEM((lanes // LANES, dp * rank, LANES), f32),
        ],
        compiler_params=PARAMS,
        name="gradients",
    )(pub_len, priv_len, own, other, *held)
    ranked = sorted(range(1, dp), key=lambda k: (k & 1, k if k & 1 else -k))
    far, near = [k for k in ranked if 2 * k >= dp], [k for k in ranked if 2 * k < dp]
    order = [k for pair in zip(far, near + [0]) for k in pair]
    blocks = [exchange(blocks[k], "dp", k) if k else blocks[k] for k in order]

    group, shares = pl.pallas_call(
        functools.partial(gram_kernel, order, n_pub, n_priv),
        out_shape=[
            jax.ShapeDtypeStruct((dp * examples * 2 * rank, lanes), bf16),
            jax.ShapeDtypeStruct((dp * mp, dp * n_pub // 2, LANES), f32),
        ],
        in_specs=[VMEM] * dp,
        out_specs=[VMEM] * 2,
        compiler_params=PARAMS,
        name="inner_products",
    )(*blocks)
    shares = lax.all_to_all(shares, ("dp", "mp"), 0, 0, tiled=True)

    gain = 1.0 / math.sqrt(n_priv * dp * tokens)
    return pl.pallas_call(
        functools.partial(update_kernel, gain),
        out_shape=[
            jax.ShapeDtypeStruct(down_noise.shape, f32),
            jax.ShapeDtypeStruct(up_noise.shape, f32),
        ],
        in_specs=[VMEM, VMEM, SMEM, VMEM, VMEM],
        out_specs=[VMEM] * 2,
        compiler_params=PARAMS,
        name="update",
    )(shares, group, noise, down_noise, up_noise)


def fits(mesh, pub_in, priv_in, up):
    dp = mesh.shape["dp"]
    width = pub_in.shape[2] // mesh.shape["mp"]
    publics = pub_in.shape[0]
    return (
        up.shape[0] == 16
        and dp in (2, 4, 8)
        and width % (dp * LANES) == 0
        and publics == 8
        and priv_in.shape[0] % 8 == 0
        and publics + priv_in.shape[0] + priv_in.shape[0] // 2 <= LANES // 2
        and pub_in.shape[1] <= LANES
    )


def partial_gram_terms(
    input_activations, output_cotangents, adapter_down_matrix, adapter_up_matrix
):
    projected_gradients = jnp.einsum(
        "umo,ov->umv", input_activations, adapter_down_matrix, preferred_element_type=jnp.float32
    )
    reconstructed_gradients = jnp.einsum(
        "fpb,ab->fpa", output_cotangents, adapter_up_matrix, preferred_element_type=jnp.float32
    )
    return (projected_gradients, reconstructed_gradients)


def shard_grads(
    input_activations,
    output_cotangents,
    token_lengths,
    projected_gradients,
    reconstructed_gradients,
):
    example_total_count = input_activations.shape[0]
    token_steps = input_activations.shape[1]
    positions = lax.broadcasted_iota(jnp.int32, (example_total_count, token_steps), 1)
    live_mask = (positions < token_lengths[:, None]).astype(jnp.float32)[:, :, None]
    projected_live = (projected_gradients * live_mask).astype(jnp.bfloat16)
    returned_live = (reconstructed_gradients * live_mask).astype(jnp.bfloat16)
    grad_down = jnp.einsum(
        "etd,etr->edr", input_activations, returned_live, preferred_element_type=jnp.float32
    ).astype(jnp.bfloat16)
    grad_up = jnp.einsum(
        "etr,eto->ero", projected_live, output_cotangents, preferred_element_type=jnp.float32
    ).astype(jnp.bfloat16)
    return (grad_down.reshape(example_total_count, -1), grad_up.reshape(example_total_count, -1))


def lower_solve(factor, right_side, backward):
    return lax.linalg.triangular_solve(
        factor, right_side, left_side=True, lower=True, transpose_a=backward
    )


def limits(gram_matrix):
    factor = jnp.linalg.cholesky(gram_matrix)
    norm_scale = jnp.mean(jnp.sqrt(jnp.diagonal(gram_matrix)))
    return (factor, CLIP_COEF * norm_scale, CLIP_RESIDUAL * norm_scale)


def keep_factors(coeffs, residual_squares, coefficient_limit, residual_limit):
    coefficient_norm = jnp.sqrt(jnp.sum(coeffs * coeffs, axis=0))
    keep_coefficient = coefficient_limit / jnp.maximum(coefficient_norm, coefficient_limit)
    keep_residual = residual_limit / jnp.maximum(jnp.sqrt(residual_squares), residual_limit)
    return (keep_coefficient, keep_residual)


def large_group(
    public_input_activations,
    public_output_cotangents,
    public_token_lengths,
    private_input_activations,
    private_output_cotangents,
    private_token_lengths,
    adapter_down_matrix,
    adapter_up_matrix,
    embedding_coefficient_noise,
    residual_down_noise,
    residual_up_noise,
):
    public_projected, public_returned = partial_gram_terms(
        public_input_activations, public_output_cotangents, adapter_down_matrix, adapter_up_matrix
    )
    private_projected, private_returned = partial_gram_terms(
        private_input_activations, private_output_cotangents, adapter_down_matrix, adapter_up_matrix
    )
    public_projected, public_returned, private_projected, private_returned = lax.psum(
        (public_projected, public_returned, private_projected, private_returned), "mp"
    )
    public_down, public_up = shard_grads(
        public_input_activations,
        public_output_cotangents,
        public_token_lengths,
        public_projected,
        public_returned,
    )
    private_down, private_up = shard_grads(
        private_input_activations,
        private_output_cotangents,
        private_token_lengths,
        private_projected,
        private_returned,
    )
    public_down, public_up, private_down, private_up = (
        lax.all_to_all(public_down, "dp", split_axis=1, concat_axis=0, tiled=True),
        lax.all_to_all(public_up, "dp", split_axis=1, concat_axis=0, tiled=True),
        lax.all_to_all(private_down, "dp", split_axis=1, concat_axis=0, tiled=True),
        lax.all_to_all(private_up, "dp", split_axis=1, concat_axis=0, tiled=True),
    )
    public_group = jnp.concatenate([public_down, public_up], axis=1)
    private_group = jnp.concatenate([private_down, private_up], axis=1)
    public_wide = public_group.astype(jnp.float32)
    private_wide = private_group.astype(jnp.float32)
    gram_partial = jnp.einsum(
        "pk,qk->pq", public_group, public_group, preferred_element_type=jnp.float32
    )
    cross_partial = jnp.einsum(
        "pk,qk->pq", public_group, private_group, preferred_element_type=jnp.float32
    )
    square_partial = jnp.sum(private_wide * private_wide, axis=1)
    gram_matrix, cross_terms, square_totals = lax.psum(
        (gram_partial, cross_partial, square_partial), ("dp", "mp")
    )
    factor, coefficient_limit, residual_limit = limits(gram_matrix)
    coeffs = lower_solve(factor, cross_terms, False)
    residual_squares = square_totals - jnp.sum(coeffs * coeffs, axis=0)
    keep_coefficient, keep_residual = keep_factors(
        coeffs, residual_squares, coefficient_limit, residual_limit
    )
    correction = jnp.dot(coeffs, keep_coefficient - keep_residual, precision=PRECISE)
    target = correction + SIGMA_COEF * coefficient_limit * embedding_coefficient_noise
    anchor = lower_solve(factor, target[:, None], True)[:, 0]
    update = jnp.dot(anchor, public_wide, precision=PRECISE) + jnp.dot(
        keep_residual, private_wide, precision=PRECISE
    )
    noise_shard = jnp.concatenate([residual_down_noise[0], residual_up_noise[0]], axis=0)
    private_total = private_input_activations.shape[0] * lax.axis_size("dp")
    update_gain = 1.0 / math.sqrt(private_total * private_input_activations.shape[1])
    result = (update + SIGMA_RESIDUAL * residual_limit * noise_shard) * update_gain
    split_point = public_down.shape[1]
    return (result[None, :split_point], result[None, split_point:])


def solution(mesh):
    placed = (
        P("dp", None, "mp"),
        P("dp", None, "mp"),
        P("dp"),
        P("dp", None, "mp"),
        P("dp", None, "mp"),
        P("dp"),
        P("mp", None),
        P(None, "mp"),
        P(),
        P("mp", "dp"),
        P("mp", "dp"),
    )

    def run(*arrays):
        body = small_group if fits(mesh, arrays[0], arrays[3], arrays[7]) else large_group
        return jax.shard_map(
            body,
            mesh=mesh,
            in_specs=placed,
            out_specs=(P("mp", "dp"), P("mp", "dp")),
            check_vma=False,
        )(*arrays)

    return run
```

```python
import functools
import math

import jax
import jax.numpy as jnp
from jax import lax
from jax.experimental import pallas as pl
from jax.experimental.pallas import tpu as pltpu
from jax.sharding import PartitionSpec as P

CLIP_COEF = 0.5
CLIP_RESIDUAL = 0.7
SIGMA_COEF = 1.0
SIGMA_RESIDUAL = 0.04
PRECISE = lax.Precision.HIGHEST
LANES = 128
GROUP = 4
VMEM = pl.BlockSpec(memory_space=pltpu.VMEM)
HBM = pl.BlockSpec(memory_space=pltpu.HBM)
SMEM = pl.BlockSpec(memory_space=pltpu.SMEM)
BOTH_LAST = (((1,), (1,)), ((), ()))
FIRST_LAST = (((1,), (0,)), ((), ()))
PARAMS = pltpu.CompilerParams(vmem_limit_bytes=40 * 1024 * 1024)


def dot(a, b, dims, precision=None):
    return lax.dot_general(a, b, dims, precision=precision, preferred_element_type=jnp.float32)


def iota(shape, axis):
    return lax.broadcasted_iota(jnp.int32, shape, axis)


def exact_parts(x):
    high = x.astype(jnp.bfloat16)
    rest = x - high.astype(jnp.float32)
    middle = rest.astype(jnp.bfloat16)
    return [high, middle, (rest - middle.astype(jnp.float32)).astype(jnp.bfloat16)]


def project_kernel(pub_in, pub_out, priv_in, priv_out, down_t, up, *rest):
    out, held, (down_held, up_held, sems) = rest[0], rest[1:5], rest[5:]
    rank = up.shape[0]
    tokens = pub_in.shape[1]
    copies = [
        pltpu.make_async_copy(down_t, down_held, sems.at[0]),
        pltpu.make_async_copy(up, up_held, sems.at[1]),
    ]
    pieces = []
    for inputs, cotangents, inputs_held, cotangents_held in (
        (pub_in, pub_out, held[0], held[1]),
        (priv_in, priv_out, held[2], held[3]),
    ):
        for e in range(inputs.shape[0]):
            pieces += [(down_held, inputs_held.at[e]), (up_held, cotangents_held.at[e])]
            for source, to in ((inputs, inputs_held), (cotangents, cotangents_held)):
                copies.append(
                    pltpu.make_async_copy(source.at[e], to.at[e], sems.at[len(copies)])
                )
    for copy in copies:
        copy.start()
    out[...] = jnp.zeros_like(out)
    for copy in copies[:2]:
        copy.wait()
    for i, (weights, piece) in enumerate(pieces):
        if i % GROUP == 0:
            for copy in copies[2 + i : 2 + i + GROUP]:
                copy.wait()
        slot, half = i // 2, i % 2
        out[half * rank : (half + 1) * rank, slot * LANES : slot * LANES + tokens] = dot(
            weights[...], piece[...], BOTH_LAST
        )


def gradient_kernel(dp, pub_len, priv_len, own, other, pub_in, pub_out, priv_in, priv_out, *rest):
    blocks, down_rows, up_rows = rest[:dp], rest[dp], rest[dp + 1]
    me = lax.axis_index("dp")
    rank = own.shape[0] // 2
    tokens, width = pub_in.shape[1:]
    lanes = width // dp
    per = rank // dp
    slot = 0
    for inputs, cotangents, lengths in (
        (pub_in, pub_out, pub_len),
        (priv_in, priv_out, priv_len),
    ):
        for e in range(inputs.shape[0]):
            at = slice(slot * LANES, slot * LANES + tokens)
            both = own[:, at] + other[:, at]
            live = iota(both.shape, 1) < lengths[e]
            both = jnp.where(live, both, 0.0).astype(jnp.bfloat16)
            down_whole = dot(both[rank:], inputs[e], FIRST_LAST)
            up_whole = dot(both[:rank], cotangents[e], FIRST_LAST)
            for c in range(dp):
                features = slice(c * lanes, (c + 1) * lanes)
                at = slice(c * rank, (c + 1) * rank)
                down_part = down_whole[:, features]
                up_part = up_whole[:, features]
                down_rows[at, :] = down_part.astype(jnp.bfloat16)
                for h in range(lanes // LANES):
                    up_rows[h, at, :] = up_part[:, h * LANES : (h + 1) * LANES]
            for k in range(dp):
                to = me ^ k
                rows = slice(slot * rank, (slot + 1) * rank)
                blocks[k][rows, :lanes] = down_rows[
                    pl.ds(pl.multiple_of(to * rank, rank), rank), :
                ]
                for h in range(lanes // LANES):
                    pieces = [
                        up_rows[h, pl.ds(to * per + r, dp, stride=rank), :] for r in range(per)
                    ]
                    start = lanes + h * LANES
                    blocks[k][rows, start : start + LANES] = jnp.concatenate(
                        pieces, axis=0
                    ).astype(jnp.bfloat16)
            slot += 1


def gram_kernel(order, n_pub, n_priv, *refs):
    dp = len(order)
    blocks, group, out = refs[:dp], refs[dp], refs[dp + 1]
    me = lax.axis_index("dp")
    rows = blocks[0].shape[0] // (n_pub + n_priv)
    pub_rows, priv_rows = n_pub * rows, n_priv * rows
    for k, block in zip(order, blocks):
        source = me ^ k
        group[pl.ds(pl.multiple_of(source * pub_rows, pub_rows), pub_rows), :] = block[:pub_rows]
        group[
            pl.ds(pl.multiple_of(dp * pub_rows + source * priv_rows, priv_rows), priv_rows), :
        ] = block[pub_rows:]
    publics, privates = dp * n_pub, dp * n_priv
    span = publics * rows
    lanes = group.shape[1]
    public = group[:span, :]
    same = iota((span, span), 0) % rows == iota((span, span), 1) % rows
    parts, squares = [], []
    for c in range(group.shape[0] // span):
        part = group[c * span : (c + 1) * span, :]
        products = jnp.where(same, dot(public, part, BOTH_LAST), 0.0)
        products = jnp.sum(products.reshape(publics, rows // 8, 8, span), axis=1)
        parts += exact_parts(products.reshape(publics * 8, span))
        if c > 0:
            wide = part.astype(jnp.float32)
            squares.append(jnp.sum((wide * wide).reshape(publics, rows, lanes), axis=1))
    pick = (iota((span, LANES), 0) // rows == iota((span, LANES), 1)).astype(jnp.bfloat16)
    sums = dot(jnp.concatenate(parts, axis=0), pick, FIRST_LAST).reshape(-1, 3, publics * 8, LANES)
    total = jnp.zeros((publics * 8, LANES), jnp.float32)
    for c in range(sums.shape[0]):
        total += pltpu.roll(sums[c, 0] + sums[c, 1] + sums[c, 2], c * publics, 1)
    total = jnp.sum(total.reshape(publics, 8, LANES), axis=1)
    half, each = LANES // 2, privates // 2
    squares = jnp.concatenate(squares, axis=0)
    used = publics + privates
    gap = jnp.zeros((used, lanes), jnp.float32)
    rest = jnp.zeros((half - used - each, lanes), jnp.float32)
    stacked = jnp.concatenate([gap, squares[:each], rest, gap, squares[each:], rest], axis=0)
    total_squares = dot(jnp.ones((8, lanes), jnp.float32), stacked, BOTH_LAST, PRECISE)
    short = publics // 2
    lane = iota((short, LANES), 1)
    packed = jnp.where(lane < half, total[:short], pltpu.roll(total[short:], half, 1))
    beside = jnp.logical_and(lane % half >= used, iota((short, LANES), 0) == 0)
    packed = jnp.where(beside, total_squares[:short], packed)
    for d in range(out.shape[0]):
        out[d] = packed


def update_kernel(gain, shares, group, noise, down_noise, up_noise, down, up):
    packed = shares[0]
    for d in range(1, shares.shape[0]):
        packed = packed + shares[d]
    publics = 2 * packed.shape[0]
    half = LANES // 2
    rows = 2 * up.shape[1] // group.shape[1]
    examples = group.shape[0] // rows
    each = (examples - publics) // 2
    total = jnp.concatenate([packed, pltpu.roll(packed, half, 1)], axis=0)
    row, lane = iota(total.shape, 0), iota(total.shape, 1)
    squares = jnp.where(
        lane[0:1] < publics + each,
        pltpu.roll(packed[0:1], LANES - (examples - publics), 1),
        pltpu.roll(packed[0:1], LANES - (half + each), 1),
    )
    gram_diagonal = jnp.sum(jnp.where(row == lane, total, 0.0), axis=1, keepdims=True)
    norm_scale = jnp.mean(jnp.sqrt(gram_diagonal), axis=0, keepdims=True)
    coefficient_limit = CLIP_COEF * norm_scale
    residual_limit = CLIP_RESIDUAL * norm_scale
    work = jnp.where(lane < half, total, jnp.where(lane == row + half, 1.0, 0.0))
    for j in range(0, publics, 2):
        first = jnp.broadcast_to(work[:, j : j + 1], work.shape)
        second = jnp.broadcast_to(work[:, j + 1 : j + 2], work.shape)
        inverse = lax.rsqrt(first[j : j + 1])
        pivot = work[j : j + 1] * inverse
        below = first[j + 1 : j + 2] * inverse
        next_inverse = lax.rsqrt(second[j + 1 : j + 2] - below * below)
        next_pivot = (work[j + 1 : j + 2] - below * pivot) * next_inverse
        first = first * inverse
        second = (second - first * below) * next_inverse
        work = jnp.where(
            row > j + 1,
            work - first * pivot - second * next_pivot,
            jnp.where(row == j, pivot, jnp.where(row == j + 1, next_pivot, work)),
        )
    private = jnp.logical_and(lane >= publics, lane < examples)
    coeffs = jnp.where(private, work, 0.0)
    coefficient_squares = jnp.sum(coeffs * coeffs, axis=0, keepdims=True)
    residual_squares = jnp.maximum(squares - coefficient_squares, 0.0)
    keep_coefficient = coefficient_limit / jnp.maximum(
        jnp.sqrt(coefficient_squares), coefficient_limit
    )
    keep_residual = residual_limit / jnp.maximum(jnp.sqrt(residual_squares), residual_limit)
    correction = jnp.sum(
        coeffs * (keep_coefficient - keep_residual), axis=1, keepdims=True
    )
    noise_column = jnp.zeros((publics, 1), jnp.float32)
    for j in range(publics):
        noise_column = jnp.where(iota((publics, 1), 0) == j, noise[j], noise_column)
    target = correction + SIGMA_COEF * coefficient_limit * noise_column
    inverse_factor = jnp.where(lane >= half, work, 0.0)
    anchor = pltpu.roll(jnp.sum(inverse_factor * target, axis=0, keepdims=True), half, 1)
    weights = jnp.where(lane[0:1] < publics, anchor, keep_residual)

    rank, lanes = rows, group.shape[1] // 2
    acc = jnp.zeros((rows, 2 * lanes), jnp.float32)
    for i in range(examples):
        acc = acc + weights[:, i : i + 1] * group[i * rows : (i + 1) * rows, :].astype(jnp.float32)
    scale = SIGMA_RESIDUAL * residual_limit
    per = LANES // rank
    flat = lanes * rank // LANES
    wide = jnp.concatenate([acc[:, :lanes]] * per, axis=0)
    wide = jnp.where(iota((LANES, lanes), 0) // rank == iota((LANES, lanes), 1) % per, wide, 0.0)
    pick = (iota((flat, lanes), 0) == iota((flat, lanes), 1) // per).astype(jnp.bfloat16)
    parts = dot(pick, jnp.concatenate(exact_parts(wide), axis=0), BOTH_LAST)
    turned = parts[:, :LANES] + parts[:, LANES : 2 * LANES] + parts[:, 2 * LANES :]
    for a in range(flat):
        at = slice(a * LANES, (a + 1) * LANES)
        down[0:1, at] = (turned[a : a + 1] + scale * down_noise[0:1, at]) * gain
    for a in range(rank):
        at = slice(a * lanes, (a + 1) * lanes)
        up[0:1, at] = (acc[a : a + 1, lanes:] + scale * up_noise[0:1, at]) * gain


def exchange(x, axis, step):
    return lax.ppermute(x, axis, [(s, s ^ step) for s in range(lax.axis_size(axis))])


def small_group(
    pub_in, pub_out, pub_len, priv_in, priv_out, priv_len, down, up, noise, down_noise, up_noise
):
    dp, mp = lax.axis_size("dp"), lax.axis_size("mp")
    n_pub, tokens, width = pub_in.shape
    n_priv = priv_in.shape[0]
    examples = n_pub + n_priv
    rank = up.shape[0]
    lanes = width // dp
    f32, bf16 = jnp.float32, jnp.bfloat16

    own, *held = pl.pallas_call(
        project_kernel,
        out_shape=[jax.ShapeDtypeStruct((2 * rank, examples * LANES), f32)]
        + [jax.ShapeDtypeStruct(x.shape, bf16) for x in (pub_in, pub_out, priv_in, priv_out)],
        in_specs=[HBM] * 6,
        out_specs=[VMEM] * 5,
        scratch_shapes=[
            pltpu.VMEM(up.shape, bf16),
            pltpu.VMEM(up.shape, bf16),
            pltpu.SemaphoreType.DMA((2 + 2 * examples,)),
        ],
        compiler_params=PARAMS,
        name="project",
    )(
        *(
            pltpu.with_memory_space_constraint(x, pltpu.HBM)
            for x in (pub_in, pub_out, priv_in, priv_out, down.T, up)
        )
    )
    step = 1
    while step < mp:
        other = exchange(own, "mp", step)
        step *= 2
        if step < mp:
            own = own + other

    block = jax.ShapeDtypeStruct((examples * rank, 2 * lanes), bf16)
    blocks = pl.pallas_call(
        functools.partial(gradient_kernel, dp),
        out_shape=[block] * dp,
        in_specs=[SMEM] * 2 + [VMEM] * 6,
        out_specs=[VMEM] * dp,
        scratch_shapes=[
            pltpu.VMEM((dp * rank, lanes), bf16),
            pltpu.VMEM((lanes // LANES, dp * rank, LANES), f32),
        ],
        compiler_params=PARAMS,
        name="gradients",
    )(pub_len, priv_len, own, other, *held)
    ranked = sorted(range(1, dp), key=lambda k: (k & 1, k if k & 1 else -k))
    far, near = [k for k in ranked if 2 * k >= dp], [k for k in ranked if 2 * k < dp]
    order = [k for pair in zip(far, near + [0]) for k in pair]
    blocks = [exchange(blocks[k], "dp", k) if k else blocks[k] for k in order]

    group, shares = pl.pallas_call(
        functools.partial(gram_kernel, order, n_pub, n_priv),
        out_shape=[
            jax.ShapeDtypeStruct((dp * examples * rank, 2 * lanes), bf16),
            jax.ShapeDtypeStruct((dp * mp, dp * n_pub // 2, LANES), f32),
        ],
        in_specs=[VMEM] * dp,
        out_specs=[VMEM] * 2,
        compiler_params=PARAMS,
        name="inner_products",
    )(*blocks)
    shares = lax.all_to_all(shares, ("dp", "mp"), 0, 0, tiled=True)

    gain = 1.0 / math.sqrt(n_priv * dp * tokens)
    return pl.pallas_call(
        functools.partial(update_kernel, gain),
        out_shape=[
            jax.ShapeDtypeStruct(down_noise.shape, f32),
            jax.ShapeDtypeStruct(up_noise.shape, f32),
        ],
        in_specs=[VMEM, VMEM, SMEM, VMEM, VMEM],
        out_specs=[VMEM] * 2,
        compiler_params=PARAMS,
        name="update",
    )(shares, group, noise, down_noise, up_noise)


def fits(mesh, pub_in, priv_in, up):
    dp = mesh.shape["dp"]
    width = pub_in.shape[2] // mesh.shape["mp"]
    publics = pub_in.shape[0]
    return (
        up.shape[0] == 16
        and dp in (2, 4, 8)
        and width % (dp * LANES) == 0
        and publics == 8
        and priv_in.shape[0] % 8 == 0
        and publics + priv_in.shape[0] + priv_in.shape[0] // 2 <= LANES // 2
        and pub_in.shape[1] <= LANES
    )


def partial_gram_terms(
    input_activations, output_cotangents, adapter_down_matrix, adapter_up_matrix
):
    projected_gradients = jnp.einsum(
        "umo,ov->umv", input_activations, adapter_down_matrix, preferred_element_type=jnp.float32
    )
    reconstructed_gradients = jnp.einsum(
        "fpb,ab->fpa", output_cotangents, adapter_up_matrix, preferred_element_type=jnp.float32
    )
    return (projected_gradients, reconstructed_gradients)


def shard_grads(
    input_activations,
    output_cotangents,
    token_lengths,
    projected_gradients,
    reconstructed_gradients,
):
    example_total_count = input_activations.shape[0]
    token_steps = input_activations.shape[1]
    positions = lax.broadcasted_iota(jnp.int32, (example_total_count, token_steps), 1)
    live_mask = (positions < token_lengths[:, None]).astype(jnp.float32)[:, :, None]
    projected_live = (projected_gradients * live_mask).astype(jnp.bfloat16)
    returned_live = (reconstructed_gradients * live_mask).astype(jnp.bfloat16)
    grad_down = jnp.einsum(
        "etd,etr->edr", input_activations, returned_live, preferred_element_type=jnp.float32
    ).astype(jnp.bfloat16)
    grad_up = jnp.einsum(
        "etr,eto->ero", projected_live, output_cotangents, preferred_element_type=jnp.float32
    ).astype(jnp.bfloat16)
    return (grad_down.reshape(example_total_count, -1), grad_up.reshape(example_total_count, -1))


def lower_solve(factor, right_side, backward):
    return lax.linalg.triangular_solve(
        factor, right_side, left_side=True, lower=True, transpose_a=backward
    )


def limits(gram_matrix):
    factor = jnp.linalg.cholesky(gram_matrix)
    norm_scale = jnp.mean(jnp.sqrt(jnp.diagonal(gram_matrix)))
    return (factor, CLIP_COEF * norm_scale, CLIP_RESIDUAL * norm_scale)


def keep_factors(coeffs, residual_squares, coefficient_limit, residual_limit):
    coefficient_norm = jnp.sqrt(jnp.sum(coeffs * coeffs, axis=0))
    keep_coefficient = coefficient_limit / jnp.maximum(coefficient_norm, coefficient_limit)
    keep_residual = residual_limit / jnp.maximum(jnp.sqrt(residual_squares), residual_limit)
    return (keep_coefficient, keep_residual)


def large_group(
    public_input_activations,
    public_output_cotangents,
    public_token_lengths,
    private_input_activations,
    private_output_cotangents,
    private_token_lengths,
    adapter_down_matrix,
    adapter_up_matrix,
    embedding_coefficient_noise,
    residual_down_noise,
    residual_up_noise,
):
    public_projected, public_returned = partial_gram_terms(
        public_input_activations, public_output_cotangents, adapter_down_matrix, adapter_up_matrix
    )
    private_projected, private_returned = partial_gram_terms(
        private_input_activations, private_output_cotangents, adapter_down_matrix, adapter_up_matrix
    )
    public_projected, public_returned, private_projected, private_returned = lax.psum(
        (public_projected, public_returned, private_projected, private_returned), "mp"
    )
    public_down, public_up = shard_grads(
        public_input_activations,
        public_output_cotangents,
        public_token_lengths,
        public_projected,
        public_returned,
    )
    private_down, private_up = shard_grads(
        private_input_activations,
        private_output_cotangents,
        private_token_lengths,
        private_projected,
        private_returned,
    )
    public_down, public_up, private_down, private_up = (
        lax.all_to_all(public_down, "dp", split_axis=1, concat_axis=0, tiled=True),
        lax.all_to_all(public_up, "dp", split_axis=1, concat_axis=0, tiled=True),
        lax.all_to_all(private_down, "dp", split_axis=1, concat_axis=0, tiled=True),
        lax.all_to_all(private_up, "dp", split_axis=1, concat_axis=0, tiled=True),
    )
    public_group = jnp.concatenate([public_down, public_up], axis=1)
    private_group = jnp.concatenate([private_down, private_up], axis=1)
    public_wide = public_group.astype(jnp.float32)
    private_wide = private_group.astype(jnp.float32)
    gram_partial = jnp.einsum(
        "pk,qk->pq", public_group, public_group, preferred_element_type=jnp.float32
    )
    cross_partial = jnp.einsum(
        "pk,qk->pq", public_group, private_group, preferred_element_type=jnp.float32
    )
    square_partial = jnp.sum(private_wide * private_wide, axis=1)
    gram_matrix, cross_terms, square_totals = lax.psum(
        (gram_partial, cross_partial, square_partial), ("dp", "mp")
    )
    factor, coefficient_limit, residual_limit = limits(gram_matrix)
    coeffs = lower_solve(factor, cross_terms, False)
    residual_squares = square_totals - jnp.sum(coeffs * coeffs, axis=0)
    keep_coefficient, keep_residual = keep_factors(
        coeffs, residual_squares, coefficient_limit, residual_limit
    )
    correction = jnp.dot(coeffs, keep_coefficient - keep_residual, precision=PRECISE)
    target = correction + SIGMA_COEF * coefficient_limit * embedding_coefficient_noise
    anchor = lower_solve(factor, target[:, None], True)[:, 0]
    update = jnp.dot(anchor, public_wide, precision=PRECISE) + jnp.dot(
        keep_residual, private_wide, precision=PRECISE
    )
    noise_shard = jnp.concatenate([residual_down_noise[0], residual_up_noise[0]], axis=0)
    private_total = private_input_activations.shape[0] * lax.axis_size("dp")
    update_gain = 1.0 / math.sqrt(private_total * private_input_activations.shape[1])
    result = (update + SIGMA_RESIDUAL * residual_limit * noise_shard) * update_gain
    split_point = public_down.shape[1]
    return (result[None, :split_point], result[None, split_point:])


def solution(mesh):
    placed = (
        P("dp", None, "mp"),
        P("dp", None, "mp"),
        P("dp"),
        P("dp", None, "mp"),
        P("dp", None, "mp"),
        P("dp"),
        P("mp", None),
        P(None, "mp"),
        P(),
        P("mp", "dp"),
        P("mp", "dp"),
    )

    def run(*arrays):
        body = small_group if fits(mesh, arrays[0], arrays[3], arrays[7]) else large_group
        return jax.shard_map(
            body,
            mesh=mesh,
            in_specs=placed,
            out_specs=(P("mp", "dp"), P("mp", "dp")),
            check_vma=False,
        )(*arrays)

    return run
```

```python
import functools
import math

import jax
import jax.numpy as jnp
from jax import lax
from jax.experimental import pallas as pl
from jax.experimental.pallas import tpu as pltpu
from jax.sharding import PartitionSpec as P

CLIP_COEF = 0.5
CLIP_RESIDUAL = 0.7
SIGMA_COEF = 1.0
SIGMA_RESIDUAL = 0.04
PRECISE = lax.Precision.HIGHEST
LANES = 128
GROUP = 4
VMEM = pl.BlockSpec(memory_space=pltpu.VMEM)
HBM = pl.BlockSpec(memory_space=pltpu.HBM)
SMEM = pl.BlockSpec(memory_space=pltpu.SMEM)
BOTH_LAST = (((1,), (1,)), ((), ()))
FIRST_LAST = (((1,), (0,)), ((), ()))
PARAMS = pltpu.CompilerParams(vmem_limit_bytes=40 * 1024 * 1024)


def dot(a, b, dims, precision=None):
    return lax.dot_general(a, b, dims, precision=precision, preferred_element_type=jnp.float32)


def iota(shape, axis):
    return lax.broadcasted_iota(jnp.int32, shape, axis)


def exact_parts(x):
    limit = float(jnp.finfo(jnp.bfloat16).max)
    high = jnp.clip(x, -limit, limit).astype(jnp.bfloat16)
    rest = x - high.astype(jnp.float32)
    middle = rest.astype(jnp.bfloat16)
    return [high, middle, (rest - middle.astype(jnp.float32)).astype(jnp.bfloat16)]


def project_kernel(pub_in, pub_out, priv_in, priv_out, down_t, up, *rest):
    out, held, (down_held, up_held, sems) = rest[0], rest[1:5], rest[5:]
    rank = up.shape[0]
    tokens = pub_in.shape[1]
    copies = [
        pltpu.make_async_copy(down_t, down_held, sems.at[0]),
        pltpu.make_async_copy(up, up_held, sems.at[1]),
    ]
    pieces = []
    for inputs, cotangents, inputs_held, cotangents_held in (
        (pub_in, pub_out, held[0], held[1]),
        (priv_in, priv_out, held[2], held[3]),
    ):
        for e in range(inputs.shape[0]):
            pieces += [(down_held, inputs_held.at[e]), (up_held, cotangents_held.at[e])]
            for source, to in ((inputs, inputs_held), (cotangents, cotangents_held)):
                copies.append(
                    pltpu.make_async_copy(source.at[e], to.at[e], sems.at[len(copies)])
                )
    for copy in copies:
        copy.start()
    out[...] = jnp.zeros_like(out)
    for copy in copies[:2]:
        copy.wait()
    for i, (weights, piece) in enumerate(pieces):
        if i % GROUP == 0:
            for copy in copies[2 + i : 2 + i + GROUP]:
                copy.wait()
        slot, half = i // 2, i % 2
        out[half * rank : (half + 1) * rank, slot * LANES : slot * LANES + tokens] = dot(
            weights[...], piece[...], BOTH_LAST
        )


def gradient_kernel(dp, pub_len, priv_len, own, other, pub_in, pub_out, priv_in, priv_out, *rest):
    blocks, down_rows, up_rows = rest[:dp], rest[dp], rest[dp + 1]
    me = lax.axis_index("dp")
    rank = own.shape[0] // 2
    tokens, width = pub_in.shape[1:]
    lanes = width // dp
    per = rank // dp
    slot = 0
    for inputs, cotangents, lengths in (
        (pub_in, pub_out, pub_len),
        (priv_in, priv_out, priv_len),
    ):
        for e in range(inputs.shape[0]):
            at = slice(slot * LANES, slot * LANES + tokens)
            both = own[:, at] + other[:, at].astype(jnp.float32)
            live = iota(both.shape, 1) < lengths[e]
            both = jnp.where(live, both, 0.0).astype(jnp.bfloat16)
            down_whole = dot(both[rank:], inputs[e], FIRST_LAST)
            up_whole = dot(both[:rank], cotangents[e], FIRST_LAST)
            for c in range(dp):
                features = slice(c * lanes, (c + 1) * lanes)
                at = slice(c * rank, (c + 1) * rank)
                down_part = down_whole[:, features]
                up_part = up_whole[:, features]
                down_rows[at, :] = down_part.astype(jnp.bfloat16)
                for h in range(lanes // LANES):
                    up_rows[h, at, :] = up_part[:, h * LANES : (h + 1) * LANES]
            for k in range(dp):
                to = me ^ k
                rows = slice(slot * rank, (slot + 1) * rank)
                blocks[k][rows, :lanes] = down_rows[
                    pl.ds(pl.multiple_of(to * rank, rank), rank), :
                ]
                for h in range(lanes // LANES):
                    pieces = [
                        up_rows[h, pl.ds(to * per + r, dp, stride=rank), :] for r in range(per)
                    ]
                    start = lanes + h * LANES
                    blocks[k][rows, start : start + LANES] = jnp.concatenate(
                        pieces, axis=0
                    ).astype(jnp.bfloat16)
            slot += 1


def gram_kernel(order, n_pub, n_priv, *refs):
    dp = len(order)
    blocks, group, out = refs[:dp], refs[dp], refs[dp + 1]
    me = lax.axis_index("dp")
    rows = blocks[0].shape[0] // (n_pub + n_priv)
    pub_rows, priv_rows = n_pub * rows, n_priv * rows
    for k, block in zip(order, blocks):
        source = me ^ k
        group[pl.ds(pl.multiple_of(source * pub_rows, pub_rows), pub_rows), :] = block[:pub_rows]
        group[
            pl.ds(pl.multiple_of(dp * pub_rows + source * priv_rows, priv_rows), priv_rows), :
        ] = block[pub_rows:]
    publics, privates = dp * n_pub, dp * n_priv
    span = publics * rows
    lanes = group.shape[1]
    public = group[:span, :]
    same = iota((span, span), 0) % rows == iota((span, span), 1) % rows
    parts, squares = [], []
    for c in range(group.shape[0] // span):
        part = group[c * span : (c + 1) * span, :]
        products = jnp.where(same, dot(public, part, BOTH_LAST), 0.0)
        products = jnp.sum(products.reshape(publics, rows // 8, 8, span), axis=1)
        parts += exact_parts(products.reshape(publics * 8, span))
        if c > 0:
            wide = part.astype(jnp.float32)
            squares.append(jnp.sum((wide * wide).reshape(publics, rows, lanes), axis=1))
    pick = (iota((span, LANES), 0) // rows == iota((span, LANES), 1)).astype(jnp.bfloat16)
    sums = dot(jnp.concatenate(parts, axis=0), pick, FIRST_LAST).reshape(-1, 3, publics * 8, LANES)
    total = jnp.zeros((publics * 8, LANES), jnp.float32)
    for c in range(sums.shape[0]):
        total += pltpu.roll(sums[c, 0] + sums[c, 1] + sums[c, 2], c * publics, 1)
    total = jnp.sum(total.reshape(publics, 8, LANES), axis=1)
    half, each = LANES // 2, privates // 2
    squares = jnp.concatenate(squares, axis=0)
    used = publics + privates
    gap = jnp.zeros((used, lanes), jnp.float32)
    rest = jnp.zeros((half - used - each, lanes), jnp.float32)
    stacked = jnp.concatenate([gap, squares[:each], rest, gap, squares[each:], rest], axis=0)
    total_squares = dot(jnp.ones((8, lanes), jnp.float32), stacked, BOTH_LAST, PRECISE)
    short = publics // 2
    lane = iota((short, LANES), 1)
    packed = jnp.where(lane < half, total[:short], pltpu.roll(total[short:], half, 1))
    beside = jnp.logical_and(lane % half >= used, iota((short, LANES), 0) == 0)
    packed = jnp.where(beside, total_squares[:short], packed)
    for d in range(out.shape[0]):
        out[d] = packed


def update_kernel(gain, shares, group, noise, down_noise, up_noise, down, up):
    packed = shares[0]
    for d in range(1, shares.shape[0]):
        packed = packed + shares[d]
    publics = 2 * packed.shape[0]
    half = LANES // 2
    rows = 2 * up.shape[1] // group.shape[1]
    examples = group.shape[0] // rows
    each = (examples - publics) // 2
    total = jnp.concatenate([packed, pltpu.roll(packed, half, 1)], axis=0)
    row, lane = iota(total.shape, 0), iota(total.shape, 1)
    squares = jnp.where(
        lane[0:1] < publics + each,
        pltpu.roll(packed[0:1], LANES - (examples - publics), 1),
        pltpu.roll(packed[0:1], LANES - (half + each), 1),
    )
    gram_diagonal = jnp.sum(jnp.where(row == lane, total, 0.0), axis=1, keepdims=True)
    norm_scale = jnp.mean(jnp.sqrt(gram_diagonal), axis=0, keepdims=True)
    coefficient_limit = CLIP_COEF * norm_scale
    residual_limit = CLIP_RESIDUAL * norm_scale
    work = jnp.where(lane < half, total, jnp.where(lane == row + half, 1.0, 0.0))
    for j in range(0, publics, 2):
        first = jnp.broadcast_to(work[:, j : j + 1], work.shape)
        second = jnp.broadcast_to(work[:, j + 1 : j + 2], work.shape)
        inverse = lax.rsqrt(first[j : j + 1])
        pivot = work[j : j + 1] * inverse
        below = first[j + 1 : j + 2] * inverse
        next_inverse = lax.rsqrt(second[j + 1 : j + 2] - below * below)
        next_pivot = (work[j + 1 : j + 2] - below * pivot) * next_inverse
        first = first * inverse
        second = (second - first * below) * next_inverse
        work = jnp.where(
            row > j + 1,
            work - first * pivot - second * next_pivot,
            jnp.where(row == j, pivot, jnp.where(row == j + 1, next_pivot, work)),
        )
    private = jnp.logical_and(lane >= publics, lane < examples)
    coeffs = jnp.where(private, work, 0.0)
    coefficient_squares = jnp.sum(coeffs * coeffs, axis=0, keepdims=True)
    residual_squares = jnp.maximum(squares - coefficient_squares, 0.0)
    keep_coefficient = coefficient_limit / jnp.maximum(
        jnp.sqrt(coefficient_squares), coefficient_limit
    )
    keep_residual = residual_limit / jnp.maximum(jnp.sqrt(residual_squares), residual_limit)
    correction = jnp.sum(
        coeffs * (keep_coefficient - keep_residual), axis=1, keepdims=True
    )
    noise_column = jnp.zeros((publics, 1), jnp.float32)
    for j in range(publics):
        noise_column = jnp.where(iota((publics, 1), 0) == j, noise[j], noise_column)
    target = correction + SIGMA_COEF * coefficient_limit * noise_column
    inverse_factor = jnp.where(lane >= half, work, 0.0)
    anchor = pltpu.roll(jnp.sum(inverse_factor * target, axis=0, keepdims=True), half, 1)
    weights = jnp.where(lane[0:1] < publics, anchor, keep_residual)

    rank, lanes = rows, group.shape[1] // 2
    acc = jnp.zeros((rows, 2 * lanes), jnp.float32)
    for i in range(examples):
        acc = acc + weights[:, i : i + 1] * group[i * rows : (i + 1) * rows, :].astype(jnp.float32)
    scale = SIGMA_RESIDUAL * residual_limit
    per = LANES // rank
    flat = lanes * rank // LANES
    wide = jnp.concatenate([acc[:, :lanes]] * per, axis=0)
    wide = jnp.where(iota((LANES, lanes), 0) // rank == iota((LANES, lanes), 1) % per, wide, 0.0)
    pick = (iota((flat, lanes), 0) == iota((flat, lanes), 1) // per).astype(jnp.bfloat16)
    parts = dot(pick, jnp.concatenate(exact_parts(wide), axis=0), BOTH_LAST)
    turned = parts[:, :LANES] + parts[:, LANES : 2 * LANES] + parts[:, 2 * LANES :]
    for a in range(flat):
        at = slice(a * LANES, (a + 1) * LANES)
        down[0:1, at] = (turned[a : a + 1] + scale * down_noise[0:1, at]) * gain
    for a in range(rank):
        at = slice(a * lanes, (a + 1) * lanes)
        up[0:1, at] = (acc[a : a + 1, lanes:] + scale * up_noise[0:1, at]) * gain


def exchange(x, axis, step):
    return lax.ppermute(x, axis, [(s, s ^ step) for s in range(lax.axis_size(axis))])


def small_group(
    pub_in, pub_out, pub_len, priv_in, priv_out, priv_len, down, up, noise, down_noise, up_noise
):
    dp, mp = lax.axis_size("dp"), lax.axis_size("mp")
    n_pub, tokens, width = pub_in.shape
    n_priv = priv_in.shape[0]
    examples = n_pub + n_priv
    rank = up.shape[0]
    lanes = width // dp
    f32, bf16 = jnp.float32, jnp.bfloat16

    own, *held = pl.pallas_call(
        project_kernel,
        out_shape=[jax.ShapeDtypeStruct((2 * rank, examples * LANES), f32)]
        + [jax.ShapeDtypeStruct(x.shape, bf16) for x in (pub_in, pub_out, priv_in, priv_out)],
        in_specs=[HBM] * 6,
        out_specs=[VMEM] * 5,
        scratch_shapes=[
            pltpu.VMEM(up.shape, bf16),
            pltpu.VMEM(up.shape, bf16),
            pltpu.SemaphoreType.DMA((2 + 2 * examples,)),
        ],
        compiler_params=PARAMS,
        name="project",
    )(
        *(
            pltpu.with_memory_space_constraint(x, pltpu.HBM)
            for x in (pub_in, pub_out, priv_in, priv_out, down.T, up)
        )
    )
    step = 1
    while step < mp:
        other = exchange(own if 2 * step < mp else own.astype(bf16), "mp", step)
        step *= 2
        if step < mp:
            own = own + other

    block = jax.ShapeDtypeStruct((examples * rank, 2 * lanes), bf16)
    blocks = pl.pallas_call(
        functools.partial(gradient_kernel, dp),
        out_shape=[block] * dp,
        in_specs=[SMEM] * 2 + [VMEM] * 6,
        out_specs=[VMEM] * dp,
        scratch_shapes=[
            pltpu.VMEM((dp * rank, lanes), bf16),
            pltpu.VMEM((lanes // LANES, dp * rank, LANES), f32),
        ],
        compiler_params=PARAMS,
        name="gradients",
    )(pub_len, priv_len, own, other, *held)
    far = sorted(range(dp // 2, dp), key=lambda k: (k & 1, k if k & 1 else -k))
    near = sorted(range(1, dp // 2), key=lambda k: (-k.bit_length(), k))
    order = [k for pair in zip(far, near + [0]) for k in pair]
    blocks = [exchange(blocks[k], "dp", k) if k else blocks[k] for k in order]

    group, shares = pl.pallas_call(
        functools.partial(gram_kernel, order, n_pub, n_priv),
        out_shape=[
            jax.ShapeDtypeStruct((dp * examples * rank, 2 * lanes), bf16),
            jax.ShapeDtypeStruct((dp * mp, dp * n_pub // 2, LANES), f32),
        ],
        in_specs=[VMEM] * dp,
        out_specs=[VMEM] * 2,
        compiler_params=PARAMS,
        name="inner_products",
    )(*blocks)
    shares = lax.all_to_all(shares, ("dp", "mp"), 0, 0, tiled=True)

    gain = 1.0 / math.sqrt(n_priv * dp * tokens)
    return pl.pallas_call(
        functools.partial(update_kernel, gain),
        out_shape=[
            jax.ShapeDtypeStruct(down_noise.shape, f32),
            jax.ShapeDtypeStruct(up_noise.shape, f32),
        ],
        in_specs=[VMEM, VMEM, SMEM, VMEM, VMEM],
        out_specs=[VMEM] * 2,
        compiler_params=PARAMS,
        name="update",
    )(shares, group, noise, down_noise, up_noise)


def fits(mesh, pub_in, priv_in, up):
    dp = mesh.shape["dp"]
    width = pub_in.shape[2] // mesh.shape["mp"]
    publics = pub_in.shape[0]
    return (
        up.shape[0] == 16
        and dp in (2, 4, 8)
        and width % (dp * LANES) == 0
        and publics == 8
        and priv_in.shape[0] % 8 == 0
        and publics + priv_in.shape[0] + priv_in.shape[0] // 2 <= LANES // 2
        and pub_in.shape[1] <= LANES
    )


def partial_gram_terms(
    input_activations, output_cotangents, adapter_down_matrix, adapter_up_matrix
):
    projected_gradients = jnp.einsum(
        "umo,ov->umv", input_activations, adapter_down_matrix, preferred_element_type=jnp.float32
    )
    reconstructed_gradients = jnp.einsum(
        "fpb,ab->fpa", output_cotangents, adapter_up_matrix, preferred_element_type=jnp.float32
    )
    return (projected_gradients, reconstructed_gradients)


def shard_grads(
    input_activations,
    output_cotangents,
    token_lengths,
    projected_gradients,
    reconstructed_gradients,
):
    example_total_count = input_activations.shape[0]
    token_steps = input_activations.shape[1]
    positions = lax.broadcasted_iota(jnp.int32, (example_total_count, token_steps), 1)
    live_mask = (positions < token_lengths[:, None]).astype(jnp.float32)[:, :, None]
    projected_live = (projected_gradients * live_mask).astype(jnp.bfloat16)
    returned_live = (reconstructed_gradients * live_mask).astype(jnp.bfloat16)
    grad_down = jnp.einsum(
        "etd,etr->edr", input_activations, returned_live, preferred_element_type=jnp.float32
    ).astype(jnp.bfloat16)
    grad_up = jnp.einsum(
        "etr,eto->ero", projected_live, output_cotangents, preferred_element_type=jnp.float32
    ).astype(jnp.bfloat16)
    return (grad_down.reshape(example_total_count, -1), grad_up.reshape(example_total_count, -1))


def lower_solve(factor, right_side, backward):
    return lax.linalg.triangular_solve(
        factor, right_side, left_side=True, lower=True, transpose_a=backward
    )


def limits(gram_matrix):
    factor = jnp.linalg.cholesky(gram_matrix)
    norm_scale = jnp.mean(jnp.sqrt(jnp.diagonal(gram_matrix)))
    return (factor, CLIP_COEF * norm_scale, CLIP_RESIDUAL * norm_scale)


def keep_factors(coeffs, residual_squares, coefficient_limit, residual_limit):
    coefficient_norm = jnp.sqrt(jnp.sum(coeffs * coeffs, axis=0))
    keep_coefficient = coefficient_limit / jnp.maximum(coefficient_norm, coefficient_limit)
    keep_residual = residual_limit / jnp.maximum(jnp.sqrt(residual_squares), residual_limit)
    return (keep_coefficient, keep_residual)


def large_group(
    public_input_activations,
    public_output_cotangents,
    public_token_lengths,
    private_input_activations,
    private_output_cotangents,
    private_token_lengths,
    adapter_down_matrix,
    adapter_up_matrix,
    embedding_coefficient_noise,
    residual_down_noise,
    residual_up_noise,
):
    public_projected, public_returned = partial_gram_terms(
        public_input_activations, public_output_cotangents, adapter_down_matrix, adapter_up_matrix
    )
    private_projected, private_returned = partial_gram_terms(
        private_input_activations, private_output_cotangents, adapter_down_matrix, adapter_up_matrix
    )
    public_projected, public_returned, private_projected, private_returned = lax.psum(
        (public_projected, public_returned, private_projected, private_returned), "mp"
    )
    public_down, public_up = shard_grads(
        public_input_activations,
        public_output_cotangents,
        public_token_lengths,
        public_projected,
        public_returned,
    )
    private_down, private_up = shard_grads(
        private_input_activations,
        private_output_cotangents,
        private_token_lengths,
        private_projected,
        private_returned,
    )
    public_down, public_up, private_down, private_up = (
        lax.all_to_all(public_down, "dp", split_axis=1, concat_axis=0, tiled=True),
        lax.all_to_all(public_up, "dp", split_axis=1, concat_axis=0, tiled=True),
        lax.all_to_all(private_down, "dp", split_axis=1, concat_axis=0, tiled=True),
        lax.all_to_all(private_up, "dp", split_axis=1, concat_axis=0, tiled=True),
    )
    public_group = jnp.concatenate([public_down, public_up], axis=1)
    private_group = jnp.concatenate([private_down, private_up], axis=1)
    public_wide = public_group.astype(jnp.float32)
    private_wide = private_group.astype(jnp.float32)
    gram_partial = jnp.einsum(
        "pk,qk->pq", public_group, public_group, preferred_element_type=jnp.float32
    )
    cross_partial = jnp.einsum(
        "pk,qk->pq", public_group, private_group, preferred_element_type=jnp.float32
    )
    square_partial = jnp.sum(private_wide * private_wide, axis=1)
    gram_matrix, cross_terms, square_totals = lax.psum(
        (gram_partial, cross_partial, square_partial), ("dp", "mp")
    )
    factor, coefficient_limit, residual_limit = limits(gram_matrix)
    coeffs = lower_solve(factor, cross_terms, False)
    residual_squares = square_totals - jnp.sum(coeffs * coeffs, axis=0)
    keep_coefficient, keep_residual = keep_factors(
        coeffs, residual_squares, coefficient_limit, residual_limit
    )
    correction = jnp.dot(coeffs, keep_coefficient - keep_residual, precision=PRECISE)
    target = correction + SIGMA_COEF * coefficient_limit * embedding_coefficient_noise
    anchor = lower_solve(factor, target[:, None], True)[:, 0]
    update = jnp.dot(anchor, public_wide, precision=PRECISE) + jnp.dot(
        keep_residual, private_wide, precision=PRECISE
    )
    noise_shard = jnp.concatenate([residual_down_noise[0], residual_up_noise[0]], axis=0)
    private_total = private_input_activations.shape[0] * lax.axis_size("dp")
    update_gain = 1.0 / math.sqrt(private_total * private_input_activations.shape[1])
    result = (update + SIGMA_RESIDUAL * residual_limit * noise_shard) * update_gain
    split_point = public_down.shape[1]
    return (result[None, :split_point], result[None, split_point:])


def solution(mesh):
    placed = (
        P("dp", None, "mp"),
        P("dp", None, "mp"),
        P("dp"),
        P("dp", None, "mp"),
        P("dp", None, "mp"),
        P("dp"),
        P("mp", None),
        P(None, "mp"),
        P(),
        P("mp", "dp"),
        P("mp", "dp"),
    )

    def run(*arrays):
        body = small_group if fits(mesh, arrays[0], arrays[3], arrays[7]) else large_group
        return jax.shard_map(
            body,
            mesh=mesh,
            in_specs=placed,
            out_specs=(P("mp", "dp"), P("mp", "dp")),
            check_vma=False,
        )(*arrays)

    return run
```

```python
import functools
import math

import jax
import jax.numpy as jnp
from jax import lax
from jax.experimental import pallas as pl
from jax.experimental.pallas import tpu as pltpu
from jax.sharding import PartitionSpec as P

CLIP_COEF = 0.5
CLIP_RESIDUAL = 0.7
SIGMA_COEF = 1.0
SIGMA_RESIDUAL = 0.04
PRECISE = lax.Precision.HIGHEST
LANES = 128
GROUP = 4
VMEM = pl.BlockSpec(memory_space=pltpu.VMEM)
HBM = pl.BlockSpec(memory_space=pltpu.HBM)
SMEM = pl.BlockSpec(memory_space=pltpu.SMEM)
BOTH_LAST = (((1,), (1,)), ((), ()))
FIRST_LAST = (((1,), (0,)), ((), ()))
PARAMS = pltpu.CompilerParams(vmem_limit_bytes=40 * 1024 * 1024)


def dot(a, b, dims, precision=None):
    return lax.dot_general(a, b, dims, precision=precision, preferred_element_type=jnp.float32)


def iota(shape, axis):
    return lax.broadcasted_iota(jnp.int32, shape, axis)


def exact_parts(x):
    limit = float(jnp.finfo(jnp.bfloat16).max)
    high = jnp.clip(x, -limit, limit).astype(jnp.bfloat16)
    rest = x - high.astype(jnp.float32)
    middle = rest.astype(jnp.bfloat16)
    return [high, middle, (rest - middle.astype(jnp.float32)).astype(jnp.bfloat16)]


def project_kernel(pub_in, pub_out, priv_in, priv_out, down_t, up, *rest):
    outs, held, (down_held, up_held, sems) = rest[:2], rest[2:6], rest[6:]
    tokens = pub_in.shape[1]
    copies = [
        pltpu.make_async_copy(down_t, down_held, sems.at[0]),
        pltpu.make_async_copy(up, up_held, sems.at[1]),
    ]
    pieces = []
    for inputs, cotangents, inputs_held, cotangents_held in (
        (pub_in, pub_out, held[0], held[1]),
        (priv_in, priv_out, held[2], held[3]),
    ):
        for e in range(inputs.shape[0]):
            pieces += [(down_held, inputs_held.at[e]), (up_held, cotangents_held.at[e])]
            for source, to in ((inputs, inputs_held), (cotangents, cotangents_held)):
                copies.append(
                    pltpu.make_async_copy(source.at[e], to.at[e], sems.at[len(copies)])
                )
    for copy in copies:
        copy.start()
    for out in outs:
        out[...] = jnp.zeros_like(out)
    for copy in copies[:2]:
        copy.wait()
    for i, (weights, piece) in enumerate(pieces):
        if i % GROUP == 0:
            for copy in copies[2 + i : 2 + i + GROUP]:
                copy.wait()
        slot, half = i // 2, i % 2
        outs[half][:, slot * LANES : slot * LANES + tokens] = dot(
            weights[...], piece[...], BOTH_LAST
        )


def gradient_kernel(dp, pub_len, priv_len, *rest):
    projected, returned, (pub_in, pub_out, priv_in, priv_out) = rest[:2], rest[2:4], rest[4:8]
    blocks, (down_rows, up_rows) = rest[8 : 8 + dp], rest[8 + dp :]
    me = lax.axis_index("dp")
    rank = projected[0].shape[0]
    tokens, width = pub_in.shape[1:]
    lanes = width // dp
    per = rank // dp
    slot = 0
    for inputs, cotangents, lengths in (
        (pub_in, pub_out, pub_len),
        (priv_in, priv_out, priv_len),
    ):
        for e in range(inputs.shape[0]):
            at = slice(slot * LANES, slot * LANES + tokens)
            live = iota((rank, tokens), 1) < lengths[e]
            down_live, up_live = (
                jnp.where(live, own[:, at] + other[:, at], 0.0).astype(jnp.bfloat16)
                for own, other in (returned, projected)
            )
            down_whole = dot(down_live, inputs[e], FIRST_LAST)
            up_whole = dot(up_live, cotangents[e], FIRST_LAST)
            for c in range(dp):
                features = slice(c * lanes, (c + 1) * lanes)
                at = slice(c * rank, (c + 1) * rank)
                down_part = down_whole[:, features]
                up_part = up_whole[:, features]
                down_rows[at, :] = down_part.astype(jnp.bfloat16)
                for h in range(lanes // LANES):
                    up_rows[h, at, :] = up_part[:, h * LANES : (h + 1) * LANES]
            for k in range(dp):
                to = me ^ k
                rows = slice(slot * rank, (slot + 1) * rank)
                blocks[k][rows, :lanes] = down_rows[
                    pl.ds(pl.multiple_of(to * rank, rank), rank), :
                ]
                for h in range(lanes // LANES):
                    pieces = [
                        up_rows[h, pl.ds(to * per + r, dp, stride=rank), :] for r in range(per)
                    ]
                    start = lanes + h * LANES
                    blocks[k][rows, start : start + LANES] = jnp.concatenate(
                        pieces, axis=0
                    ).astype(jnp.bfloat16)
            slot += 1


def gram_kernel(order, n_pub, n_priv, *refs):
    dp = len(order)
    blocks, group, out = refs[:dp], refs[dp], refs[dp + 1]
    me = lax.axis_index("dp")
    rows = blocks[0].shape[0] // (n_pub + n_priv)
    pub_rows, priv_rows = n_pub * rows, n_priv * rows
    for k, block in zip(order, blocks):
        source = me ^ k
        group[pl.ds(pl.multiple_of(source * pub_rows, pub_rows), pub_rows), :] = block[:pub_rows]
        group[
            pl.ds(pl.multiple_of(dp * pub_rows + source * priv_rows, priv_rows), priv_rows), :
        ] = block[pub_rows:]
    publics, privates = dp * n_pub, dp * n_priv
    span = publics * rows
    lanes = group.shape[1]
    public = group[:span, :]
    same = iota((span, span), 0) % rows == iota((span, span), 1) % rows
    parts, squares = [], []
    for c in range(group.shape[0] // span):
        part = group[c * span : (c + 1) * span, :]
        products = jnp.where(same, dot(public, part, BOTH_LAST), 0.0)
        products = jnp.sum(products.reshape(publics, rows // 8, 8, span), axis=1)
        parts += exact_parts(products.reshape(publics * 8, span))
        if c > 0:
            wide = part.astype(jnp.float32)
            squares.append(jnp.sum((wide * wide).reshape(publics, rows, lanes), axis=1))
    pick = (iota((span, LANES), 0) // rows == iota((span, LANES), 1)).astype(jnp.bfloat16)
    sums = dot(jnp.concatenate(parts, axis=0), pick, FIRST_LAST).reshape(-1, 3, publics * 8, LANES)
    total = jnp.zeros((publics * 8, LANES), jnp.float32)
    for c in range(sums.shape[0]):
        total += pltpu.roll(sums[c, 0] + sums[c, 1] + sums[c, 2], c * publics, 1)
    total = jnp.sum(total.reshape(publics, 8, LANES), axis=1)
    half, each = LANES // 2, privates // 2
    squares = jnp.concatenate(squares, axis=0)
    used = publics + privates
    gap = jnp.zeros((used, lanes), jnp.float32)
    rest = jnp.zeros((half - used - each, lanes), jnp.float32)
    stacked = jnp.concatenate([gap, squares[:each], rest, gap, squares[each:], rest], axis=0)
    total_squares = dot(jnp.ones((8, lanes), jnp.float32), stacked, BOTH_LAST, PRECISE)
    short = publics // 2
    lane = iota((short, LANES), 1)
    packed = jnp.where(lane < half, total[:short], pltpu.roll(total[short:], half, 1))
    beside = jnp.logical_and(lane % half >= used, iota((short, LANES), 0) == 0)
    packed = jnp.where(beside, total_squares[:short], packed)
    for d in range(out.shape[0]):
        out[d] = packed


def update_kernel(gain, shares, group, noise, down_noise, up_noise, down, up):
    packed = shares[0]
    for d in range(1, shares.shape[0]):
        packed = packed + shares[d]
    publics = 2 * packed.shape[0]
    half = LANES // 2
    rows = 2 * up.shape[1] // group.shape[1]
    examples = group.shape[0] // rows
    each = (examples - publics) // 2
    total = jnp.concatenate([packed, pltpu.roll(packed, half, 1)], axis=0)
    row, lane = iota(total.shape, 0), iota(total.shape, 1)
    squares = jnp.where(
        lane[0:1] < publics + each,
        pltpu.roll(packed[0:1], LANES - (examples - publics), 1),
        pltpu.roll(packed[0:1], LANES - (half + each), 1),
    )
    gram_diagonal = jnp.sum(jnp.where(row == lane, total, 0.0), axis=1, keepdims=True)
    norm_scale = jnp.mean(jnp.sqrt(gram_diagonal), axis=0, keepdims=True)
    coefficient_limit = CLIP_COEF * norm_scale
    residual_limit = CLIP_RESIDUAL * norm_scale
    work = jnp.where(lane < half, total, jnp.where(lane == row + half, 1.0, 0.0))
    for j in range(0, publics, 2):
        first = jnp.broadcast_to(work[:, j : j + 1], work.shape)
        second = jnp.broadcast_to(work[:, j + 1 : j + 2], work.shape)
        inverse = lax.rsqrt(first[j : j + 1])
        pivot = work[j : j + 1] * inverse
        below = first[j + 1 : j + 2] * inverse
        next_inverse = lax.rsqrt(second[j + 1 : j + 2] - below * below)
        next_pivot = (work[j + 1 : j + 2] - below * pivot) * next_inverse
        first = first * inverse
        second = (second - first * below) * next_inverse
        work = jnp.where(
            row > j + 1,
            work - first * pivot - second * next_pivot,
            jnp.where(row == j, pivot, jnp.where(row == j + 1, next_pivot, work)),
        )
    private = jnp.logical_and(lane >= publics, lane < examples)
    coeffs = jnp.where(private, work, 0.0)
    coefficient_squares = jnp.sum(coeffs * coeffs, axis=0, keepdims=True)
    residual_squares = jnp.maximum(squares - coefficient_squares, 0.0)
    keep_coefficient = coefficient_limit / jnp.maximum(
        jnp.sqrt(coefficient_squares), coefficient_limit
    )
    keep_residual = residual_limit / jnp.maximum(jnp.sqrt(residual_squares), residual_limit)
    correction = jnp.sum(
        coeffs * (keep_coefficient - keep_residual), axis=1, keepdims=True
    )
    noise_column = jnp.zeros((publics, 1), jnp.float32)
    for j in range(publics):
        noise_column = jnp.where(iota((publics, 1), 0) == j, noise[j], noise_column)
    target = correction + SIGMA_COEF * coefficient_limit * noise_column
    inverse_factor = jnp.where(lane >= half, work, 0.0)
    anchor = pltpu.roll(jnp.sum(inverse_factor * target, axis=0, keepdims=True), half, 1)
    weights = jnp.where(lane[0:1] < publics, anchor, keep_residual)

    rank, lanes = rows, group.shape[1] // 2
    acc = jnp.zeros((rows, 2 * lanes), jnp.float32)
    for i in range(examples):
        acc = acc + weights[:, i : i + 1] * group[i * rows : (i + 1) * rows, :].astype(jnp.float32)
    scale = SIGMA_RESIDUAL * residual_limit
    per = LANES // rank
    flat = lanes * rank // LANES
    wide = jnp.concatenate([acc[:, :lanes]] * per, axis=0)
    wide = jnp.where(iota((LANES, lanes), 0) // rank == iota((LANES, lanes), 1) % per, wide, 0.0)
    pick = (iota((flat, lanes), 0) == iota((flat, lanes), 1) // per).astype(jnp.bfloat16)
    parts = dot(pick, jnp.concatenate(exact_parts(wide), axis=0), BOTH_LAST)
    turned = parts[:, :LANES] + parts[:, LANES : 2 * LANES] + parts[:, 2 * LANES :]
    for a in range(flat):
        at = slice(a * LANES, (a + 1) * LANES)
        down[0:1, at] = (turned[a : a + 1] + scale * down_noise[0:1, at]) * gain
    for a in range(rank):
        at = slice(a * lanes, (a + 1) * lanes)
        up[0:1, at] = (acc[a : a + 1, lanes:] + scale * up_noise[0:1, at]) * gain


def exchange(x, axis, step):
    return lax.ppermute(x, axis, [(s, s ^ step) for s in range(lax.axis_size(axis))])


def sum_over(axis, own, steps):
    for step in steps[:-1]:
        own = own + exchange(own, axis, step)
    return own, exchange(own, axis, steps[-1])


def small_group(
    pub_in, pub_out, pub_len, priv_in, priv_out, priv_len, down, up, noise, down_noise, up_noise
):
    dp, mp = lax.axis_size("dp"), lax.axis_size("mp")
    n_pub, tokens, width = pub_in.shape
    n_priv = priv_in.shape[0]
    examples = n_pub + n_priv
    rank = up.shape[0]
    lanes = width // dp
    f32, bf16 = jnp.float32, jnp.bfloat16

    projected, returned, *held = pl.pallas_call(
        project_kernel,
        out_shape=[jax.ShapeDtypeStruct((rank, examples * LANES), f32)] * 2
        + [jax.ShapeDtypeStruct(x.shape, bf16) for x in (pub_in, pub_out, priv_in, priv_out)],
        in_specs=[HBM] * 6,
        out_specs=[VMEM] * 6,
        scratch_shapes=[
            pltpu.VMEM(up.shape, bf16),
            pltpu.VMEM(up.shape, bf16),
            pltpu.SemaphoreType.DMA((2 + 2 * examples,)),
        ],
        compiler_params=PARAMS,
        name="project",
    )(
        *(
            pltpu.with_memory_space_constraint(x, pltpu.HBM)
            for x in (pub_in, pub_out, priv_in, priv_out, down.T, up)
        )
    )
    steps = [1 << i for i in range(mp.bit_length() - 1)]
    projected = sum_over("mp", projected, steps)
    returned = sum_over("mp", returned, steps[::-1])

    block = jax.ShapeDtypeStruct((examples * rank, 2 * lanes), bf16)
    blocks = pl.pallas_call(
        functools.partial(gradient_kernel, dp),
        out_shape=[block] * dp,
        in_specs=[SMEM] * 2 + [VMEM] * 8,
        out_specs=[VMEM] * dp,
        scratch_shapes=[
            pltpu.VMEM((dp * rank, lanes), bf16),
            pltpu.VMEM((lanes // LANES, dp * rank, LANES), f32),
        ],
        compiler_params=PARAMS,
        name="gradients",
    )(pub_len, priv_len, *projected, *returned, *held)
    far = sorted(range(dp // 2, dp), key=lambda k: (k & 1, k if k & 1 else -k))
    near = sorted(range(1, dp // 2), key=lambda k: (-k.bit_length(), k))
    order = [k for pair in zip(far, near + [0]) for k in pair]
    blocks = [exchange(blocks[k], "dp", k) if k else blocks[k] for k in order]

    group, shares = pl.pallas_call(
        functools.partial(gram_kernel, order, n_pub, n_priv),
        out_shape=[
            jax.ShapeDtypeStruct((dp * examples * rank, 2 * lanes), bf16),
            jax.ShapeDtypeStruct((dp * mp, dp * n_pub // 2, LANES), f32),
        ],
        in_specs=[VMEM] * dp,
        out_specs=[VMEM] * 2,
        compiler_params=PARAMS,
        name="inner_products",
    )(*blocks)
    shares = lax.all_to_all(shares, ("dp", "mp"), 0, 0, tiled=True)

    gain = 1.0 / math.sqrt(n_priv * dp * tokens)
    return pl.pallas_call(
        functools.partial(update_kernel, gain),
        out_shape=[
            jax.ShapeDtypeStruct(down_noise.shape, f32),
            jax.ShapeDtypeStruct(up_noise.shape, f32),
        ],
        in_specs=[VMEM, VMEM, SMEM, VMEM, VMEM],
        out_specs=[VMEM] * 2,
        compiler_params=PARAMS,
        name="update",
    )(shares, group, noise, down_noise, up_noise)


def fits(mesh, pub_in, priv_in, up):
    dp = mesh.shape["dp"]
    width = pub_in.shape[2] // mesh.shape["mp"]
    publics = pub_in.shape[0]
    return (
        up.shape[0] == 16
        and dp in (2, 4, 8)
        and width % (dp * LANES) == 0
        and publics == 8
        and priv_in.shape[0] % 8 == 0
        and publics + priv_in.shape[0] + priv_in.shape[0] // 2 <= LANES // 2
        and pub_in.shape[1] <= LANES
    )


def partial_gram_terms(
    input_activations, output_cotangents, adapter_down_matrix, adapter_up_matrix
):
    projected_gradients = jnp.einsum(
        "umo,ov->umv", input_activations, adapter_down_matrix, preferred_element_type=jnp.float32
    )
    reconstructed_gradients = jnp.einsum(
        "fpb,ab->fpa", output_cotangents, adapter_up_matrix, preferred_element_type=jnp.float32
    )
    return (projected_gradients, reconstructed_gradients)


def shard_grads(
    input_activations,
    output_cotangents,
    token_lengths,
    projected_gradients,
    reconstructed_gradients,
):
    example_total_count = input_activations.shape[0]
    token_steps = input_activations.shape[1]
    positions = lax.broadcasted_iota(jnp.int32, (example_total_count, token_steps), 1)
    live_mask = (positions < token_lengths[:, None]).astype(jnp.float32)[:, :, None]
    projected_live = (projected_gradients * live_mask).astype(jnp.bfloat16)
    returned_live = (reconstructed_gradients * live_mask).astype(jnp.bfloat16)
    grad_down = jnp.einsum(
        "etd,etr->edr", input_activations, returned_live, preferred_element_type=jnp.float32
    ).astype(jnp.bfloat16)
    grad_up = jnp.einsum(
        "etr,eto->ero", projected_live, output_cotangents, preferred_element_type=jnp.float32
    ).astype(jnp.bfloat16)
    return (grad_down.reshape(example_total_count, -1), grad_up.reshape(example_total_count, -1))


def lower_solve(factor, right_side, backward):
    return lax.linalg.triangular_solve(
        factor, right_side, left_side=True, lower=True, transpose_a=backward
    )


def limits(gram_matrix):
    factor = jnp.linalg.cholesky(gram_matrix)
    norm_scale = jnp.mean(jnp.sqrt(jnp.diagonal(gram_matrix)))
    return (factor, CLIP_COEF * norm_scale, CLIP_RESIDUAL * norm_scale)


def keep_factors(coeffs, residual_squares, coefficient_limit, residual_limit):
    coefficient_norm = jnp.sqrt(jnp.sum(coeffs * coeffs, axis=0))
    keep_coefficient = coefficient_limit / jnp.maximum(coefficient_norm, coefficient_limit)
    keep_residual = residual_limit / jnp.maximum(jnp.sqrt(residual_squares), residual_limit)
    return (keep_coefficient, keep_residual)


def large_group(
    public_input_activations,
    public_output_cotangents,
    public_token_lengths,
    private_input_activations,
    private_output_cotangents,
    private_token_lengths,
    adapter_down_matrix,
    adapter_up_matrix,
    embedding_coefficient_noise,
    residual_down_noise,
    residual_up_noise,
):
    public_projected, public_returned = partial_gram_terms(
        public_input_activations, public_output_cotangents, adapter_down_matrix, adapter_up_matrix
    )
    private_projected, private_returned = partial_gram_terms(
        private_input_activations, private_output_cotangents, adapter_down_matrix, adapter_up_matrix
    )
    public_projected, public_returned, private_projected, private_returned = lax.psum(
        (public_projected, public_returned, private_projected, private_returned), "mp"
    )
    public_down, public_up = shard_grads(
        public_input_activations,
        public_output_cotangents,
        public_token_lengths,
        public_projected,
        public_returned,
    )
    private_down, private_up = shard_grads(
        private_input_activations,
        private_output_cotangents,
        private_token_lengths,
        private_projected,
        private_returned,
    )
    public_down, public_up, private_down, private_up = (
        lax.all_to_all(public_down, "dp", split_axis=1, concat_axis=0, tiled=True),
        lax.all_to_all(public_up, "dp", split_axis=1, concat_axis=0, tiled=True),
        lax.all_to_all(private_down, "dp", split_axis=1, concat_axis=0, tiled=True),
        lax.all_to_all(private_up, "dp", split_axis=1, concat_axis=0, tiled=True),
    )
    public_group = jnp.concatenate([public_down, public_up], axis=1)
    private_group = jnp.concatenate([private_down, private_up], axis=1)
    public_wide = public_group.astype(jnp.float32)
    private_wide = private_group.astype(jnp.float32)
    gram_partial = jnp.einsum(
        "pk,qk->pq", public_group, public_group, preferred_element_type=jnp.float32
    )
    cross_partial = jnp.einsum(
        "pk,qk->pq", public_group, private_group, preferred_element_type=jnp.float32
    )
    square_partial = jnp.sum(private_wide * private_wide, axis=1)
    gram_matrix, cross_terms, square_totals = lax.psum(
        (gram_partial, cross_partial, square_partial), ("dp", "mp")
    )
    factor, coefficient_limit, residual_limit = limits(gram_matrix)
    coeffs = lower_solve(factor, cross_terms, False)
    residual_squares = square_totals - jnp.sum(coeffs * coeffs, axis=0)
    keep_coefficient, keep_residual = keep_factors(
        coeffs, residual_squares, coefficient_limit, residual_limit
    )
    correction = jnp.dot(coeffs, keep_coefficient - keep_residual, precision=PRECISE)
    target = correction + SIGMA_COEF * coefficient_limit * embedding_coefficient_noise
    anchor = lower_solve(factor, target[:, None], True)[:, 0]
    update = jnp.dot(anchor, public_wide, precision=PRECISE) + jnp.dot(
        keep_residual, private_wide, precision=PRECISE
    )
    noise_shard = jnp.concatenate([residual_down_noise[0], residual_up_noise[0]], axis=0)
    private_total = private_input_activations.shape[0] * lax.axis_size("dp")
    update_gain = 1.0 / math.sqrt(private_total * private_input_activations.shape[1])
    result = (update + SIGMA_RESIDUAL * residual_limit * noise_shard) * update_gain
    split_point = public_down.shape[1]
    return (result[None, :split_point], result[None, split_point:])


def solution(mesh):
    placed = (
        P("dp", None, "mp"),
        P("dp", None, "mp"),
        P("dp"),
        P("dp", None, "mp"),
        P("dp", None, "mp"),
        P("dp"),
        P("mp", None),
        P(None, "mp"),
        P(),
        P("mp", "dp"),
        P("mp", "dp"),
    )

    def run(*arrays):
        body = small_group if fits(mesh, arrays[0], arrays[3], arrays[7]) else large_group
        return jax.shard_map(
            body,
            mesh=mesh,
            in_specs=placed,
            out_specs=(P("mp", "dp"), P("mp", "dp")),
            check_vma=False,
        )(*arrays)

    return run
```

```python
import functools
import math

import jax
import jax.numpy as jnp
from jax import lax
from jax.experimental import pallas as pl
from jax.experimental.pallas import tpu as pltpu
from jax.sharding import PartitionSpec as P

CLIP_COEF = 0.5
CLIP_RESIDUAL = 0.7
SIGMA_COEF = 1.0
SIGMA_RESIDUAL = 0.04
PRECISE = lax.Precision.HIGHEST
LANES = 128
GROUP = 4
VMEM = pl.BlockSpec(memory_space=pltpu.VMEM)
HBM = pl.BlockSpec(memory_space=pltpu.HBM)
SMEM = pl.BlockSpec(memory_space=pltpu.SMEM)
BOTH_LAST = (((1,), (1,)), ((), ()))
FIRST_LAST = (((1,), (0,)), ((), ()))
PARAMS = pltpu.CompilerParams(vmem_limit_bytes=40 * 1024 * 1024)


def dot(a, b, dims, precision=None):
    return lax.dot_general(a, b, dims, precision=precision, preferred_element_type=jnp.float32)


def iota(shape, axis):
    return lax.broadcasted_iota(jnp.int32, shape, axis)


def exact_parts(x):
    limit = float(jnp.finfo(jnp.bfloat16).max)
    high = jnp.clip(x, -limit, limit).astype(jnp.bfloat16)
    rest = x - high.astype(jnp.float32)
    middle = rest.astype(jnp.bfloat16)
    return [high, middle, (rest - middle.astype(jnp.float32)).astype(jnp.bfloat16)]


def project_kernel(pub_in, pub_out, priv_in, priv_out, down_t, up, *rest):
    outs, held, (down_held, up_held, sems) = rest[:2], rest[2:6], rest[6:]
    tokens = pub_in.shape[1]
    copies = [
        pltpu.make_async_copy(down_t, down_held, sems.at[0]),
        pltpu.make_async_copy(up, up_held, sems.at[1]),
    ]
    pieces = []
    for inputs, cotangents, inputs_held, cotangents_held in (
        (pub_in, pub_out, held[0], held[1]),
        (priv_in, priv_out, held[2], held[3]),
    ):
        for e in range(inputs.shape[0]):
            pieces += [(down_held, inputs_held.at[e]), (up_held, cotangents_held.at[e])]
            for source, to in ((inputs, inputs_held), (cotangents, cotangents_held)):
                copies.append(
                    pltpu.make_async_copy(source.at[e], to.at[e], sems.at[len(copies)])
                )
    for copy in copies:
        copy.start()
    for out in outs:
        out[...] = jnp.zeros_like(out)
    for copy in copies[:2]:
        copy.wait()
    for i, (weights, piece) in enumerate(pieces):
        if i % GROUP == 0:
            for copy in copies[2 + i : 2 + i + GROUP]:
                copy.wait()
        slot, half = i // 2, i % 2
        outs[half][:, slot * LANES : slot * LANES + tokens] = dot(
            weights[...], piece[...], BOTH_LAST
        )


def gradient_kernel(dp, pub_len, priv_len, *rest):
    projected, returned, (pub_in, pub_out, priv_in, priv_out) = rest[:2], rest[2:4], rest[4:8]
    blocks, (down_rows, up_rows) = rest[8 : 8 + dp], rest[8 + dp :]
    me = lax.axis_index("dp")
    rank = projected[0].shape[0]
    tokens, width = pub_in.shape[1:]
    lanes = width // dp
    per = rank // dp
    slot = 0
    for inputs, cotangents, lengths in (
        (pub_in, pub_out, pub_len),
        (priv_in, priv_out, priv_len),
    ):
        for e in range(inputs.shape[0]):
            at = slice(slot * LANES, slot * LANES + tokens)
            live = iota((rank, tokens), 1) < lengths[e]
            down_live, up_live = (
                jnp.where(live, own[:, at] + other[:, at], 0.0).astype(jnp.bfloat16)
                for own, other in (returned, projected)
            )
            down_whole = dot(down_live, inputs[e], FIRST_LAST)
            up_whole = dot(up_live, cotangents[e], FIRST_LAST)
            for c in range(dp):
                features = slice(c * lanes, (c + 1) * lanes)
                at = slice(c * rank, (c + 1) * rank)
                down_part = down_whole[:, features]
                up_part = up_whole[:, features]
                down_rows[at, :] = down_part.astype(jnp.bfloat16)
                for h in range(lanes // LANES):
                    up_rows[h, at, :] = up_part[:, h * LANES : (h + 1) * LANES]
            for k in range(dp):
                to = me ^ k
                rows = slice(slot * rank, (slot + 1) * rank)
                blocks[k][rows, :lanes] = down_rows[
                    pl.ds(pl.multiple_of(to * rank, rank), rank), :
                ]
                for h in range(lanes // LANES):
                    pieces = [
                        up_rows[h, pl.ds(to * per + r, dp, stride=rank), :] for r in range(per)
                    ]
                    start = lanes + h * LANES
                    blocks[k][rows, start : start + LANES] = jnp.concatenate(
                        pieces, axis=0
                    ).astype(jnp.bfloat16)
            slot += 1


def gram_kernel(order, n_pub, n_priv, *refs):
    dp = len(order)
    blocks, group, out = refs[:dp], refs[dp], refs[dp + 1]
    me = lax.axis_index("dp")
    rows = blocks[0].shape[0] // (n_pub + n_priv)
    pub_rows, priv_rows = n_pub * rows, n_priv * rows
    for k, block in zip(order, blocks):
        source = me ^ k
        group[pl.ds(pl.multiple_of(source * pub_rows, pub_rows), pub_rows), :] = block[:pub_rows]
        group[
            pl.ds(pl.multiple_of(dp * pub_rows + source * priv_rows, priv_rows), priv_rows), :
        ] = block[pub_rows:]
    publics, privates = dp * n_pub, dp * n_priv
    span = publics * rows
    lanes = group.shape[1]
    public = group[:span, :]
    same = iota((span, span), 0) % rows == iota((span, span), 1) % rows
    parts, squares = [], []
    for c in range(group.shape[0] // span):
        part = group[c * span : (c + 1) * span, :]
        products = jnp.where(same, dot(public, part, BOTH_LAST), 0.0)
        products = jnp.sum(products.reshape(publics, rows // 8, 8, span), axis=1)
        parts += exact_parts(products.reshape(publics * 8, span))
        if c > 0:
            wide = part.astype(jnp.float32)
            squares.append(jnp.sum((wide * wide).reshape(publics, rows, lanes), axis=1))
    pick = (iota((span, LANES), 0) // rows == iota((span, LANES), 1)).astype(jnp.bfloat16)
    sums = dot(jnp.concatenate(parts, axis=0), pick, FIRST_LAST).reshape(-1, 3, publics * 8, LANES)
    total = jnp.zeros((publics * 8, LANES), jnp.float32)
    for c in range(sums.shape[0]):
        total += pltpu.roll(sums[c, 0] + sums[c, 1] + sums[c, 2], c * publics, 1)
    total = jnp.sum(total.reshape(publics, 8, LANES), axis=1)
    half, each = LANES // 2, privates // 2
    squares = jnp.concatenate(squares, axis=0)
    used = publics + privates
    gap = jnp.zeros((used, lanes), jnp.float32)
    rest = jnp.zeros((half - used - each, lanes), jnp.float32)
    stacked = jnp.concatenate([gap, squares[:each], rest, gap, squares[each:], rest], axis=0)
    ones = jnp.ones((16, lanes), jnp.bfloat16)
    three = dot(ones, jnp.concatenate(exact_parts(stacked), axis=0), BOTH_LAST)[:8]
    total_squares = three[:, :LANES] + three[:, LANES : 2 * LANES] + three[:, 2 * LANES :]
    short = publics // 2
    lane = iota((short, LANES), 1)
    packed = jnp.where(lane < half, total[:short], pltpu.roll(total[short:], half, 1))
    beside = jnp.logical_and(lane % half >= used, iota((short, LANES), 0) == 0)
    packed = jnp.where(beside, total_squares[:short], packed)
    for d in range(out.shape[0]):
        out[d] = packed


def update_kernel(gain, shares, group, noise, down_noise, up_noise, down, up):
    packed = shares[0]
    for d in range(1, shares.shape[0]):
        packed = packed + shares[d]
    publics = 2 * packed.shape[0]
    half = LANES // 2
    rows = 2 * up.shape[1] // group.shape[1]
    examples = group.shape[0] // rows
    each = (examples - publics) // 2
    total = jnp.concatenate([packed, pltpu.roll(packed, half, 1)], axis=0)
    row, lane = iota(total.shape, 0), iota(total.shape, 1)
    squares = jnp.where(
        lane[0:1] < publics + each,
        pltpu.roll(packed[0:1], LANES - (examples - publics), 1),
        pltpu.roll(packed[0:1], LANES - (half + each), 1),
    )
    gram_diagonal = jnp.sum(jnp.where(row == lane, total, 0.0), axis=1, keepdims=True)
    norm_scale = jnp.mean(jnp.sqrt(gram_diagonal), axis=0, keepdims=True)
    coefficient_limit = CLIP_COEF * norm_scale
    residual_limit = CLIP_RESIDUAL * norm_scale
    work = jnp.where(lane < half, total, jnp.where(lane == row + half, 1.0, 0.0))
    for j in range(0, publics, 2):
        first = jnp.broadcast_to(work[:, j : j + 1], work.shape)
        second = jnp.broadcast_to(work[:, j + 1 : j + 2], work.shape)
        inverse = lax.rsqrt(first[j : j + 1])
        pivot = work[j : j + 1] * inverse
        below = first[j + 1 : j + 2] * inverse
        next_inverse = lax.rsqrt(second[j + 1 : j + 2] - below * below)
        next_pivot = (work[j + 1 : j + 2] - below * pivot) * next_inverse
        first = first * inverse
        second = (second - first * below) * next_inverse
        work = jnp.where(
            row > j + 1,
            work - first * pivot - second * next_pivot,
            jnp.where(row == j, pivot, jnp.where(row == j + 1, next_pivot, work)),
        )
    private = jnp.logical_and(lane >= publics, lane < examples)
    coeffs = jnp.where(private, work, 0.0)
    coefficient_squares = jnp.sum(coeffs * coeffs, axis=0, keepdims=True)
    residual_squares = jnp.maximum(squares - coefficient_squares, 0.0)
    keep_coefficient = coefficient_limit / jnp.maximum(
        jnp.sqrt(coefficient_squares), coefficient_limit
    )
    keep_residual = residual_limit / jnp.maximum(jnp.sqrt(residual_squares), residual_limit)
    correction = jnp.sum(
        coeffs * (keep_coefficient - keep_residual), axis=1, keepdims=True
    )
    noise_column = jnp.zeros((publics, 1), jnp.float32)
    for j in range(publics):
        noise_column = jnp.where(iota((publics, 1), 0) == j, noise[j], noise_column)
    target = correction + SIGMA_COEF * coefficient_limit * noise_column
    inverse_factor = jnp.where(lane >= half, work, 0.0)
    anchor = pltpu.roll(jnp.sum(inverse_factor * target, axis=0, keepdims=True), half, 1)
    weights = jnp.where(lane[0:1] < publics, anchor, keep_residual)

    rank, lanes = rows, group.shape[1] // 2
    acc = jnp.zeros((rows, 2 * lanes), jnp.float32)
    for i in range(examples):
        acc = acc + weights[:, i : i + 1] * group[i * rows : (i + 1) * rows, :].astype(jnp.float32)
    scale = SIGMA_RESIDUAL * residual_limit
    per = LANES // rank
    flat = lanes * rank // LANES
    wide = jnp.concatenate([acc[:, :lanes]] * per, axis=0)
    wide = jnp.where(iota((LANES, lanes), 0) // rank == iota((LANES, lanes), 1) % per, wide, 0.0)
    pick = (iota((flat, lanes), 0) == iota((flat, lanes), 1) // per).astype(jnp.bfloat16)
    parts = dot(pick, jnp.concatenate(exact_parts(wide), axis=0), BOTH_LAST)
    turned = parts[:, :LANES] + parts[:, LANES : 2 * LANES] + parts[:, 2 * LANES :]
    for a in range(flat):
        at = slice(a * LANES, (a + 1) * LANES)
        down[0:1, at] = (turned[a : a + 1] + scale * down_noise[0:1, at]) * gain
    for a in range(rank):
        at = slice(a * lanes, (a + 1) * lanes)
        up[0:1, at] = (acc[a : a + 1, lanes:] + scale * up_noise[0:1, at]) * gain


def exchange(x, axis, step):
    return lax.ppermute(x, axis, [(s, s ^ step) for s in range(lax.axis_size(axis))])


def sum_over(axis, own, steps):
    for step in steps[:-1]:
        own = own + exchange(own, axis, step)
    return own, exchange(own, axis, steps[-1])


def small_group(
    pub_in, pub_out, pub_len, priv_in, priv_out, priv_len, down, up, noise, down_noise, up_noise
):
    dp, mp = lax.axis_size("dp"), lax.axis_size("mp")
    n_pub, tokens, width = pub_in.shape
    n_priv = priv_in.shape[0]
    examples = n_pub + n_priv
    rank = up.shape[0]
    lanes = width // dp
    f32, bf16 = jnp.float32, jnp.bfloat16

    projected, returned, *held = pl.pallas_call(
        project_kernel,
        out_shape=[jax.ShapeDtypeStruct((rank, examples * LANES), f32)] * 2
        + [jax.ShapeDtypeStruct(x.shape, bf16) for x in (pub_in, pub_out, priv_in, priv_out)],
        in_specs=[HBM] * 6,
        out_specs=[VMEM] * 6,
        scratch_shapes=[
            pltpu.VMEM(up.shape, bf16),
            pltpu.VMEM(up.shape, bf16),
            pltpu.SemaphoreType.DMA((2 + 2 * examples,)),
        ],
        compiler_params=PARAMS,
        name="project",
    )(
        *(
            pltpu.with_memory_space_constraint(x, pltpu.HBM)
            for x in (pub_in, pub_out, priv_in, priv_out, down.T, up)
        )
    )
    steps = [1 << i for i in range(mp.bit_length() - 1)]
    projected = sum_over("mp", projected, steps)
    returned = sum_over("mp", returned, steps[::-1])

    block = jax.ShapeDtypeStruct((examples * rank, 2 * lanes), bf16)
    blocks = pl.pallas_call(
        functools.partial(gradient_kernel, dp),
        out_shape=[block] * dp,
        in_specs=[SMEM] * 2 + [VMEM] * 8,
        out_specs=[VMEM] * dp,
        scratch_shapes=[
            pltpu.VMEM((dp * rank, lanes), bf16),
            pltpu.VMEM((lanes // LANES, dp * rank, LANES), f32),
        ],
        compiler_params=PARAMS,
        name="gradients",
    )(pub_len, priv_len, *projected, *returned, *held)
    far = sorted(range(dp // 2, dp), key=lambda k: (k & 1, k if k & 1 else -k))
    near = sorted(range(1, dp // 2), key=lambda k: (-k.bit_length(), k))
    order = [k for pair in zip(far, near + [0]) for k in pair]
    blocks = [exchange(blocks[k], "dp", k) if k else blocks[k] for k in order]

    group, shares = pl.pallas_call(
        functools.partial(gram_kernel, order, n_pub, n_priv),
        out_shape=[
            jax.ShapeDtypeStruct((dp * examples * rank, 2 * lanes), bf16),
            jax.ShapeDtypeStruct((dp * mp, dp * n_pub // 2, LANES), f32),
        ],
        in_specs=[VMEM] * dp,
        out_specs=[VMEM] * 2,
        compiler_params=PARAMS,
        name="inner_products",
    )(*blocks)
    shares = lax.all_to_all(shares, ("dp", "mp"), 0, 0, tiled=True)

    gain = 1.0 / math.sqrt(n_priv * dp * tokens)
    return pl.pallas_call(
        functools.partial(update_kernel, gain),
        out_shape=[
            jax.ShapeDtypeStruct(down_noise.shape, f32),
            jax.ShapeDtypeStruct(up_noise.shape, f32),
        ],
        in_specs=[VMEM, VMEM, SMEM, VMEM, VMEM],
        out_specs=[VMEM] * 2,
        compiler_params=PARAMS,
        name="update",
    )(shares, group, noise, down_noise, up_noise)


def fits(mesh, pub_in, priv_in, up):
    dp = mesh.shape["dp"]
    width = pub_in.shape[2] // mesh.shape["mp"]
    publics = pub_in.shape[0]
    return (
        up.shape[0] == 16
        and dp in (2, 4, 8)
        and width % (dp * LANES) == 0
        and publics == 8
        and priv_in.shape[0] % 8 == 0
        and publics + priv_in.shape[0] + priv_in.shape[0] // 2 <= LANES // 2
        and pub_in.shape[1] <= LANES
    )


def partial_gram_terms(
    input_activations, output_cotangents, adapter_down_matrix, adapter_up_matrix
):
    projected_gradients = jnp.einsum(
        "umo,ov->umv", input_activations, adapter_down_matrix, preferred_element_type=jnp.float32
    )
    reconstructed_gradients = jnp.einsum(
        "fpb,ab->fpa", output_cotangents, adapter_up_matrix, preferred_element_type=jnp.float32
    )
    return (projected_gradients, reconstructed_gradients)


def shard_grads(
    input_activations,
    output_cotangents,
    token_lengths,
    projected_gradients,
    reconstructed_gradients,
):
    example_total_count = input_activations.shape[0]
    token_steps = input_activations.shape[1]
    positions = lax.broadcasted_iota(jnp.int32, (example_total_count, token_steps), 1)
    live_mask = (positions < token_lengths[:, None]).astype(jnp.float32)[:, :, None]
    projected_live = (projected_gradients * live_mask).astype(jnp.bfloat16)
    returned_live = (reconstructed_gradients * live_mask).astype(jnp.bfloat16)
    grad_down = jnp.einsum(
        "etd,etr->edr", input_activations, returned_live, preferred_element_type=jnp.float32
    ).astype(jnp.bfloat16)
    grad_up = jnp.einsum(
        "etr,eto->ero", projected_live, output_cotangents, preferred_element_type=jnp.float32
    ).astype(jnp.bfloat16)
    return (grad_down.reshape(example_total_count, -1), grad_up.reshape(example_total_count, -1))


def lower_solve(factor, right_side, backward):
    return lax.linalg.triangular_solve(
        factor, right_side, left_side=True, lower=True, transpose_a=backward
    )


def limits(gram_matrix):
    factor = jnp.linalg.cholesky(gram_matrix)
    norm_scale = jnp.mean(jnp.sqrt(jnp.diagonal(gram_matrix)))
    return (factor, CLIP_COEF * norm_scale, CLIP_RESIDUAL * norm_scale)


def keep_factors(coeffs, residual_squares, coefficient_limit, residual_limit):
    coefficient_norm = jnp.sqrt(jnp.sum(coeffs * coeffs, axis=0))
    keep_coefficient = coefficient_limit / jnp.maximum(coefficient_norm, coefficient_limit)
    keep_residual = residual_limit / jnp.maximum(jnp.sqrt(residual_squares), residual_limit)
    return (keep_coefficient, keep_residual)


def large_group(
    public_input_activations,
    public_output_cotangents,
    public_token_lengths,
    private_input_activations,
    private_output_cotangents,
    private_token_lengths,
    adapter_down_matrix,
    adapter_up_matrix,
    embedding_coefficient_noise,
    residual_down_noise,
    residual_up_noise,
):
    public_projected, public_returned = partial_gram_terms(
        public_input_activations, public_output_cotangents, adapter_down_matrix, adapter_up_matrix
    )
    private_projected, private_returned = partial_gram_terms(
        private_input_activations, private_output_cotangents, adapter_down_matrix, adapter_up_matrix
    )
    public_projected, public_returned, private_projected, private_returned = lax.psum(
        (public_projected, public_returned, private_projected, private_returned), "mp"
    )
    public_down, public_up = shard_grads(
        public_input_activations,
        public_output_cotangents,
        public_token_lengths,
        public_projected,
        public_returned,
    )
    private_down, private_up = shard_grads(
        private_input_activations,
        private_output_cotangents,
        private_token_lengths,
        private_projected,
        private_returned,
    )
    public_down, public_up, private_down, private_up = (
        lax.all_to_all(public_down, "dp", split_axis=1, concat_axis=0, tiled=True),
        lax.all_to_all(public_up, "dp", split_axis=1, concat_axis=0, tiled=True),
        lax.all_to_all(private_down, "dp", split_axis=1, concat_axis=0, tiled=True),
        lax.all_to_all(private_up, "dp", split_axis=1, concat_axis=0, tiled=True),
    )
    public_group = jnp.concatenate([public_down, public_up], axis=1)
    private_group = jnp.concatenate([private_down, private_up], axis=1)
    public_wide = public_group.astype(jnp.float32)
    private_wide = private_group.astype(jnp.float32)
    gram_partial = jnp.einsum(
        "pk,qk->pq", public_group, public_group, preferred_element_type=jnp.float32
    )
    cross_partial = jnp.einsum(
        "pk,qk->pq", public_group, private_group, preferred_element_type=jnp.float32
    )
    square_partial = jnp.sum(private_wide * private_wide, axis=1)
    gram_matrix, cross_terms, square_totals = lax.psum(
        (gram_partial, cross_partial, square_partial), ("dp", "mp")
    )
    factor, coefficient_limit, residual_limit = limits(gram_matrix)
    coeffs = lower_solve(factor, cross_terms, False)
    residual_squares = square_totals - jnp.sum(coeffs * coeffs, axis=0)
    keep_coefficient, keep_residual = keep_factors(
        coeffs, residual_squares, coefficient_limit, residual_limit
    )
    correction = jnp.dot(coeffs, keep_coefficient - keep_residual, precision=PRECISE)
    target = correction + SIGMA_COEF * coefficient_limit * embedding_coefficient_noise
    anchor = lower_solve(factor, target[:, None], True)[:, 0]
    update = jnp.dot(anchor, public_wide, precision=PRECISE) + jnp.dot(
        keep_residual, private_wide, precision=PRECISE
    )
    noise_shard = jnp.concatenate([residual_down_noise[0], residual_up_noise[0]], axis=0)
    private_total = private_input_activations.shape[0] * lax.axis_size("dp")
    update_gain = 1.0 / math.sqrt(private_total * private_input_activations.shape[1])
    result = (update + SIGMA_RESIDUAL * residual_limit * noise_shard) * update_gain
    split_point = public_down.shape[1]
    return (result[None, :split_point], result[None, split_point:])


def solution(mesh):
    placed = (
        P("dp", None, "mp"),
        P("dp", None, "mp"),
        P("dp"),
        P("dp", None, "mp"),
        P("dp", None, "mp"),
        P("dp"),
        P("mp", None),
        P(None, "mp"),
        P(),
        P("mp", "dp"),
        P("mp", "dp"),
    )

    def run(*arrays):
        body = small_group if fits(mesh, arrays[0], arrays[3], arrays[7]) else large_group
        return jax.shard_map(
            body,
            mesh=mesh,
            in_specs=placed,
            out_specs=(P("mp", "dp"), P("mp", "dp")),
            check_vma=False,
        )(*arrays)

    return run
```

```python
import functools
import math

import jax
import jax.numpy as jnp
from jax import lax
from jax.experimental import pallas as pl
from jax.experimental.pallas import tpu as pltpu
from jax.sharding import PartitionSpec as P

CLIP_COEF = 0.5
CLIP_RESIDUAL = 0.7
SIGMA_COEF = 1.0
SIGMA_RESIDUAL = 0.04
PRECISE = lax.Precision.HIGHEST
LANES = 128
GROUP = 4
VMEM = pl.BlockSpec(memory_space=pltpu.VMEM)
HBM = pl.BlockSpec(memory_space=pltpu.HBM)
SMEM = pl.BlockSpec(memory_space=pltpu.SMEM)
BOTH_LAST = (((1,), (1,)), ((), ()))
FIRST_LAST = (((1,), (0,)), ((), ()))
PARAMS = pltpu.CompilerParams(vmem_limit_bytes=40 * 1024 * 1024)


def dot(a, b, dims, precision=None):
    return lax.dot_general(a, b, dims, precision=precision, preferred_element_type=jnp.float32)


def iota(shape, axis):
    return lax.broadcasted_iota(jnp.int32, shape, axis)


def exact_parts(x):
    limit = float(jnp.finfo(jnp.bfloat16).max)
    high = jnp.clip(x, -limit, limit).astype(jnp.bfloat16)
    rest = x - high.astype(jnp.float32)
    middle = rest.astype(jnp.bfloat16)
    return [high, middle, (rest - middle.astype(jnp.float32)).astype(jnp.bfloat16)]


def project_kernel(pub_in, pub_out, priv_in, priv_out, down_t, up, *rest):
    outs, held, (down_held, up_held, sems) = rest[:2], rest[2:6], rest[6:]
    tokens = pub_in.shape[1]
    copies = [
        pltpu.make_async_copy(down_t, down_held, sems.at[0]),
        pltpu.make_async_copy(up, up_held, sems.at[1]),
    ]
    pieces = []
    for inputs, cotangents, inputs_held, cotangents_held in (
        (pub_in, pub_out, held[0], held[1]),
        (priv_in, priv_out, held[2], held[3]),
    ):
        for e in range(inputs.shape[0]):
            pieces += [(down_held, inputs_held.at[e]), (up_held, cotangents_held.at[e])]
            for source, to in ((inputs, inputs_held), (cotangents, cotangents_held)):
                copies.append(
                    pltpu.make_async_copy(source.at[e], to.at[e], sems.at[len(copies)])
                )
    for copy in copies:
        copy.start()
    for out in outs:
        out[...] = jnp.zeros_like(out)
    for copy in copies[:2]:
        copy.wait()
    for i, (weights, piece) in enumerate(pieces):
        if i % GROUP == 0:
            for copy in copies[2 + i : 2 + i + GROUP]:
                copy.wait()
        slot, half = i // 2, i % 2
        outs[half][:, slot * LANES : slot * LANES + tokens] = dot(
            weights[...], piece[...], BOTH_LAST
        )


def gradient_kernel(dp, pub_len, priv_len, *rest):
    projected, returned, (pub_in, pub_out, priv_in, priv_out) = rest[:2], rest[2:4], rest[4:8]
    blocks, (down_rows, up_rows) = rest[8 : 8 + dp], rest[8 + dp :]
    me = lax.axis_index("dp")
    rank = projected[0].shape[0]
    tokens, width = pub_in.shape[1:]
    lanes = width // dp
    per = rank // dp
    slot = 0
    for inputs, cotangents, lengths in (
        (pub_in, pub_out, pub_len),
        (priv_in, priv_out, priv_len),
    ):
        for e in range(inputs.shape[0]):
            at = slice(slot * LANES, slot * LANES + tokens)
            live = iota((rank, tokens), 1) < lengths[e]
            down_live, up_live = (
                jnp.where(live, own[:, at] + other[:, at], 0.0).astype(jnp.bfloat16)
                for own, other in (returned, projected)
            )
            up_whole = dot(up_live, cotangents[e], FIRST_LAST)
            down_whole = dot(down_live, inputs[e], FIRST_LAST)
            for c in range(dp):
                features = slice(c * lanes, (c + 1) * lanes)
                at = slice(c * rank, (c + 1) * rank)
                down_part = down_whole[:, features]
                up_part = up_whole[:, features]
                down_rows[slot % 2, at, :] = down_part.astype(jnp.bfloat16)
                for h in range(lanes // LANES):
                    up_rows[slot % 2, h, at, :] = up_part[:, h * LANES : (h + 1) * LANES]
            for k in range(dp):
                to = me ^ k
                rows = slice(slot * rank, (slot + 1) * rank)
                blocks[k][rows, :lanes] = down_rows[
                    slot % 2, pl.ds(pl.multiple_of(to * rank, rank), rank), :
                ]
                for h in range(lanes // LANES):
                    pieces = [
                        up_rows[slot % 2, h, pl.ds(to * per + r, dp, stride=rank), :] for r in range(per)
                    ]
                    start = lanes + h * LANES
                    blocks[k][rows, start : start + LANES] = jnp.concatenate(
                        pieces, axis=0
                    ).astype(jnp.bfloat16)
            slot += 1


def gram_kernel(order, n_pub, n_priv, *refs):
    dp = len(order)
    blocks, group, out = refs[:dp], refs[dp], refs[dp + 1]
    me = lax.axis_index("dp")
    rows = blocks[0].shape[0] // (n_pub + n_priv)
    pub_rows, priv_rows = n_pub * rows, n_priv * rows
    for k, block in zip(order, blocks):
        source = me ^ k
        group[pl.ds(pl.multiple_of(source * pub_rows, pub_rows), pub_rows), :] = block[:pub_rows]
        group[
            pl.ds(pl.multiple_of(dp * pub_rows + source * priv_rows, priv_rows), priv_rows), :
        ] = block[pub_rows:]
    publics, privates = dp * n_pub, dp * n_priv
    span = publics * rows
    lanes = group.shape[1]
    public = group[:span, :]
    same = iota((span, span), 0) % rows == iota((span, span), 1) % rows
    parts, squares = [], []
    for c in range(group.shape[0] // span):
        part = group[c * span : (c + 1) * span, :]
        products = jnp.where(same, dot(public, part, BOTH_LAST), 0.0)
        products = jnp.sum(products.reshape(publics, rows // 8, 8, span), axis=1)
        parts += exact_parts(products.reshape(publics * 8, span))
        if c > 0:
            wide = part.astype(jnp.float32)
            squares.append(jnp.sum((wide * wide).reshape(publics, rows, lanes), axis=1))
    pick = (iota((span, LANES), 0) // rows == iota((span, LANES), 1)).astype(jnp.bfloat16)
    sums = dot(jnp.concatenate(parts, axis=0), pick, FIRST_LAST).reshape(-1, 3, publics * 8, LANES)
    total = jnp.zeros((publics * 8, LANES), jnp.float32)
    for c in range(sums.shape[0]):
        total += pltpu.roll(sums[c, 0] + sums[c, 1] + sums[c, 2], c * publics, 1)
    total = jnp.sum(total.reshape(publics, 8, LANES), axis=1)
    half, each = LANES // 2, privates // 2
    squares = jnp.concatenate(squares, axis=0)
    used = publics + privates
    gap = jnp.zeros((used, lanes), jnp.float32)
    rest = jnp.zeros((half - used - each, lanes), jnp.float32)
    stacked = jnp.concatenate([gap, squares[:each], rest, gap, squares[each:], rest], axis=0)
    ones = jnp.ones((16, lanes), jnp.bfloat16)
    three = dot(ones, jnp.concatenate(exact_parts(stacked), axis=0), BOTH_LAST)[:8]
    total_squares = three[:, :LANES] + three[:, LANES : 2 * LANES] + three[:, 2 * LANES :]
    short = publics // 2
    lane = iota((short, LANES), 1)
    packed = jnp.where(lane < half, total[:short], pltpu.roll(total[short:], half, 1))
    beside = jnp.logical_and(lane % half >= used, iota((short, LANES), 0) == 0)
    packed = jnp.where(beside, total_squares[:short], packed)
    for d in range(out.shape[0]):
        out[d] = packed


def update_kernel(gain, shares, group, noise, down_noise, up_noise, down, up):
    packed = shares[0]
    for d in range(1, shares.shape[0]):
        packed = packed + shares[d]
    publics = 2 * packed.shape[0]
    half = LANES // 2
    rows = 2 * up.shape[1] // group.shape[1]
    examples = group.shape[0] // rows
    each = (examples - publics) // 2
    total = jnp.concatenate([packed, pltpu.roll(packed, half, 1)], axis=0)
    row, lane = iota(total.shape, 0), iota(total.shape, 1)
    squares = jnp.where(
        lane[0:1] < publics + each,
        pltpu.roll(packed[0:1], LANES - (examples - publics), 1),
        pltpu.roll(packed[0:1], LANES - (half + each), 1),
    )
    gram_diagonal = jnp.sum(jnp.where(row == lane, total, 0.0), axis=1, keepdims=True)
    norm_scale = jnp.mean(jnp.sqrt(gram_diagonal), axis=0, keepdims=True)
    coefficient_limit = CLIP_COEF * norm_scale
    residual_limit = CLIP_RESIDUAL * norm_scale
    work = jnp.where(lane < half, total, jnp.where(lane == row + half, 1.0, 0.0))
    for j in range(0, publics, 2):
        first = jnp.broadcast_to(work[:, j : j + 1], work.shape)
        second = jnp.broadcast_to(work[:, j + 1 : j + 2], work.shape)
        inverse = lax.rsqrt(first[j : j + 1])
        pivot = work[j : j + 1] * inverse
        below = first[j + 1 : j + 2] * inverse
        next_inverse = lax.rsqrt(second[j + 1 : j + 2] - below * below)
        next_pivot = (work[j + 1 : j + 2] - below * pivot) * next_inverse
        first = first * inverse
        second = (second - first * below) * next_inverse
        work = jnp.where(
            row > j + 1,
            work - first * pivot - second * next_pivot,
            jnp.where(row == j, pivot, jnp.where(row == j + 1, next_pivot, work)),
        )
    private = jnp.logical_and(lane >= publics, lane < examples)
    coeffs = jnp.where(private, work, 0.0)
    coefficient_squares = jnp.sum(coeffs * coeffs, axis=0, keepdims=True)
    residual_squares = jnp.maximum(squares - coefficient_squares, 0.0)
    keep_coefficient = coefficient_limit / jnp.maximum(
        jnp.sqrt(coefficient_squares), coefficient_limit
    )
    keep_residual = residual_limit / jnp.maximum(jnp.sqrt(residual_squares), residual_limit)
    correction = jnp.sum(
        coeffs * (keep_coefficient - keep_residual), axis=1, keepdims=True
    )
    noise_column = jnp.zeros((publics, 1), jnp.float32)
    for j in range(publics):
        noise_column = jnp.where(iota((publics, 1), 0) == j, noise[j], noise_column)
    target = correction + SIGMA_COEF * coefficient_limit * noise_column
    inverse_factor = jnp.where(lane >= half, work, 0.0)
    anchor = pltpu.roll(jnp.sum(inverse_factor * target, axis=0, keepdims=True), half, 1)
    weights = jnp.where(lane[0:1] < publics, anchor, keep_residual)

    rank, lanes = rows, group.shape[1] // 2
    acc = jnp.zeros((rows, 2 * lanes), jnp.float32)
    for i in range(examples):
        acc = acc + weights[:, i : i + 1] * group[i * rows : (i + 1) * rows, :].astype(jnp.float32)
    scale = SIGMA_RESIDUAL * residual_limit
    per = LANES // rank
    flat = lanes * rank // LANES
    wide = jnp.concatenate([acc[:, :lanes]] * per, axis=0)
    wide = jnp.where(iota((LANES, lanes), 0) // rank == iota((LANES, lanes), 1) % per, wide, 0.0)
    pick = (iota((flat, lanes), 0) == iota((flat, lanes), 1) // per).astype(jnp.bfloat16)
    parts = dot(pick, jnp.concatenate(exact_parts(wide), axis=0), BOTH_LAST)
    turned = parts[:, :LANES] + parts[:, LANES : 2 * LANES] + parts[:, 2 * LANES :]
    for a in range(flat):
        at = slice(a * LANES, (a + 1) * LANES)
        down[0:1, at] = (turned[a : a + 1] + scale * down_noise[0:1, at]) * gain
    for a in range(rank):
        at = slice(a * lanes, (a + 1) * lanes)
        up[0:1, at] = (acc[a : a + 1, lanes:] + scale * up_noise[0:1, at]) * gain


def exchange(x, axis, step):
    return lax.ppermute(x, axis, [(s, s ^ step) for s in range(lax.axis_size(axis))])


def sum_over(axis, own, steps):
    for step in steps[:-1]:
        own = own + exchange(own, axis, step)
    return own, exchange(own, axis, steps[-1])


def small_group(
    pub_in, pub_out, pub_len, priv_in, priv_out, priv_len, down, up, noise, down_noise, up_noise
):
    dp, mp = lax.axis_size("dp"), lax.axis_size("mp")
    n_pub, tokens, width = pub_in.shape
    n_priv = priv_in.shape[0]
    examples = n_pub + n_priv
    rank = up.shape[0]
    lanes = width // dp
    f32, bf16 = jnp.float32, jnp.bfloat16

    projected, returned, *held = pl.pallas_call(
        project_kernel,
        out_shape=[jax.ShapeDtypeStruct((rank, examples * LANES), f32)] * 2
        + [jax.ShapeDtypeStruct(x.shape, bf16) for x in (pub_in, pub_out, priv_in, priv_out)],
        in_specs=[HBM] * 6,
        out_specs=[VMEM] * 6,
        scratch_shapes=[
            pltpu.VMEM(up.shape, bf16),
            pltpu.VMEM(up.shape, bf16),
            pltpu.SemaphoreType.DMA((2 + 2 * examples,)),
        ],
        compiler_params=PARAMS,
        name="project",
    )(
        *(
            pltpu.with_memory_space_constraint(x, pltpu.HBM)
            for x in (pub_in, pub_out, priv_in, priv_out, down.T, up)
        )
    )
    steps = [1 << i for i in range(mp.bit_length() - 1)]
    projected = sum_over("mp", projected, steps)
    returned = sum_over("mp", returned, steps[::-1])

    block = jax.ShapeDtypeStruct((examples * rank, 2 * lanes), bf16)
    blocks = pl.pallas_call(
        functools.partial(gradient_kernel, dp),
        out_shape=[block] * dp,
        in_specs=[SMEM] * 2 + [VMEM] * 8,
        out_specs=[VMEM] * dp,
        scratch_shapes=[
            pltpu.VMEM((2, dp * rank, lanes), bf16),
            pltpu.VMEM((2, lanes // LANES, dp * rank, LANES), f32),
        ],
        compiler_params=PARAMS,
        name="gradients",
    )(pub_len, priv_len, *projected, *returned, *held)
    far = sorted(range(dp // 2, dp), key=lambda k: (k & 1, k if k & 1 else -k))
    near = sorted(range(1, dp // 2), key=lambda k: (-k.bit_length(), k))
    order = [k for pair in zip(far, near + [0]) for k in pair]
    blocks = [exchange(blocks[k], "dp", k) if k else blocks[k] for k in order]

    group, shares = pl.pallas_call(
        functools.partial(gram_kernel, order, n_pub, n_priv),
        out_shape=[
            jax.ShapeDtypeStruct((dp * examples * rank, 2 * lanes), bf16),
            jax.ShapeDtypeStruct((dp * mp, dp * n_pub // 2, LANES), f32),
        ],
        in_specs=[VMEM] * dp,
        out_specs=[VMEM] * 2,
        compiler_params=PARAMS,
        name="inner_products",
    )(*blocks)
    shares = lax.all_to_all(shares, ("dp", "mp"), 0, 0, tiled=True)

    gain = 1.0 / math.sqrt(n_priv * dp * tokens)
    return pl.pallas_call(
        functools.partial(update_kernel, gain),
        out_shape=[
            jax.ShapeDtypeStruct(down_noise.shape, f32),
            jax.ShapeDtypeStruct(up_noise.shape, f32),
        ],
        in_specs=[VMEM, VMEM, SMEM, VMEM, VMEM],
        out_specs=[VMEM] * 2,
        compiler_params=PARAMS,
        name="update",
    )(shares, group, noise, down_noise, up_noise)


def fits(mesh, pub_in, priv_in, up):
    dp = mesh.shape["dp"]
    width = pub_in.shape[2] // mesh.shape["mp"]
    publics = pub_in.shape[0]
    return (
        up.shape[0] == 16
        and dp in (2, 4, 8)
        and width % (dp * LANES) == 0
        and publics == 8
        and priv_in.shape[0] % 8 == 0
        and publics + priv_in.shape[0] + priv_in.shape[0] // 2 <= LANES // 2
        and pub_in.shape[1] <= LANES
    )


def partial_gram_terms(
    input_activations, output_cotangents, adapter_down_matrix, adapter_up_matrix
):
    projected_gradients = jnp.einsum(
        "umo,ov->umv", input_activations, adapter_down_matrix, preferred_element_type=jnp.float32
    )
    reconstructed_gradients = jnp.einsum(
        "fpb,ab->fpa", output_cotangents, adapter_up_matrix, preferred_element_type=jnp.float32
    )
    return (projected_gradients, reconstructed_gradients)


def shard_grads(
    input_activations,
    output_cotangents,
    token_lengths,
    projected_gradients,
    reconstructed_gradients,
):
    example_total_count = input_activations.shape[0]
    token_steps = input_activations.shape[1]
    positions = lax.broadcasted_iota(jnp.int32, (example_total_count, token_steps), 1)
    live_mask = (positions < token_lengths[:, None]).astype(jnp.float32)[:, :, None]
    projected_live = (projected_gradients * live_mask).astype(jnp.bfloat16)
    returned_live = (reconstructed_gradients * live_mask).astype(jnp.bfloat16)
    grad_down = jnp.einsum(
        "etd,etr->edr", input_activations, returned_live, preferred_element_type=jnp.float32
    ).astype(jnp.bfloat16)
    grad_up = jnp.einsum(
        "etr,eto->ero", projected_live, output_cotangents, preferred_element_type=jnp.float32
    ).astype(jnp.bfloat16)
    return (grad_down.reshape(example_total_count, -1), grad_up.reshape(example_total_count, -1))


def lower_solve(factor, right_side, backward):
    return lax.linalg.triangular_solve(
        factor, right_side, left_side=True, lower=True, transpose_a=backward
    )


def limits(gram_matrix):
    factor = jnp.linalg.cholesky(gram_matrix)
    norm_scale = jnp.mean(jnp.sqrt(jnp.diagonal(gram_matrix)))
    return (factor, CLIP_COEF * norm_scale, CLIP_RESIDUAL * norm_scale)


def keep_factors(coeffs, residual_squares, coefficient_limit, residual_limit):
    coefficient_norm = jnp.sqrt(jnp.sum(coeffs * coeffs, axis=0))
    keep_coefficient = coefficient_limit / jnp.maximum(coefficient_norm, coefficient_limit)
    keep_residual = residual_limit / jnp.maximum(jnp.sqrt(residual_squares), residual_limit)
    return (keep_coefficient, keep_residual)


def large_group(
    public_input_activations,
    public_output_cotangents,
    public_token_lengths,
    private_input_activations,
    private_output_cotangents,
    private_token_lengths,
    adapter_down_matrix,
    adapter_up_matrix,
    embedding_coefficient_noise,
    residual_down_noise,
    residual_up_noise,
):
    public_projected, public_returned = partial_gram_terms(
        public_input_activations, public_output_cotangents, adapter_down_matrix, adapter_up_matrix
    )
    private_projected, private_returned = partial_gram_terms(
        private_input_activations, private_output_cotangents, adapter_down_matrix, adapter_up_matrix
    )
    public_projected, public_returned, private_projected, private_returned = lax.psum(
        (public_projected, public_returned, private_projected, private_returned), "mp"
    )
    public_down, public_up = shard_grads(
        public_input_activations,
        public_output_cotangents,
        public_token_lengths,
        public_projected,
        public_returned,
    )
    private_down, private_up = shard_grads(
        private_input_activations,
        private_output_cotangents,
        private_token_lengths,
        private_projected,
        private_returned,
    )
    public_down, public_up, private_down, private_up = (
        lax.all_to_all(public_down, "dp", split_axis=1, concat_axis=0, tiled=True),
        lax.all_to_all(public_up, "dp", split_axis=1, concat_axis=0, tiled=True),
        lax.all_to_all(private_down, "dp", split_axis=1, concat_axis=0, tiled=True),
        lax.all_to_all(private_up, "dp", split_axis=1, concat_axis=0, tiled=True),
    )
    public_group = jnp.concatenate([public_down, public_up], axis=1)
    private_group = jnp.concatenate([private_down, private_up], axis=1)
    public_wide = public_group.astype(jnp.float32)
    private_wide = private_group.astype(jnp.float32)
    gram_partial = jnp.einsum(
        "pk,qk->pq", public_group, public_group, preferred_element_type=jnp.float32
    )
    cross_partial = jnp.einsum(
        "pk,qk->pq", public_group, private_group, preferred_element_type=jnp.float32
    )
    square_partial = jnp.sum(private_wide * private_wide, axis=1)
    gram_matrix, cross_terms, square_totals = lax.psum(
        (gram_partial, cross_partial, square_partial), ("dp", "mp")
    )
    factor, coefficient_limit, residual_limit = limits(gram_matrix)
    coeffs = lower_solve(factor, cross_terms, False)
    residual_squares = square_totals - jnp.sum(coeffs * coeffs, axis=0)
    keep_coefficient, keep_residual = keep_factors(
        coeffs, residual_squares, coefficient_limit, residual_limit
    )
    correction = jnp.dot(coeffs, keep_coefficient - keep_residual, precision=PRECISE)
    target = correction + SIGMA_COEF * coefficient_limit * embedding_coefficient_noise
    anchor = lower_solve(factor, target[:, None], True)[:, 0]
    update = jnp.dot(anchor, public_wide, precision=PRECISE) + jnp.dot(
        keep_residual, private_wide, precision=PRECISE
    )
    noise_shard = jnp.concatenate([residual_down_noise[0], residual_up_noise[0]], axis=0)
    private_total = private_input_activations.shape[0] * lax.axis_size("dp")
    update_gain = 1.0 / math.sqrt(private_total * private_input_activations.shape[1])
    result = (update + SIGMA_RESIDUAL * residual_limit * noise_shard) * update_gain
    split_point = public_down.shape[1]
    return (result[None, :split_point], result[None, split_point:])


def solution(mesh):
    placed = (
        P("dp", None, "mp"),
        P("dp", None, "mp"),
        P("dp"),
        P("dp", None, "mp"),
        P("dp", None, "mp"),
        P("dp"),
        P("mp", None),
        P(None, "mp"),
        P(),
        P("mp", "dp"),
        P("mp", "dp"),
    )

    def run(*arrays):
        body = small_group if fits(mesh, arrays[0], arrays[3], arrays[7]) else large_group
        return jax.shard_map(
            body,
            mesh=mesh,
            in_specs=placed,
            out_specs=(P("mp", "dp"), P("mp", "dp")),
            check_vma=False,
        )(*arrays)

    return run
```

```python
import functools
import math

import jax
import jax.numpy as jnp
from jax import lax
from jax.experimental import pallas as pl
from jax.experimental.pallas import tpu as pltpu
from jax.sharding import PartitionSpec as P

CLIP_COEF = 0.5
CLIP_RESIDUAL = 0.7
SIGMA_COEF = 1.0
SIGMA_RESIDUAL = 0.04
PRECISE = lax.Precision.HIGHEST
LANES = 128
GROUP = 4
VMEM = pl.BlockSpec(memory_space=pltpu.VMEM)
HBM = pl.BlockSpec(memory_space=pltpu.HBM)
SMEM = pl.BlockSpec(memory_space=pltpu.SMEM)
BOTH_LAST = (((1,), (1,)), ((), ()))
FIRST_LAST = (((1,), (0,)), ((), ()))
PARAMS = pltpu.CompilerParams(vmem_limit_bytes=40 * 1024 * 1024)


def dot(a, b, dims, precision=None):
    return lax.dot_general(a, b, dims, precision=precision, preferred_element_type=jnp.float32)


def iota(shape, axis):
    return lax.broadcasted_iota(jnp.int32, shape, axis)


def exact_parts(x):
    limit = float(jnp.finfo(jnp.bfloat16).max)
    high = jnp.clip(x, -limit, limit).astype(jnp.bfloat16)
    rest = x - high.astype(jnp.float32)
    middle = rest.astype(jnp.bfloat16)
    return [high, middle, (rest - middle.astype(jnp.float32)).astype(jnp.bfloat16)]


def project_kernel(pub_in, pub_out, priv_in, priv_out, down_t, up, *rest):
    outs, held, (down_held, up_held, sems) = rest[:2], rest[2:6], rest[6:]
    tokens = pub_in.shape[1]
    copies = [
        pltpu.make_async_copy(down_t, down_held, sems.at[0]),
        pltpu.make_async_copy(up, up_held, sems.at[1]),
    ]
    pieces = []
    for inputs, cotangents, inputs_held, cotangents_held in (
        (pub_in, pub_out, held[0], held[1]),
        (priv_in, priv_out, held[2], held[3]),
    ):
        for e in range(inputs.shape[0]):
            pieces += [(down_held, inputs_held.at[e]), (up_held, cotangents_held.at[e])]
            for source, to in ((inputs, inputs_held), (cotangents, cotangents_held)):
                copies.append(
                    pltpu.make_async_copy(source.at[e], to.at[e], sems.at[len(copies)])
                )
    for copy in copies:
        copy.start()
    for out in outs:
        out[...] = jnp.zeros_like(out)
    for copy in copies[:2]:
        copy.wait()
    for i, (weights, piece) in enumerate(pieces):
        if i % GROUP == 0:
            for copy in copies[2 + i : 2 + i + GROUP]:
                copy.wait()
        slot, half = i // 2, i % 2
        outs[half][:, slot * LANES : slot * LANES + tokens] = dot(
            weights[...], piece[...], BOTH_LAST
        )


def gradient_kernel(dp, pub_len, priv_len, *rest):
    projected, returned, (pub_in, pub_out, priv_in, priv_out) = rest[:2], rest[2:4], rest[4:8]
    blocks, (down_rows, up_rows) = rest[8 : 8 + dp], rest[8 + dp :]
    me = lax.axis_index("dp")
    rank = projected[0].shape[0]
    tokens, width = pub_in.shape[1:]
    lanes = width // dp
    per = rank // dp
    slot = 0
    for inputs, cotangents, lengths in (
        (pub_in, pub_out, pub_len),
        (priv_in, priv_out, priv_len),
    ):
        for e in range(inputs.shape[0]):
            at = slice(slot * LANES, slot * LANES + tokens)
            live = iota((rank, tokens), 1) < lengths[e]
            down_live, up_live = (
                jnp.where(live, own[:, at] + other[:, at], 0.0).astype(jnp.bfloat16)
                for own, other in (returned, projected)
            )
            up_whole = dot(up_live, cotangents[e], FIRST_LAST)
            down_whole = dot(down_live, inputs[e], FIRST_LAST)
            for c in range(dp):
                features = slice(c * lanes, (c + 1) * lanes)
                at = slice(c * rank, (c + 1) * rank)
                down_part = down_whole[:, features]
                up_part = up_whole[:, features]
                down_rows[slot % 2, at, :] = down_part.astype(jnp.bfloat16)
                for h in range(lanes // LANES):
                    up_rows[slot % 2, h, at, :] = up_part[:, h * LANES : (h + 1) * LANES]
            for k in range(dp):
                to = me ^ k
                rows = slice(slot * rank, (slot + 1) * rank)
                blocks[k][rows, :lanes] = down_rows[
                    slot % 2, pl.ds(pl.multiple_of(to * rank, rank), rank), :
                ]
                for h in range(lanes // LANES):
                    pieces = [
                        up_rows[slot % 2, h, pl.ds(to * per + r, dp, stride=rank), :] for r in range(per)
                    ]
                    start = lanes + h * LANES
                    blocks[k][rows, start : start + LANES] = jnp.concatenate(
                        pieces, axis=0
                    ).astype(jnp.bfloat16)
            slot += 1


def gram_kernel(order, n_pub, n_priv, *refs):
    dp = len(order)
    blocks, group, out = refs[:dp], refs[dp], refs[dp + 1]
    me = lax.axis_index("dp")
    rows = blocks[0].shape[0] // (n_pub + n_priv)
    pub_rows, priv_rows = n_pub * rows, n_priv * rows
    for k, block in zip(order, blocks):
        source = me ^ k
        group[pl.ds(pl.multiple_of(source * pub_rows, pub_rows), pub_rows), :] = block[:pub_rows]
        group[
            pl.ds(pl.multiple_of(dp * pub_rows + source * priv_rows, priv_rows), priv_rows), :
        ] = block[pub_rows:]
    publics, privates = dp * n_pub, dp * n_priv
    span = publics * rows
    lanes = group.shape[1]
    public = group[:span, :]
    same = iota((span, span), 0) % rows == iota((span, span), 1) % rows
    parts, squares = [], []
    for c in range(group.shape[0] // span):
        part = group[c * span : (c + 1) * span, :]
        products = jnp.where(same, dot(public, part, BOTH_LAST), 0.0)
        products = jnp.sum(products.reshape(publics, rows // 8, 8, span), axis=1)
        parts += exact_parts(products.reshape(publics * 8, span))
        if c > 0:
            wide = part.astype(jnp.float32)
            squares.append(jnp.sum((wide * wide).reshape(publics, rows, lanes), axis=1))
    pick = (iota((span, LANES), 0) // rows == iota((span, LANES), 1)).astype(jnp.bfloat16)
    sums = dot(jnp.concatenate(parts, axis=0), pick, FIRST_LAST).reshape(-1, 3, publics * 8, LANES)
    total = jnp.zeros((publics * 8, LANES), jnp.float32)
    for c in range(sums.shape[0]):
        total += pltpu.roll(sums[c, 0] + sums[c, 1] + sums[c, 2], c * publics, 1)
    total = jnp.sum(total.reshape(publics, 8, LANES), axis=1)
    half, each = LANES // 2, privates // 2
    squares = jnp.concatenate(squares, axis=0)
    used = publics + privates
    gap = jnp.zeros((used, lanes), jnp.float32)
    rest = jnp.zeros((half - used - each, lanes), jnp.float32)
    stacked = jnp.concatenate([gap, squares[:each], rest, gap, squares[each:], rest], axis=0)
    ones = jnp.ones((16, lanes), jnp.bfloat16)
    three = dot(ones, jnp.concatenate(exact_parts(stacked), axis=0), BOTH_LAST)[:8]
    total_squares = three[:, :LANES] + three[:, LANES : 2 * LANES] + three[:, 2 * LANES :]
    short = publics // 2
    lane = iota((short, LANES), 1)
    packed = jnp.where(lane < half, total[:short], pltpu.roll(total[short:], half, 1))
    beside = jnp.logical_and(lane % half >= used, iota((short, LANES), 0) == 0)
    packed = jnp.where(beside, total_squares[:short], packed)
    for d in range(out.shape[0]):
        out[d] = packed


def update_kernel(gain, shares, group, noise, down_noise, up_noise, down, up):
    packed = shares[0]
    for d in range(1, shares.shape[0]):
        packed = packed + shares[d]
    publics = 2 * packed.shape[0]
    half = LANES // 2
    rows = 2 * up.shape[1] // group.shape[1]
    examples = group.shape[0] // rows
    each = (examples - publics) // 2
    total = jnp.concatenate([packed, pltpu.roll(packed, half, 1)], axis=0)
    row, lane = iota(total.shape, 0), iota(total.shape, 1)
    squares = jnp.where(
        lane[0:1] < publics + each,
        pltpu.roll(packed[0:1], LANES - (examples - publics), 1),
        pltpu.roll(packed[0:1], LANES - (half + each), 1),
    )
    gram_diagonal = jnp.sum(jnp.where(row == lane, total, 0.0), axis=1, keepdims=True)
    norm_scale = jnp.mean(jnp.sqrt(gram_diagonal), axis=0, keepdims=True)
    coefficient_limit = CLIP_COEF * norm_scale
    residual_limit = CLIP_RESIDUAL * norm_scale
    work = jnp.where(lane < half, total, jnp.where(lane == row + half, 1.0, 0.0))
    for j in range(0, publics, 2):
        first = jnp.broadcast_to(work[:, j : j + 1], work.shape)
        second = jnp.broadcast_to(work[:, j + 1 : j + 2], work.shape)
        inverse = lax.rsqrt(first[j : j + 1])
        pivot = work[j : j + 1] * inverse
        below = first[j + 1 : j + 2] * inverse
        next_inverse = lax.rsqrt(second[j + 1 : j + 2] - below * below)
        next_pivot = (work[j + 1 : j + 2] - below * pivot) * next_inverse
        first = first * inverse
        second = (second - first * below) * next_inverse
        work = jnp.where(
            row > j + 1,
            work - first * pivot - second * next_pivot,
            jnp.where(row == j, pivot, jnp.where(row == j + 1, next_pivot, work)),
        )
    private = jnp.logical_and(lane >= publics, lane < examples)
    coeffs = jnp.where(private, work, 0.0)
    coefficient_squares = jnp.sum(coeffs * coeffs, axis=0, keepdims=True)
    residual_squares = jnp.maximum(squares - coefficient_squares, 0.0)
    keep_coefficient = coefficient_limit / jnp.maximum(
        jnp.sqrt(coefficient_squares), coefficient_limit
    )
    keep_residual = residual_limit / jnp.maximum(jnp.sqrt(residual_squares), residual_limit)
    correction = jnp.sum(
        coeffs * (keep_coefficient - keep_residual), axis=1, keepdims=True
    )
    noise_column = jnp.zeros((publics, 1), jnp.float32)
    for j in range(publics):
        noise_column = jnp.where(iota((publics, 1), 0) == j, noise[j], noise_column)
    target = correction + SIGMA_COEF * coefficient_limit * noise_column
    inverse_factor = jnp.where(lane >= half, work, 0.0)
    anchor = pltpu.roll(jnp.sum(inverse_factor * target, axis=0, keepdims=True), half, 1)
    weights = jnp.where(lane[0:1] < publics, anchor, keep_residual) * gain

    rank, lanes = rows, group.shape[1] // 2
    acc = jnp.zeros((rows, 2 * lanes), jnp.float32)
    for i in range(examples):
        acc = acc + weights[:, i : i + 1] * group[i * rows : (i + 1) * rows, :].astype(jnp.float32)
    scale = (SIGMA_RESIDUAL * gain) * residual_limit
    per = LANES // rank
    flat = lanes * rank // LANES
    wide = jnp.concatenate([acc[:, :lanes]] * per, axis=0)
    wide = jnp.where(iota((LANES, lanes), 0) // rank == iota((LANES, lanes), 1) % per, wide, 0.0)
    pick = (iota((flat, lanes), 0) == iota((flat, lanes), 1) // per).astype(jnp.bfloat16)
    parts = dot(pick, jnp.concatenate(exact_parts(wide), axis=0), BOTH_LAST)
    turned = parts[:, :LANES] + parts[:, LANES : 2 * LANES] + parts[:, 2 * LANES :]
    for a in range(flat):
        at = slice(a * LANES, (a + 1) * LANES)
        down[0:1, at] = turned[a : a + 1] + scale * down_noise[0:1, at]
    for a in range(rank):
        at = slice(a * lanes, (a + 1) * lanes)
        up[0:1, at] = acc[a : a + 1, lanes:] + scale * up_noise[0:1, at]


def exchange(x, axis, step):
    return lax.ppermute(x, axis, [(s, s ^ step) for s in range(lax.axis_size(axis))])


def sum_over(axis, own, steps):
    for step in steps[:-1]:
        own = own + exchange(own, axis, step)
    return own, exchange(own, axis, steps[-1])


def small_group(
    pub_in, pub_out, pub_len, priv_in, priv_out, priv_len, down, up, noise, down_noise, up_noise
):
    dp, mp = lax.axis_size("dp"), lax.axis_size("mp")
    n_pub, tokens, width = pub_in.shape
    n_priv = priv_in.shape[0]
    examples = n_pub + n_priv
    rank = up.shape[0]
    lanes = width // dp
    f32, bf16 = jnp.float32, jnp.bfloat16

    projected, returned, *held = pl.pallas_call(
        project_kernel,
        out_shape=[jax.ShapeDtypeStruct((rank, examples * LANES), f32)] * 2
        + [jax.ShapeDtypeStruct(x.shape, bf16) for x in (pub_in, pub_out, priv_in, priv_out)],
        in_specs=[HBM] * 6,
        out_specs=[VMEM] * 6,
        scratch_shapes=[
            pltpu.VMEM(up.shape, bf16),
            pltpu.VMEM(up.shape, bf16),
            pltpu.SemaphoreType.DMA((2 + 2 * examples,)),
        ],
        compiler_params=PARAMS,
        name="project",
    )(
        *(
            pltpu.with_memory_space_constraint(x, pltpu.HBM)
            for x in (pub_in, pub_out, priv_in, priv_out, down.T, up)
        )
    )
    steps = [1 << i for i in range(mp.bit_length() - 1)]
    projected = sum_over("mp", projected, steps)
    returned = sum_over("mp", returned, steps[::-1])

    block = jax.ShapeDtypeStruct((examples * rank, 2 * lanes), bf16)
    blocks = pl.pallas_call(
        functools.partial(gradient_kernel, dp),
        out_shape=[block] * dp,
        in_specs=[SMEM] * 2 + [VMEM] * 8,
        out_specs=[VMEM] * dp,
        scratch_shapes=[
            pltpu.VMEM((2, dp * rank, lanes), bf16),
            pltpu.VMEM((2, lanes // LANES, dp * rank, LANES), f32),
        ],
        compiler_params=PARAMS,
        name="gradients",
    )(pub_len, priv_len, *projected, *returned, *held)
    far = sorted(range(dp // 2, dp), key=lambda k: (k & 1, k if k & 1 else -k))
    near = sorted(range(1, dp // 2), key=lambda k: (-k.bit_length(), k))
    order = [k for pair in zip(far, near + [0]) for k in pair]
    blocks = [exchange(blocks[k], "dp", k) if k else blocks[k] for k in order]

    group, shares = pl.pallas_call(
        functools.partial(gram_kernel, order, n_pub, n_priv),
        out_shape=[
            jax.ShapeDtypeStruct((dp * examples * rank, 2 * lanes), bf16),
            jax.ShapeDtypeStruct((dp * mp, dp * n_pub // 2, LANES), f32),
        ],
        in_specs=[VMEM] * dp,
        out_specs=[VMEM] * 2,
        compiler_params=PARAMS,
        name="inner_products",
    )(*blocks)
    shares = lax.all_to_all(shares, ("dp", "mp"), 0, 0, tiled=True)

    gain = 1.0 / math.sqrt(n_priv * dp * tokens)
    return pl.pallas_call(
        functools.partial(update_kernel, gain),
        out_shape=[
            jax.ShapeDtypeStruct(down_noise.shape, f32),
            jax.ShapeDtypeStruct(up_noise.shape, f32),
        ],
        in_specs=[VMEM, VMEM, SMEM, VMEM, VMEM],
        out_specs=[VMEM] * 2,
        compiler_params=PARAMS,
        name="update",
    )(shares, group, noise, down_noise, up_noise)


def fits(mesh, pub_in, priv_in, up):
    dp = mesh.shape["dp"]
    width = pub_in.shape[2] // mesh.shape["mp"]
    publics = pub_in.shape[0]
    return (
        up.shape[0] == 16
        and dp in (2, 4, 8)
        and width % (dp * LANES) == 0
        and publics == 8
        and priv_in.shape[0] % 8 == 0
        and publics + priv_in.shape[0] + priv_in.shape[0] // 2 <= LANES // 2
        and pub_in.shape[1] <= LANES
    )


def partial_gram_terms(
    input_activations, output_cotangents, adapter_down_matrix, adapter_up_matrix
):
    projected_gradients = jnp.einsum(
        "umo,ov->umv", input_activations, adapter_down_matrix, preferred_element_type=jnp.float32
    )
    reconstructed_gradients = jnp.einsum(
        "fpb,ab->fpa", output_cotangents, adapter_up_matrix, preferred_element_type=jnp.float32
    )
    return (projected_gradients, reconstructed_gradients)


def shard_grads(
    input_activations,
    output_cotangents,
    token_lengths,
    projected_gradients,
    reconstructed_gradients,
):
    example_total_count = input_activations.shape[0]
    token_steps = input_activations.shape[1]
    positions = lax.broadcasted_iota(jnp.int32, (example_total_count, token_steps), 1)
    live_mask = (positions < token_lengths[:, None]).astype(jnp.float32)[:, :, None]
    projected_live = (projected_gradients * live_mask).astype(jnp.bfloat16)
    returned_live = (reconstructed_gradients * live_mask).astype(jnp.bfloat16)
    grad_down = jnp.einsum(
        "etd,etr->edr", input_activations, returned_live, preferred_element_type=jnp.float32
    ).astype(jnp.bfloat16)
    grad_up = jnp.einsum(
        "etr,eto->ero", projected_live, output_cotangents, preferred_element_type=jnp.float32
    ).astype(jnp.bfloat16)
    return (grad_down.reshape(example_total_count, -1), grad_up.reshape(example_total_count, -1))


def lower_solve(factor, right_side, backward):
    return lax.linalg.triangular_solve(
        factor, right_side, left_side=True, lower=True, transpose_a=backward
    )


def limits(gram_matrix):
    factor = jnp.linalg.cholesky(gram_matrix)
    norm_scale = jnp.mean(jnp.sqrt(jnp.diagonal(gram_matrix)))
    return (factor, CLIP_COEF * norm_scale, CLIP_RESIDUAL * norm_scale)


def keep_factors(coeffs, residual_squares, coefficient_limit, residual_limit):
    coefficient_norm = jnp.sqrt(jnp.sum(coeffs * coeffs, axis=0))
    keep_coefficient = coefficient_limit / jnp.maximum(coefficient_norm, coefficient_limit)
    keep_residual = residual_limit / jnp.maximum(jnp.sqrt(residual_squares), residual_limit)
    return (keep_coefficient, keep_residual)


def large_group(
    public_input_activations,
    public_output_cotangents,
    public_token_lengths,
    private_input_activations,
    private_output_cotangents,
    private_token_lengths,
    adapter_down_matrix,
    adapter_up_matrix,
    embedding_coefficient_noise,
    residual_down_noise,
    residual_up_noise,
):
    public_projected, public_returned = partial_gram_terms(
        public_input_activations, public_output_cotangents, adapter_down_matrix, adapter_up_matrix
    )
    private_projected, private_returned = partial_gram_terms(
        private_input_activations, private_output_cotangents, adapter_down_matrix, adapter_up_matrix
    )
    public_projected, public_returned, private_projected, private_returned = lax.psum(
        (public_projected, public_returned, private_projected, private_returned), "mp"
    )
    public_down, public_up = shard_grads(
        public_input_activations,
        public_output_cotangents,
        public_token_lengths,
        public_projected,
        public_returned,
    )
    private_down, private_up = shard_grads(
        private_input_activations,
        private_output_cotangents,
        private_token_lengths,
        private_projected,
        private_returned,
    )
    public_down, public_up, private_down, private_up = (
        lax.all_to_all(public_down, "dp", split_axis=1, concat_axis=0, tiled=True),
        lax.all_to_all(public_up, "dp", split_axis=1, concat_axis=0, tiled=True),
        lax.all_to_all(private_down, "dp", split_axis=1, concat_axis=0, tiled=True),
        lax.all_to_all(private_up, "dp", split_axis=1, concat_axis=0, tiled=True),
    )
    public_group = jnp.concatenate([public_down, public_up], axis=1)
    private_group = jnp.concatenate([private_down, private_up], axis=1)
    public_wide = public_group.astype(jnp.float32)
    private_wide = private_group.astype(jnp.float32)
    gram_partial = jnp.einsum(
        "pk,qk->pq", public_group, public_group, preferred_element_type=jnp.float32
    )
    cross_partial = jnp.einsum(
        "pk,qk->pq", public_group, private_group, preferred_element_type=jnp.float32
    )
    square_partial = jnp.sum(private_wide * private_wide, axis=1)
    gram_matrix, cross_terms, square_totals = lax.psum(
        (gram_partial, cross_partial, square_partial), ("dp", "mp")
    )
    factor, coefficient_limit, residual_limit = limits(gram_matrix)
    coeffs = lower_solve(factor, cross_terms, False)
    residual_squares = square_totals - jnp.sum(coeffs * coeffs, axis=0)
    keep_coefficient, keep_residual = keep_factors(
        coeffs, residual_squares, coefficient_limit, residual_limit
    )
    correction = jnp.dot(coeffs, keep_coefficient - keep_residual, precision=PRECISE)
    target = correction + SIGMA_COEF * coefficient_limit * embedding_coefficient_noise
    anchor = lower_solve(factor, target[:, None], True)[:, 0]
    update = jnp.dot(anchor, public_wide, precision=PRECISE) + jnp.dot(
        keep_residual, private_wide, precision=PRECISE
    )
    noise_shard = jnp.concatenate([residual_down_noise[0], residual_up_noise[0]], axis=0)
    private_total = private_input_activations.shape[0] * lax.axis_size("dp")
    update_gain = 1.0 / math.sqrt(private_total * private_input_activations.shape[1])
    result = (update + SIGMA_RESIDUAL * residual_limit * noise_shard) * update_gain
    split_point = public_down.shape[1]
    return (result[None, :split_point], result[None, split_point:])


def solution(mesh):
    placed = (
        P("dp", None, "mp"),
        P("dp", None, "mp"),
        P("dp"),
        P("dp", None, "mp"),
        P("dp", None, "mp"),
        P("dp"),
        P("mp", None),
        P(None, "mp"),
        P(),
        P("mp", "dp"),
        P("mp", "dp"),
    )

    def run(*arrays):
        body = small_group if fits(mesh, arrays[0], arrays[3], arrays[7]) else large_group
        return jax.shard_map(
            body,
            mesh=mesh,
            in_specs=placed,
            out_specs=(P("mp", "dp"), P("mp", "dp")),
            check_vma=False,
        )(*arrays)

    return run
```
